32 devices in a mesh: dp: 16 (over z, x, core), tensor: 2 (over y).
Axes of the slice: x: 2, y: 2, z: 4, core: 2. Of those that a mesh axis runs over, the one named last changes fastest.
Arguments:
- tokens: bfloat16 [32768, 1024], P(('dp', 'tensor')), may hold values from -6 to 6
- lengths: int32 [32], P('dp'), may hold values from 1 to 1024, 24576 in all
- in_proj: float32 [3, 1024, 1024], P(None, 'dp', 'tensor'), may hold values from -0.1875 to 0.1875
- conv_weight: float32 [3, 1024], replicated, may hold values from -3.5 to 3.5
- out_proj: float32 [1024, 1024], P('tensor', 'dp'), may hold values from -0.1875 to 0.1875
- norm_gain: float32 [1024], replicated, may hold values from 0.1 to 1.9
- ffn_gain: float32 [1024], replicated, may hold values from 0.1 to 1.9
- w_gate: float32 [1024, 4608], P('dp', 'tensor'), may hold values from -0.1875 to 0.1875
- w_up: float32 [1024, 4608], P('dp', 'tensor'), may hold values from -0.1875 to 0.1875
- w_down: float32 [4608, 1024], P('tensor', 'dp'), may hold values from -0.09375 to 0.09375
- cotangent: bfloat16 [32768, 1024], P(('dp', 'tensor')), may hold values from -6 to 6
Outputs:
- result: bfloat16 [32768, 1024], P(('dp', 'tensor'))
- grad_tokens: float32 [32768, 1024], P(('dp', 'tensor'))
- grad_in_proj: float32 [3, 1024, 1024], P(None, 'dp', 'tensor')
- grad_conv: float32 [3, 1024], replicated
- grad_out_proj: float32 [1024, 1024], P('tensor', 'dp')
- grad_norm_gain: float32 [1024], replicated
- grad_ffn_gain: float32 [1024], replicated
- grad_gate: float32 [1024, 4608], P('dp', 'tensor')
- grad_up: float32 [1024, 4608], P('dp', 'tensor')
- grad_down: float32 [4608, 1024], P('tensor', 'dp')
The draws below stay inside these ranges and needn't reach their ends.
All inputs are finite; a program needn't handle non-finite values. No bound on the sum of `lengths` on one device may be relied on, other than what follows from the above.
Results may differ from the reference program's by a relative error of at most 0.025.
Values may be sent and summed in bfloat16 or wider, within the bound.
No kernel may reach another device: no remote copies, remote signals or barrier semaphores. Data moves between devices by JAX's collectives and lax.ppermute only.
A program may use at most 256 MiB of HBM per device.

```python
import math
import jax
import jax.numpy as jnp
import numpy as np
from jax import lax

D = 1024
FF = 4608
KERNEL = 3
SLOTS = 1024
SEQS = 32
TOKENS = 32768


def block_levels(rng, extent, split, smallest, top_value):
    factor_of = 1.0
    for dim, shards_of in split:
        steps = jax.random.uniform(jax.random.fold_in(jax.random.fold_in(rng, 6), dim), (shards_of,), jnp.float32, smallest / len(split), top_value / len(split))
        factor_of = factor_of * jnp.repeat(jnp.exp(steps), extent[dim] // shards_of).reshape((-1,) + (1,) * (len(extent) - 1 - dim))
    return factor_of


def length_profile(count, total, limit, slope):
    weights = [(1 << 20) // math.isqrt(grade ** slope) + 1 for grade in range(2, count + 1)]
    spare, counts = total - limit - (count - 1), [1] * (count - 1)
    while spare > 0:
        movable = [i for i in range(count - 1) if counts[i] < limit]
        pool, budget = sum([weights[i] for i in movable]), spare
        for i in movable:
            addition = min(limit - counts[i], max(1, budget * weights[i] // pool), spare)
            counts[i] = counts[i] + addition
            spare = spare - addition
    return np.array([limit] + counts)


def ragged_sizes(own_key, count, total, bound, lean):
    if count == 2:
        one = jax.random.randint(own_key, (), max(1, total - bound), min(bound, total - 1) + 1)
        return jnp.stack([one, total - one])
    sizes = jnp.asarray(length_profile(count, total, bound, lean), jnp.int32)
    twos = (count - 1) // 2
    source_of, sink = sizes[1:1 + 2 * twos:2], sizes[2:2 + 2 * twos:2]
    room = jnp.minimum(source_of - 1, bound - sink)
    passed = jax.random.randint(jax.random.fold_in(own_key, 1), (twos,), 0, 1 << 20) % (room + 1)
    sizes = sizes.at[1:1 + 2 * twos:2].set(source_of - passed).at[2:2 + 2 * twos:2].set(sink + passed)
    return sizes[jax.random.permutation(jax.random.fold_in(own_key, 2), count)]


def scatter_about(rng, dims, scale, most, shards=(), held_as=jnp.bfloat16):
    drawn = scale * jax.random.normal(rng, dims, jnp.float32)
    if shards:
        drawn = drawn * block_levels(rng, dims, shards, -0.22, 0.18)
    return jnp.clip(drawn, -most, most).astype(held_as)


def setup_inputs(seed: int = 0) -> dict:
    key_list = jax.random.split(jax.random.key(seed), 12)
    tokens = scatter_about(key_list[0], (TOKENS, D), 1.0, 6.0, ((0, 32),))
    lengths = ragged_sizes(key_list[1], SEQS, SEQS * SLOTS * 3 // 4, SLOTS, 1).astype(jnp.int32)
    in_proj = scatter_about(key_list[2], (3, D, D), D ** -0.5, 0.1875, ((1, 16), (2, 2)), jnp.float32)
    conv_weight = scatter_about(key_list[3], (KERNEL, D), KERNEL ** -0.5, 3.5, (), jnp.float32)
    out_proj = scatter_about(key_list[4], (D, D), D ** -0.5, 0.1875, ((0, 2), (1, 16)), jnp.float32)
    norm_gain = jnp.clip(1.0 + 0.18 * jax.random.normal(key_list[5], (D,), jnp.float32), 0.1, 1.9)
    ffn_gain = jnp.clip(1.0 + 0.18 * jax.random.normal(key_list[6], (D,), jnp.float32), 0.1, 1.9)
    w_gate = scatter_about(key_list[7], (D, FF), D ** -0.5, 0.1875, ((0, 16), (1, 2)), jnp.float32)
    w_up = scatter_about(key_list[8], (D, FF), D ** -0.5, 0.1875, ((0, 16), (1, 2)), jnp.float32)
    w_down = scatter_about(key_list[9], (FF, D), FF ** -0.5, 0.09375, ((0, 2), (1, 16)), jnp.float32)
    cotangent = scatter_about(key_list[10], (TOKENS, D), 1.0, 6.0, ((0, 32),))
    return {"tokens": tokens, "lengths": lengths, "in_proj": in_proj, "conv_weight": conv_weight, "out_proj": out_proj, "norm_gain": norm_gain, "ffn_gain": ffn_gain, "w_gate": w_gate, "w_up": w_up, "w_down": w_down, "cotangent": cotangent}


EPS = 1e-05

@jax.custom_vjp
def low(v):
    return lax.optimization_barrier(v.astype(jnp.bfloat16)).astype(jnp.float32)

@jax.custom_vjp
def low_back(v):
    return v

def low_keep(v):
    return (low(v), None)

def low_pass(kept, grad):
    return (grad,)

def back_keep(v):
    return (v, None)

def back_low(kept, grad):
    return (low(grad),)
low.defvjp(low_keep, low_pass)
low_back.defvjp(back_keep, back_low)

def rms_norm(values, gain):
    scale = lax.rsqrt(lax.optimization_barrier(jnp.mean(values * values, axis=-1, keepdims=True)) + EPS)
    return values * scale * gain

def shift_down(values, shift, position):
    moved = jnp.concatenate([jnp.zeros((shift, values.shape[1]), values.dtype), values[:-shift]], axis=0)
    return jnp.where((position >= shift)[:, None], moved, jnp.zeros_like(moved))

def block(params, tokens_f, alive, position):
    in_proj, conv_weight, out_proj, norm_gain, ffn_gain, w_gate, w_up, w_down = params
    highest = lax.Precision.HIGHEST
    normed = low(rms_norm(tokens_f, norm_gain))
    project = low_back(jnp.einsum('rd,kde->kre', normed, in_proj, precision=highest))
    gated = project[0] * project[2] * alive[:, None]
    mixed = conv_weight[0] * gated
    for shift in range(1, KERNEL):
        mixed = mixed + conv_weight[shift] * shift_down(gated, shift, position)
    branch = low(project[1] * mixed)
    mixer_out = low_back(jnp.dot(branch, out_proj, precision=highest))
    hidden = tokens_f + mixer_out
    normed_two = low(rms_norm(hidden, ffn_gain))
    gate = low_back(jnp.dot(normed_two, w_gate, precision=highest))
    upward = low_back(jnp.dot(normed_two, w_up, precision=highest))
    active = low(jax.nn.silu(gate) * upward)
    ffn_out = low_back(jnp.dot(active, w_down, precision=highest))
    return hidden + ffn_out

def reference(tokens, lengths, in_proj, conv_weight, out_proj, norm_gain, ffn_gain, w_gate, w_up, w_down, cotangent):
    group_size = math.gcd(SEQS, max(1, 4096 // SLOTS))
    count = SEQS // group_size
    rows = group_size * SLOTS
    params = tuple((item.astype(jnp.float32) for item in (in_proj, conv_weight, out_proj, norm_gain, ffn_gain, w_gate, w_up, w_down)))
    inputs = tokens.astype(jnp.float32).reshape(count, rows, D)
    grads_in = cotangent.astype(jnp.float32).reshape(count, rows, D)
    group_lengths = lengths.reshape(count, group_size).astype(jnp.int32)
    index_rows = jnp.arange(rows, dtype=jnp.int32)
    position = index_rows % SLOTS
    sequence = index_rows // SLOTS
    members = jnp.arange(group_size, dtype=jnp.int32)

    def step(totals, item):
        tokens_f, cot_rows, lengths_here = item
        hits = (sequence[:, None] == members[None, :]) & (position[:, None] < lengths_here[None, :])
        alive = lax.optimization_barrier(jnp.sum(jnp.where(hits, jnp.ones(hits.shape, jnp.float32), jnp.zeros(hits.shape, jnp.float32)), axis=1))

        def forward(weights, values):
            return block(weights, values, alive, position)
        output, pull = jax.vjp(forward, params, tokens_f)
        weight_grads, token_grads = pull(cot_rows * alive[:, None])
        totals = jax.tree.map(jnp.add, totals, weight_grads)
        return (totals, (output.astype(jnp.bfloat16), token_grads))
    zeros = jax.tree.map(jnp.zeros_like, params)
    totals, (outputs, token_grads) = lax.scan(step, zeros, (inputs, grads_in, group_lengths))
    g_in, g_conv, g_out, g_norm, g_ffn, g_gate, g_up, g_down = totals
    return (outputs.reshape(TOKENS, D), token_grads.reshape(TOKENS, D), g_in, g_conv, g_out, g_norm, g_ffn, g_gate, g_up, g_down)
```

```python
import jax
import jax.numpy as jnp
from jax import lax
from jax.sharding import PartitionSpec as P

SLOTS = 1024
EPS = 1e-05
AXES = ("dp", "tensor")
PIECES = 3
BF = jnp.bfloat16
F32 = jnp.float32


def dot_nn(left, right):
    return jnp.dot(left, right, preferred_element_type=F32)


def dot_tn(left, right):
    return lax.dot_general(left, right, (((0,), (0,)), ((), ())), preferred_element_type=F32)


def dot_nt(left, right):
    return lax.dot_general(left, right, (((1,), (1,)), ((), ())), preferred_element_type=F32)


class Links:
    def __init__(self, dp, tp):
        self.dp, self.tp, self.zs = dp, tp, dp // 4

    def swap(self, value, z=0, x=0, c=0, y=0):
        flip = (z * 2 + x) * 2 + c
        pairs = [
            (q * self.tp + t, (q ^ flip) * self.tp + (t ^ y))
            for q in range(self.dp)
            for t in range(self.tp)
        ]
        return lax.ppermute(value, AXES, pairs)

    def gather(self, own):
        parts = [own] + [self.swap(own, z=z) for z in range(1, self.zs)]
        mine = jnp.concatenate(parts, axis=1)
        half = mine.shape[1] // 2
        from_x, from_y = self.swap(mine, x=1), self.swap(mine, y=1)
        corner = jnp.concatenate(
            [self.swap(from_x[:, :half], y=1), self.swap(from_y[:, half:], x=1)], axis=1
        )
        grid = [[mine, from_y], [from_x, corner]]
        twin = [[self.swap(item, c=1) for item in row] for row in grid]
        return jnp.concatenate(
            [jnp.concatenate(row, axis=2) for row in grid + twin], axis=1
        )

    def scatter(self, full):
        kinds, depth, width = full.shape
        rows, cols = depth // 4, width // 2
        half, block = rows // 2, rows // self.zs

        def cell(core, x, y):
            at = (core * 2 + x) * rows
            return full[:, at : at + rows, y * cols : (y + 1) * cols]

        def both(x, y):
            return cell(0, x, y).astype(F32) + self.swap(cell(1, x, y), c=1).astype(F32)

        corner = both(1, 1).astype(BF)
        side_x, side_y, mine = both(1, 0), both(0, 1), both(0, 0)
        got_x = self.swap(corner[:, :half], x=1).astype(F32)
        got_y = self.swap(corner[:, half:], y=1).astype(F32)
        send_y = jnp.concatenate([side_y[:, :half] + got_x, side_y[:, half:]], axis=1).astype(BF)
        send_x = jnp.concatenate([side_x[:, :half], side_x[:, half:] + got_y], axis=1).astype(BF)
        total = (
            mine + self.swap(send_x, x=1).astype(F32) + self.swap(send_y, y=1).astype(F32)
        )
        out = total[:, :block]
        for z in range(1, self.zs):
            part = total[:, z * block : (z + 1) * block].astype(BF)
            out = out + self.swap(part, z=z).astype(F32)
        return out

    def sum_all(self, value):
        value = value + self.swap(value, c=1)
        value = value + self.swap(value, x=1)
        value = value + self.swap(value, y=1)
        step = 1
        while step < self.zs:
            value = value + self.swap(value, z=step)
            step *= 2
        return value

    def relative_blocks(self):
        q = lax.axis_index("dp")
        place = jnp.arange(self.dp)
        core, x, z = place // (2 * self.zs), place // self.zs % 2, place % self.zs
        return q ^ ((z * 2 + x) * 2 + core)


def shift_down(values, shift, position):
    moved = jnp.concatenate(
        [jnp.zeros((shift, values.shape[1]), values.dtype), values[:-shift]], axis=0
    )
    return jnp.where((position >= shift)[:, None], moved, jnp.zeros_like(moved))


def shift_up(values, shift):
    return jnp.concatenate(
        [values[shift:], jnp.zeros((shift, values.shape[1]), values.dtype)], axis=0
    )


def norm_stats(values):
    inverse = lax.rsqrt(jnp.mean(values * values, axis=-1, keepdims=True) + EPS)
    return (inverse, values * inverse)


def norm_back(grad_normed, gain, inverse, unit):
    scaled = grad_normed * gain
    return inverse * (scaled - unit * jnp.mean(scaled * unit, axis=-1, keepdims=True))


def body(
    tokens,
    lengths,
    in_proj,
    conv_weight,
    out_proj,
    norm_gain,
    ffn_gain,
    w_gate,
    w_up,
    w_down,
    cotangent,
):
    rows, width = tokens.shape
    links = Links(lax.axis_size("dp"), lax.axis_size("tensor"))
    rank = lax.axis_index("tensor")
    kernel = conv_weight.shape[0]
    half = in_proj.shape[2]
    hidden_half = w_gate.shape[1]
    chunk = hidden_half // PIECES
    block = width // links.dp

    mixer_own = jnp.concatenate(
        [in_proj.astype(BF), out_proj.T.astype(BF)[None]], axis=0
    )
    ffn_own = jnp.stack([w_gate.astype(BF), w_up.astype(BF), w_down.T.astype(BF)])
    mixer_w = links.gather(mixer_own)
    ffn_w = [
        links.gather(ffn_own[:, :, p * chunk : (p + 1) * chunk]) for p in range(PIECES)
    ]

    blocks = links.relative_blocks()
    feature = jnp.repeat(blocks, block) * block + jnp.tile(jnp.arange(block), links.dp)
    order = (jnp.arange(width)[:, None] == feature[None, :]).astype(BF)
    tokens_f = dot_nn(tokens, order)
    cot = dot_nn(cotangent, order)
    gain_one = jnp.take(norm_gain.reshape(links.dp, block), blocks, axis=0).reshape(width)
    gain_two = jnp.take(ffn_gain.reshape(links.dp, block), blocks, axis=0).reshape(width)
    conv = jnp.where(rank == 0, conv_weight, jnp.roll(conv_weight, half, axis=1))

    count = rows // SLOTS
    own_lengths = lax.dynamic_slice_in_dim(lengths, rank * count, count)
    position = jnp.tile(jnp.arange(SLOTS, dtype=jnp.int32), count)
    alive = (position < jnp.repeat(own_lengths, SLOTS)).astype(F32)[:, None]

    inverse_one, unit_one = norm_stats(tokens_f)
    normed = (unit_one * gain_one).astype(BF)
    b_part, c_part, x_part = [dot_nn(normed, mixer_w[k]) for k in range(3)]
    gated = b_part * x_part * alive
    mixed = conv[0] * gated
    for shift in range(1, kernel):
        mixed = mixed + conv[shift] * shift_down(gated, shift, position)
    branch = (c_part * mixed).astype(BF)
    hidden = tokens_f + dot_nt(branch, mixer_w[3])
    inverse_two, unit_two = norm_stats(hidden)
    normed_two = (unit_two * gain_two).astype(BF)
    grad_out = cot * alive
    grad_ffn = grad_out.astype(BF)

    ffn_out = 0.0
    grad_normed_two = 0.0
    ffn_shards = []
    for w in ffn_w:
        gate = dot_nn(normed_two, w[0])
        upward = dot_nn(normed_two, w[1])
        grad_active = dot_nn(grad_ffn, w[2])
        sigma = jax.nn.sigmoid(gate)
        active = (gate * sigma * upward).astype(BF)
        grad_gate_rows = (grad_active * upward * sigma * (1.0 + gate * (1.0 - sigma))).astype(BF)
        grad_up_rows = (grad_active * gate * sigma).astype(BF)
        ffn_out = ffn_out + dot_nt(active, w[2])
        grads = jnp.stack(
            [
                dot_tn(normed_two, grad_gate_rows).astype(BF),
                dot_tn(normed_two, grad_up_rows).astype(BF),
                dot_tn(grad_ffn, active).astype(BF),
            ]
        )
        ffn_shards.append(links.scatter(grads))
        grad_normed_two = (
            grad_normed_two + dot_nt(grad_gate_rows, w[0]) + dot_nt(grad_up_rows, w[1])
        )
    result = dot_nt((hidden + ffn_out).astype(BF), order).astype(BF)

    gain_two_part = jnp.sum(grad_normed_two * unit_two, axis=0)
    grad_hidden = grad_out + norm_back(grad_normed_two, gain_two, inverse_two, unit_two)
    grad_mix = grad_hidden.astype(BF)
    grad_branch = dot_nn(grad_mix, mixer_w[3])
    grad_wout = dot_tn(grad_mix, branch)
    grad_c = grad_branch * mixed
    grad_mixed = grad_branch * c_part
    tap_grads = [jnp.sum(grad_mixed * gated, axis=0)]
    grad_gated = conv[0] * grad_mixed
    for shift in range(1, kernel):
        masked = jnp.where((position >= shift)[:, None], grad_mixed, jnp.zeros_like(grad_mixed))
        tap_grads.append(jnp.sum(grad_mixed * shift_down(gated, shift, position), axis=0))
        grad_gated = grad_gated + conv[shift] * shift_up(masked, shift)
    grad_gated = grad_gated * alive
    grad_project = [
        item.astype(BF) for item in (grad_gated * x_part, grad_c, grad_gated * b_part)
    ]
    mixer_shard = links.scatter(
        jnp.stack(
            [dot_tn(normed, item).astype(BF) for item in grad_project] + [grad_wout.astype(BF)]
        )
    )
    grad_normed = sum(dot_nt(item, mixer_w[k]) for k, item in enumerate(grad_project))
    gain_one_part = jnp.sum(grad_normed * unit_one, axis=0)
    grad_tokens = grad_hidden + norm_back(grad_normed, gain_one, inverse_one, unit_one)
    high = grad_tokens.astype(BF)
    rest = grad_tokens - high.astype(F32)
    middle = rest.astype(BF)
    low = (rest - middle.astype(F32)).astype(BF)
    grad_tokens = dot_nt(high, order) + (dot_nt(middle, order) + dot_nt(low, order))

    q = lax.axis_index("dp")
    apart = jnp.arange(links.dp) ^ q
    place = ((apart % 2) * 2 + apart // 2 % 2) * links.zs + apart // 4
    taps = jnp.stack(tap_grads)
    taps = jnp.where(rank == 0, taps, jnp.roll(taps, half, axis=1))
    gains = jnp.stack([gain_one_part, gain_two_part]).reshape(2, links.dp, block)
    gains = jnp.take(gains, place, axis=1).reshape(2, width)
    sums = links.sum_all(jnp.concatenate([gains, taps], axis=0))

    ffn_shard = jnp.concatenate(ffn_shards, axis=2)
    return (
        result,
        grad_tokens,
        mixer_shard[:3],
        sums[2:],
        mixer_shard[3].T,
        sums[0],
        sums[1],
        ffn_shard[0],
        ffn_shard[1],
        ffn_shard[2].T,
    )


def solution(mesh):
    rows = P(("dp", "tensor"), None)
    in_specs = (
        rows,
        P("dp"),
        P(None, "dp", "tensor"),
        P(),
        P("tensor", "dp"),
        P(),
        P(),
        P("dp", "tensor"),
        P("dp", "tensor"),
        P("tensor", "dp"),
        rows,
    )
    out_specs = (
        rows,
        rows,
        P(None, "dp", "tensor"),
        P(),
        P("tensor", "dp"),
        P(),
        P(),
        P("dp", "tensor"),
        P("dp", "tensor"),
        P("tensor", "dp"),
    )
    return jax.shard_map(body, mesh=mesh, in_specs=in_specs, out_specs=out_specs, check_vma=False)
```

```python
import functools

import jax
import jax.numpy as jnp
from jax import lax
from jax.experimental import pallas as pl
from jax.experimental.pallas import tpu as pltpu
from jax.sharding import PartitionSpec as P

SLOTS = 1024
EPS = 1e-05
AXES = ("dp", "tensor")
SIZES = (256, 256, 256, 256, 128)
MIXER_PARTS = 2
MIXER_TILE = 128
ROW_TILE = 256
COST = 4
VMEM = 60 * 2**20
BF = jnp.bfloat16
F32 = jnp.float32
ANYWHERE = pl.BlockSpec(memory_space=pl.ANY)


def dot_nn(left, right):
    return jnp.dot(left, right, preferred_element_type=F32)


def dot_tn(left, right):
    return lax.dot_general(left, right, (((0,), (0,)), ((), ())), preferred_element_type=F32)


def dot_nt(left, right):
    return lax.dot_general(left, right, (((1,), (1,)), ((), ())), preferred_element_type=F32)


class Links:
    def __init__(self, dp, tp):
        self.dp, self.tp, self.zs = dp, tp, dp // 4

    def swap(self, value, x=0, c=0, y=0, z=0):
        flip = (z * 2 + x) * 2 + c
        pairs = [
            (q * self.tp + t, (q ^ flip) * self.tp + (t ^ y))
            for q in range(self.dp)
            for t in range(self.tp)
        ]
        return lax.ppermute(value, AXES, pairs)

    def turn_z(self, value):
        groups = [[z * 4 + rest for z in range(self.zs)] for rest in range(4)]
        return lax.all_to_all(value, "dp", 0, 0, axis_index_groups=groups, tiled=True)

    def gather_z(self, own):
        return self.turn_z(jnp.broadcast_to(own[None], (self.zs, *own.shape)))

    def gather_sides(self, mine):
        return self.swap(mine, x=1), self.swap(mine, y=1)

    def gather_corner(self, from_x, from_y):
        half = self.zs // 2
        return self.swap(from_x[:half], y=1), self.swap(from_y[half:], x=1)

    def sum_all(self, value):
        value = value + self.swap(value, c=1)
        value = value + self.swap(value, x=1)
        value = value + self.swap(value, y=1)
        step = 1
        while step < self.zs:
            value = value + self.swap(value, z=step)
            step *= 2
        return value

    def absolute(self, place):
        q = lax.axis_index("dp")
        core, x, z = place // (2 * self.zs), place // self.zs % 2, place % self.zs
        return z * 4 + ((q % 4) ^ (x * 2 + core))

    def place(self, absolute):
        q = lax.axis_index("dp")
        apart = (absolute % 4) ^ (q % 4)
        return ((apart % 2) * 2 + apart // 2) * self.zs + absolute // 4


def whole_spec(shape, buffers=1):
    return pl.BlockSpec(
        shape, lambda *_: (0,) * len(shape), pipeline_mode=pl.Buffered(buffers)
    )


def params():
    return pltpu.CompilerParams(vmem_limit_bytes=VMEM)


def cost(flops, moved_bytes):
    return pl.CostEstimate(flops=flops, bytes_accessed=moved_bytes, transcendentals=0)


def small_call(kernel, inputs, out_shapes, work):
    columns = inputs[0].shape[-1]

    def spec(shape):
        lead = len(shape) - 1
        return pl.BlockSpec(
            (*shape[:-1], 128), lambda j: (*(0,) * lead, j)
        )

    return pl.pallas_call(
        kernel,
        grid=(columns // 128,),
        in_specs=[spec(item.shape) for item in inputs],
        out_specs=[spec(shape) for shape in out_shapes],
        out_shape=[jax.ShapeDtypeStruct(shape, BF) for shape in out_shapes],
        compiler_params=params(),
        cost_estimate=cost(0, 2 * work),
    )(*inputs)


def join_kernel(mine, from_y, from_x, one, two, out):
    half = one.shape[0]
    out[0] = mine[...]
    out[1] = from_y[...]
    out[2] = from_x[...]
    out[3, :half] = one[...]
    out[3, half:] = two[...]


def join(mine, from_y, from_x, one, two):
    shape = (4, *mine.shape)
    return small_call(
        join_kernel, [mine, from_y, from_x, one, two], [shape], 8 * mine.size
    )[0]


def both_kernel(keep, got, send_x, send_y, rest_x, rest_y, own):
    half = keep.shape[1] // 2

    def total(cell, part):
        return (keep[cell, part].astype(F32) + got[cell, part].astype(F32)).astype(BF)

    low, high = slice(0, half), slice(half, 2 * half)
    send_x[0], send_x[1] = total(3, low), total(2, low)
    send_y[0], send_y[1] = total(3, high), total(1, high)
    rest_x[...], rest_y[...] = total(2, high), total(1, low)
    own[:half], own[half:] = total(0, low), total(0, high)


def both_cores(keep, got):
    _, zs, *rest = keep.shape
    part = (zs // 2, *rest)
    shapes = [(2, *part), (2, *part), part, part, (zs, *rest)]
    return small_call(both_kernel, [keep, got], shapes, 3 * keep.size)


def sides_kernel(rest_x, rest_y, got_x, got_y, send_x, send_y):
    send_x[...] = (rest_x[...].astype(F32) + got_y[0].astype(F32)).astype(BF)
    send_y[...] = (rest_y[...].astype(F32) + got_x[0].astype(F32)).astype(BF)


def add_sides(rest_x, rest_y, got_x, got_y):
    return small_call(
        sides_kernel, [rest_x, rest_y, got_x, got_y], [rest_x.shape] * 2, 8 * rest_x.size
    )


def own_kernel(own, got_x, got_y, side_x, side_y, out):
    half = side_x.shape[0]
    low = own[:half].astype(F32) + got_x[1].astype(F32) + side_y[...].astype(F32)
    high = own[half:].astype(F32) + got_y[1].astype(F32) + side_x[...].astype(F32)
    out[:half] = low.astype(BF)
    out[half:] = high.astype(BF)


def add_own(own, got_x, got_y, side_x, side_y):
    return small_call(
        own_kernel, [own, got_x, got_y, side_x, side_y], [own.shape], 5 * own.size
    )[0]


def ffn_kernel(first, last, ties, *refs):
    feed = iter(refs)
    take = lambda n: [next(feed) for _ in range(n)]
    normed, normed_twin, grad_out, grad_out_twin = take(4)
    mine, from_y, from_x, one, two = take(5)
    before = [] if first else take(4)
    take(ties)
    send_x, send_y, rest_x, rest_y, own = take(5)
    totals = take(4)
    wide, rows_n, rows_g, active, grad_gate, grad_up = take(6)
    step = pl.program_id(0)
    steps = pl.num_programs(0)
    zs, _, kinds, block, tile = mine.shape
    half = zs // 2
    height = normed.shape[0]
    places = [(core, x, z) for core in range(2) for x in range(2) for z in range(zs)]

    @pl.when(step == 0)
    def _():
        for at, (core, x, z) in enumerate(places):
            rows = slice(at * block, (at + 1) * block)
            for k in range(kinds):
                if x == 0:
                    wide[k, rows, :tile] = mine[z, core, k]
                    wide[k, rows, tile:] = from_y[z, core, k]
                else:
                    wide[k, rows, :tile] = from_x[z, core, k]
                    corner = one[z, core, k] if z < half else two[z - half, core, k]
                    wide[k, rows, tile:] = corner

    at = pl.ds(pl.multiple_of(step * height, height), height)

    def work(normed, grad_out, before, totals, turn):
        left = normed[...]
        right = grad_out[...]
        rows_n[at, :] = left
        rows_g[at, :] = right
        gate, upward = dot_nn(left, wide[0]), dot_nn(left, wide[1])
        grad_active = dot_nn(right, wide[2])
        sigma = 1.0 / (1.0 + jnp.exp(-gate))
        silu = gate * sigma
        act = (silu * upward).astype(BF)
        g_up = (grad_active * silu).astype(BF)
        g_gate = (grad_active * upward * (sigma + silu * (1.0 - sigma))).astype(BF)
        active[at, :] = act
        grad_up[at, :] = g_up
        grad_gate[at, :] = g_gate
        ffn = dot_nt(act, wide[2])
        back = dot_nt(g_gate, wide[0]) + dot_nt(g_up, wide[1])
        if not first:
            ffn = ffn + before[0][...]
            back = back + before[1][...]
        if turn:
            ffn, back = other_core_first(ffn), other_core_first(back)
        totals[0][...] = ffn.astype(totals[0].dtype)
        totals[1][...] = back.astype(totals[1].dtype)

    @pl.when(step < steps // 2)
    def _():
        work(normed, grad_out, before[:2], totals[:2], False)

    @pl.when(step >= steps // 2)
    def _():
        work(normed_twin, grad_out_twin, before[2:], totals[2:], last)

    @pl.when(step == steps - 1)
    def _():
        group = 256 // block
        for first_place in range(0, len(places), group):
            rows = slice(first_place * block, (first_place + group) * block)
            for k, (left, right) in enumerate(
                ((rows_n, grad_gate), (rows_n, grad_up), (rows_g, active))
            ):
                value = dot_tn(left[:, rows], right[...]).astype(BF)
                for i in range(group):
                    core, x, z = places[first_place + i]
                    part = value[i * block : (i + 1) * block]
                    low, zh = z < half, z % half
                    near, far = part[:, :tile], part[:, tile:]
                    if x == 0:
                        own[z, core, k] = near
                        if low:
                            rest_y[zh, core, k] = far
                        else:
                            send_y[1, zh, core, k] = far
                    else:
                        if low:
                            send_x[1, zh, core, k] = near
                            send_x[0, zh, core, k] = far
                        else:
                            rest_x[zh, core, k] = near
                            send_y[0, zh, core, k] = far


def ffn_piece(inputs, cells, before, last, ties):
    rows, width = inputs[0].shape
    zs, _, kinds, block, columns = cells[0].shape
    first = before is None
    height = min(ROW_TILE, rows)
    half = rows // height
    near = pl.BlockSpec((height, width), lambda i: (jnp.minimum(i, half - 1), 0))
    far = pl.BlockSpec((height, width), lambda i: (jnp.maximum(i - half, 0), 0))
    operands = [*inputs, *cells, *(() if first else before), *ties]
    part = (zs // 2, 2, kinds, block, columns)
    grads = [(2, *part), (2, *part), part, part, (zs, *part[1:])]
    twin = BF if last else F32
    return pl.pallas_call(
        functools.partial(ffn_kernel, first, last, len(ties)),
        grid=(2 * half,),
        in_specs=[near, far, near, far]
        + [whole_spec(item.shape) for item in cells]
        + ([] if first else [near, near, far, far])
        + [ANYWHERE] * len(ties),
        out_specs=[whole_spec(shape) for shape in grads] + [near, near, far, far],
        out_shape=[jax.ShapeDtypeStruct(shape, BF) for shape in grads]
        + [jax.ShapeDtypeStruct((rows, width), dtype) for dtype in (F32, F32, twin, twin)],
        scratch_shapes=[pltpu.VMEM((kinds, width, 2 * columns), BF)]
        + [pltpu.VMEM((2 * rows, width), BF)] * 2
        + [pltpu.VMEM((2 * rows, 2 * columns), BF)] * 3,
        compiler_params=params(),
        cost_estimate=cost(
            72 * COST * rows * width * columns, 24 * width * columns + 40 * rows * width
        ),
    )(*operands)


def lay_out(near, twin, wide):
    _, zs, kinds, block, tile = near.shape
    for core, cells in enumerate((near, twin)):
        for x in range(2):
            for z in range(zs):
                at = ((core * 2 + x) * zs + z) * block
                for k in range(kinds):
                    for y in range(2):
                        wide[k, at : at + block, y * tile : (y + 1) * tile] = cells[
                            2 * x + y, z, k
                        ]


def cell_specs(cells, tile):
    return [
        pl.BlockSpec((*item.shape[:-1], tile), lambda j: (0, 0, 0, 0, j)) for item in cells
    ]


def other_core_first(values):
    half = values.shape[1] // 2
    return jnp.concatenate([values[:, half:], values[:, :half]], axis=1)


def moved(values, shift, position):
    rows = values.shape[0]
    turned = pltpu.roll(values, shift % rows, 0)
    inside = position >= shift if shift > 0 else position < rows + shift
    return jnp.where(inside, turned, 0.0)


def mixed_of(gated, conv, position):
    total = conv[0:1] * gated
    for shift in range(1, conv.shape[0]):
        total = total + conv[shift : shift + 1] * moved(gated, shift, position)
    return total


def tile_conv(conv):
    return jnp.concatenate([conv[0], conv[1]], axis=1)


def mixer_kernel(first, last, ties, row_tile, *refs):
    feed = iter(refs)
    take = lambda n: [next(feed) for _ in range(n)]
    lengths, normed, tokens, conv, gain = take(5)
    cells = take(2)
    before = [] if first else take(1)
    take(ties)
    project, hidden = take(2)
    normed_two, for_twin = take(2) if last else (None, None)
    wide, branch = take(2)
    step = pl.program_id(0)
    rows = normed.shape[0]
    lay_out(*cells, wide)

    @pl.loop(0, rows // row_tile)
    def _(i):
        at = pl.ds(pl.multiple_of(i * row_tile, row_tile), row_tile)
        left = normed[at, :]
        for k in range(3):
            project[k, at, :] = dot_nn(left, wide[k])

    taps = tile_conv(conv[...])
    for sequence in range(rows // SLOTS):
        at = slice(sequence * SLOTS, (sequence + 1) * SLOTS)
        position = lax.broadcasted_iota(jnp.int32, (SLOTS, wide.shape[2]), 0)
        gated = project[0, at] * project[2, at]
        gated = jnp.where(position < lengths[sequence], gated, 0.0)
        branch[at, :] = (project[1, at] * mixed_of(gated, taps, position)).astype(BF)

    @pl.when(step == 0)
    def _():
        if first:
            hidden[...] = tokens[...].astype(F32)
        else:
            hidden[...] = before[0][...]

    ending = step == pl.num_programs(0) - 1

    @pl.loop(0, rows // row_tile)
    def _(i):
        at = pl.ds(pl.multiple_of(i * row_tile, row_tile), row_tile)
        value = hidden[at, :] + dot_nt(branch[at, :], wide[3])
        hidden[at, :] = value
        if last:

            @pl.when(ending)
            def _():
                unit = norm_stats(value)[1]
                value_two = (unit * gain[...]).astype(BF)
                normed_two[at, :] = value_two
                for_twin[at, :] = other_core_first(value_two)


def mixer_part(lengths, normed, tokens, conv, gain, cells, before, last, ties):
    rows, width = normed.shape
    _, zs, kinds, block, columns = cells[0].shape
    first = before is None
    tile = MIXER_TILE
    whole = whole_spec((rows, width))
    inputs = [lengths, normed, tokens, conv, gain, *cells]
    inputs += ([] if first else [before]) + list(ties)
    outs = [jax.ShapeDtypeStruct((3, rows, 2 * columns), F32), jax.ShapeDtypeStruct((rows, width), F32)]
    out_specs = [pl.BlockSpec((3, rows, 2 * tile), lambda j: (0, 0, j)), whole]
    if last:
        outs += [jax.ShapeDtypeStruct((rows, width), BF)] * 2
        out_specs += [whole] * 2
    return pl.pallas_call(
        functools.partial(mixer_kernel, first, last, len(ties), min(rows, 256)),
        grid=(columns // tile,),
        in_specs=[pl.BlockSpec(memory_space=pltpu.SMEM), whole, whole]
        + [pl.BlockSpec((2, conv.shape[1], tile), lambda j: (0, 0, j)), whole_spec((1, width))]
        + cell_specs(cells, tile)
        + [whole] * (0 if first else 1)
        + [ANYWHERE] * len(ties),
        out_specs=out_specs,
        out_shape=outs,
        scratch_shapes=[
            pltpu.VMEM((kinds, width, 2 * tile), BF),
            pltpu.VMEM((rows, 2 * tile), BF),
        ],
        input_output_aliases={} if first else {7: 1},
        compiler_params=params(),
        cost_estimate=pl.CostEstimate(
            flops=16 * COST * rows * width * columns,
            bytes_accessed=24 * rows * columns + 16 * width * columns + 8 * rows * width,
            transcendentals=0,
        ),
    )(*inputs)


def mixer_back_kernel(first, ties, row_tile, *refs):
    feed = iter(refs)
    take = lambda n: [next(feed) for _ in range(n)]
    lengths, normed, grad_mix, project, conv = take(5)
    cells = take(2)
    before = [] if first else take(1)
    take(ties)
    keep, send, tap_grads, grad_normed = take(4)
    wide, branch, grads, grad_branch = take(4)
    step = pl.program_id(0)
    rows = normed.shape[0]
    _, zs, _, block, tile = cells[0].shape
    lay_out(*cells, wide)

    @pl.when(step == 0)
    def _():
        grad_normed[...] = jnp.zeros_like(grad_normed) if first else before[0][...]

    @pl.loop(0, rows // row_tile)
    def _(i):
        at = pl.ds(pl.multiple_of(i * row_tile, row_tile), row_tile)
        grad_branch[at, :] = dot_nn(grad_mix[at, :], wide[3])

    taps = tile_conv(conv[...])
    count = taps.shape[0]
    sums = [jnp.zeros((1, 2 * tile), F32)] * count
    for sequence in range(rows // SLOTS):
        at = slice(sequence * SLOTS, (sequence + 1) * SLOTS)
        position = lax.broadcasted_iota(jnp.int32, (SLOTS, 2 * tile), 0)
        living = position < lengths[sequence]
        gated = jnp.where(living, project[0, at] * project[2, at], 0.0)
        mixed = taps[0:1] * gated
        g_mixed = grad_branch[at, :] * project[1, at]
        sums[0] = sums[0] + jnp.sum(g_mixed * gated, axis=0, keepdims=True)
        g_gated = taps[0:1] * g_mixed
        for shift in range(1, count):
            lower = moved(gated, shift, position)
            mixed = mixed + taps[shift : shift + 1] * lower
            sums[shift] = sums[shift] + jnp.sum(g_mixed * lower, axis=0, keepdims=True)
            g_gated = g_gated + taps[shift : shift + 1] * moved(g_mixed, -shift, position)
        g_gated = jnp.where(living, g_gated, 0.0)
        branch[at, :] = (project[1, at] * mixed).astype(BF)
        grads[0, at, :] = (g_gated * project[2, at]).astype(BF)
        grads[1, at, :] = (grad_branch[at, :] * mixed).astype(BF)
        grads[2, at, :] = (g_gated * project[0, at]).astype(BF)
    tap_grads[...] = jnp.concatenate(
        sums + [jnp.zeros((8 - count, 2 * tile), F32)], axis=0
    )

    @pl.loop(0, rows // row_tile)
    def _(i):
        at = pl.ds(pl.multiple_of(i * row_tile, row_tile), row_tile)
        value = dot_nt(grads[0, at, :], wide[0]) + dot_nt(grads[1, at, :], wide[1])
        grad_normed[at, :] += value + dot_nt(grads[2, at, :], wide[2])

    depth = zs * block
    for place in range(4):
        at = slice(place * depth, (place + 1) * depth)
        core, x = divmod(place, 2)
        out = send if core else keep
        for k in range(4):
            if k < 3:
                value = dot_tn(normed[:, at], grads[k])
            else:
                value = dot_tn(grad_mix[:, at], branch[...])
            value = value.astype(BF)
            for z in range(zs):
                part = value[z * block : (z + 1) * block]
                out[2 * x, z, k] = part[:, :tile]
                out[2 * x + 1, z, k] = part[:, tile:]


def mixer_back(lengths, normed, grad_mix, project, conv, cells, before, ties):
    rows, width = normed.shape
    _, zs, kinds, block, columns = cells[0].shape
    first = before is None
    tile = MIXER_TILE
    whole = whole_spec((rows, width))
    inputs = [lengths, normed, grad_mix, project, conv, *cells]
    inputs += ([] if first else [before]) + list(ties)
    grads = pl.BlockSpec((4, zs, kinds, block, tile), lambda j: (0, 0, 0, 0, j))
    grad_shape = jax.ShapeDtypeStruct((4, zs, kinds, block, columns), BF)
    return pl.pallas_call(
        functools.partial(mixer_back_kernel, first, len(ties), min(rows, 256)),
        grid=(columns // tile,),
        in_specs=[pl.BlockSpec(memory_space=pltpu.SMEM), whole, whole]
        + [pl.BlockSpec((3, rows, 2 * tile), lambda j: (0, 0, j))]
        + [pl.BlockSpec((2, conv.shape[1], tile), lambda j: (0, 0, j))]
        + cell_specs(cells, tile)
        + [whole] * (0 if first else 1)
        + [ANYWHERE] * len(ties),
        out_specs=[grads, grads, pl.BlockSpec((8, 2 * tile), lambda j: (0, j)), whole],
        out_shape=[
            grad_shape,
            grad_shape,
            jax.ShapeDtypeStruct((8, 2 * columns), F32),
            jax.ShapeDtypeStruct((rows, width), F32),
        ],
        scratch_shapes=[
            pltpu.VMEM((kinds, width, 2 * tile), BF),
            pltpu.VMEM((rows, 2 * tile), BF),
            pltpu.VMEM((3, rows, 2 * tile), BF),
            pltpu.VMEM((rows, 2 * tile), F32),
        ],
        input_output_aliases={} if first else {7: 3},
        compiler_params=params(),
        cost_estimate=pl.CostEstimate(
            flops=32 * COST * rows * width * columns,
            bytes_accessed=24 * rows * columns + 32 * width * columns + 8 * rows * width,
            transcendentals=0,
        ),
    )(*inputs)


def norm_stats(values):
    inverse = lax.rsqrt(jnp.mean(values * values, axis=-1, keepdims=True) + EPS)
    return (inverse, values * inverse)


def norm_back(grad_normed, gain, inverse, unit):
    scaled = grad_normed * gain
    return inverse * (scaled - unit * jnp.mean(scaled * unit, axis=-1, keepdims=True))


def body(
    tokens,
    lengths,
    in_proj,
    conv_weight,
    out_proj,
    norm_gain,
    ffn_gain,
    w_gate,
    w_up,
    w_down,
    cotangent,
):
    rows, width = tokens.shape
    links = Links(lax.axis_size("dp"), lax.axis_size("tensor"))
    rank = lax.axis_index("tensor")
    kernel = conv_weight.shape[0]
    half = in_proj.shape[2]
    hidden_half = w_gate.shape[1]
    block = width // links.dp

    core = lax.axis_index("dp") % 2
    mixer_own = jnp.concatenate([in_proj.astype(BF), out_proj.T.astype(BF)[None]], axis=0)
    ffn_own = jnp.stack([w_gate.astype(BF), w_up.astype(BF), w_down.T.astype(BF)])
    part = half // MIXER_PARTS
    mixer_parts = [mixer_own[:, :, p * part : (p + 1) * part] for p in range(MIXER_PARTS)]
    shared = hidden_half // 2
    mine_of = lax.dynamic_slice_in_dim(ffn_own, core * shared, shared, 2)
    twin_of = lax.dynamic_slice_in_dim(ffn_own, (1 - core) * shared, shared, 2)
    ffn_both = jnp.stack([mine_of, links.swap(twin_of, c=1)])
    starts = [sum(SIZES[:p]) for p in range(len(SIZES))]
    own = mixer_parts + [
        ffn_both[..., at : at + size] for at, size in zip(starts, SIZES)
    ]
    pieces = len(own)
    mine, sides, corner, mixer_cells = {}, {}, {}, {}

    def cells(p):
        from_x, from_y = sides[p]
        return [mine[p], from_y, from_x, *corner[p]]

    def gather_stage(p, stage):
        if stage == 0:
            mine[p] = links.gather_z(own[p])
            return [mine[p]]
        if stage == 1:
            sides[p] = links.gather_sides(mine[p])
            return list(sides[p])
        if stage == 2:
            corner[p] = links.gather_corner(*sides[p])
            return list(corner[p])
        joined = join(*cells(p))
        mixer_cells[p] = [joined, links.swap(joined, c=1)]
        return []

    def gather_slot(p, stage):
        return p if stage == 3 else p + stage - (3 if p < MIXER_PARTS else 2)

    sums = {}

    def sum_stage(p, stage):
        item = sums[p]
        if stage == 1:
            got = links.swap(item["send"], c=1)
            item["parts"] = both_cores(item["keep"], got)
            return [got]
        send_x, send_y, rest_x, rest_y, mine_here = item["parts"]
        if stage == 2:
            item["got"] = links.swap(send_x, x=1), links.swap(send_y, y=1)
            return list(item["got"])
        if stage == 3:
            next_x, next_y = add_sides(rest_x, rest_y, *item["got"])
            item["sides"] = links.swap(next_x, x=1), links.swap(next_y, y=1)
            return list(item["sides"])
        item["z"] = links.turn_z(add_own(mine_here, *item["got"], *item["sides"]))
        return [item["z"]]

    done = set()

    def arrive(slot):
        ties = []
        for p in range(pieces):
            for stage in range(4 if p < MIXER_PARTS else 3):
                if (p, stage) not in done and gather_slot(p, stage) <= slot:
                    done.add((p, stage))
                    ties += gather_stage(p, stage)
        for p in list(sums):
            begin = 1 if p < MIXER_PARTS else 2
            for stage in range(begin, 5):
                due = sums[p]["slot"] + 2 + stage - begin
                if (p, -stage) not in done and due <= slot:
                    done.add((p, -stage))
                    ties += sum_stage(p, stage)
        return ties

    blocks = links.absolute(jnp.arange(links.dp))
    feature = jnp.repeat(blocks, block) * block + jnp.tile(jnp.arange(block), links.dp)
    order = (jnp.arange(width)[:, None] == feature[None, :]).astype(BF)
    tokens_f = dot_nn(tokens, order)
    cot = dot_nn(cotangent, order)
    gain_one = jnp.take(norm_gain.reshape(links.dp, block), blocks, axis=0).reshape(width)
    gain_two = jnp.take(ffn_gain.reshape(links.dp, block), blocks, axis=0).reshape(width)
    conv = jnp.where(rank == 0, conv_weight, jnp.roll(conv_weight, half, axis=1))

    count = rows // SLOTS
    own_lengths = lax.dynamic_slice_in_dim(lengths, rank * count, count)
    position = jnp.tile(jnp.arange(SLOTS, dtype=jnp.int32), count)
    alive = (position < jnp.repeat(own_lengths, SLOTS)).astype(F32)[:, None]
    conv = conv.reshape(kernel, 2, half).transpose(1, 0, 2)

    inverse_one, unit_one = norm_stats(tokens_f)
    normed = (unit_one * gain_one).astype(BF)
    grad_ffn = (cot * alive).astype(BF)
    grad_ffn_twin = links.swap(other_core_first(grad_ffn), c=1)
    tokens_low = tokens_f.astype(BF)

    slot = 0
    hidden, projects = None, []
    for p in range(MIXER_PARTS):
        ties = arrive(slot)
        last = p == MIXER_PARTS - 1
        project, hidden, *rest = mixer_part(
            own_lengths, normed, tokens_low, conv[:, :, p * part : (p + 1) * part],
            gain_two[None], mixer_cells[p], hidden, last, ties,
        )
        projects.append(project)
        slot += 1
    normed_two, for_twin = rest
    inputs = [normed_two, links.swap(for_twin, c=1), grad_ffn, grad_ffn_twin]

    totals = None
    for p in range(MIXER_PARTS, pieces):
        ties = arrive(slot)
        *parts, t0, t1, t2, t3 = ffn_piece(inputs, cells(p), totals, p == pieces - 1, ties)
        totals = [t0, t1, t2, t3]
        sums[p] = dict(parts=parts, slot=slot)
        slot += 1
    grad_normed_two = totals[1] + links.swap(totals[3], c=1).astype(F32)
    ffn_out = totals[0] + links.swap(totals[2], c=1).astype(F32)
    result = dot_nt((hidden + ffn_out).astype(BF), order).astype(BF)

    inverse_two, unit_two = norm_stats(hidden)
    grad_out = grad_ffn.astype(F32)
    gain_two_part = jnp.sum(grad_normed_two * unit_two, axis=0)
    grad_hidden = grad_out + norm_back(grad_normed_two, gain_two, inverse_two, unit_two)
    grad_mix = grad_hidden.astype(BF)
    grad_normed, tap_grads = None, [None] * MIXER_PARTS
    for p in reversed(range(MIXER_PARTS)):
        ties = arrive(slot)
        keep, send, tap_grads[p], grad_normed = mixer_back(
            own_lengths, normed, grad_mix, projects[p], conv[:, :, p * part : (p + 1) * part],
            mixer_cells[p], grad_normed, ties,
        )
        sums[p] = dict(keep=keep, send=send, slot=slot)
        slot += 1
    arrive(slot + 9)
    shards = [jnp.sum(sums[p]["z"].astype(F32), axis=0) for p in range(pieces)]
    mixer_shard = jnp.concatenate(shards[:MIXER_PARTS], axis=2)
    ffn_shard = jnp.concatenate(shards[MIXER_PARTS:], axis=3)
    here, there = ffn_shard[0], links.swap(ffn_shard[1], c=1)
    ffn_shard = jnp.concatenate(
        [jnp.where(core == 0, here, there), jnp.where(core == 0, there, here)], axis=2
    )
    gain_one_part = jnp.sum(grad_normed * unit_one, axis=0)
    grad_tokens = grad_hidden + norm_back(grad_normed, gain_one, inverse_one, unit_one)
    high = grad_tokens.astype(BF)
    rest = grad_tokens - high.astype(F32)
    middle = rest.astype(BF)
    low = (rest - middle.astype(F32)).astype(BF)
    grad_tokens = dot_nt(high, order) + (dot_nt(middle, order) + dot_nt(low, order))

    place = links.place(jnp.arange(links.dp))
    taps = jnp.concatenate(
        [
            item[:kernel].reshape(kernel, part // MIXER_TILE, 2, MIXER_TILE)
            for item in tap_grads
        ],
        axis=1,
    )
    taps = taps.transpose(0, 2, 1, 3).reshape(kernel, width)
    taps = jnp.where(rank == 0, taps, jnp.roll(taps, half, axis=1))
    gains = jnp.stack([gain_one_part, gain_two_part]).reshape(2, links.dp, block)
    gains = jnp.take(gains, place, axis=1).reshape(2, width)
    small = links.sum_all(jnp.concatenate([gains, taps], axis=0))

    return (
        result,
        grad_tokens,
        mixer_shard[:3],
        small[2:],
        mixer_shard[3].T,
        small[0],
        small[1],
        ffn_shard[0],
        ffn_shard[1],
        ffn_shard[2].T,
    )


def solution(mesh):
    rows = P(("dp", "tensor"), None)
    in_specs = (
        rows,
        P("dp"),
        P(None, "dp", "tensor"),
        P(),
        P("tensor", "dp"),
        P(),
        P(),
        P("dp", "tensor"),
        P("dp", "tensor"),
        P("tensor", "dp"),
        rows,
    )
    out_specs = (
        rows,
        rows,
        P(None, "dp", "tensor"),
        P(),
        P("tensor", "dp"),
        P(),
        P(),
        P("dp", "tensor"),
        P("dp", "tensor"),
        P("tensor", "dp"),
    )
    return jax.shard_map(body, mesh=mesh, in_specs=in_specs, out_specs=out_specs, check_vma=False)
```

```python
import functools

import jax
import jax.numpy as jnp
from jax import lax
from jax.experimental import pallas as pl
from jax.experimental.pallas import tpu as pltpu
from jax.sharding import PartitionSpec as P

SLOTS = 1024
EPS = 1e-05
AXES = ("dp", "tensor")
ROW_TILE = 256
SIZES = (256, 256, 384, 256)
COST = 4
VMEM = 60 * 2**20
BF = jnp.bfloat16
F32 = jnp.float32
ANYWHERE = pl.BlockSpec(memory_space=pl.ANY)


def dot_nn(left, right):
    return jnp.dot(left, right, preferred_element_type=F32)


def dot_tn(left, right):
    return lax.dot_general(left, right, (((0,), (0,)), ((), ())), preferred_element_type=F32)


def dot_nt(left, right):
    return lax.dot_general(left, right, (((1,), (1,)), ((), ())), preferred_element_type=F32)


class Links:
    def __init__(self, dp, tp):
        self.dp, self.tp, self.zs = dp, tp, dp // 4

    def swap(self, value, x=0, c=0, y=0, z=0):
        flip = (z * 2 + x) * 2 + c
        pairs = [
            (q * self.tp + t, (q ^ flip) * self.tp + (t ^ y))
            for q in range(self.dp)
            for t in range(self.tp)
        ]
        return lax.ppermute(value, AXES, pairs)

    def turn_z(self, value):
        groups = [[z * 4 + rest for z in range(self.zs)] for rest in range(4)]
        return lax.all_to_all(value, "dp", 0, 0, axis_index_groups=groups, tiled=True)

    def spread(self, own):
        return jnp.broadcast_to(own[None], (self.zs, *own.shape))

    def gather_sides(self, mine):
        return self.swap(mine, x=1), self.swap(mine, y=1)

    def gather_corner(self, from_x, from_y):
        half = self.zs // 2
        return self.swap(from_x[:half], y=1), self.swap(from_y[half:], x=1)

    def sum_chip(self, value):
        value = value + self.swap(value, c=1)
        return value + self.swap(value, y=1)

    def sum_rest(self, value):
        value = value + self.swap(value, x=1)
        step = 1
        while step < self.zs:
            value = value + self.swap(value, z=step)
            step *= 2
        return value

    def absolute(self, place):
        q = lax.axis_index("dp")
        core, x, z = place // (2 * self.zs), place // self.zs % 2, place % self.zs
        return z * 4 + ((q % 4) ^ (x * 2 + core))

    def place(self, absolute):
        q = lax.axis_index("dp")
        apart = (absolute % 4) ^ (q % 4)
        return ((apart % 2) * 2 + apart // 2) * self.zs + absolute // 4


def whole_spec(shape, buffers=1):
    return pl.BlockSpec(
        shape, lambda *_: (0,) * len(shape), pipeline_mode=pl.Buffered(buffers)
    )


def params():
    return pltpu.CompilerParams(vmem_limit_bytes=VMEM)


def cost(flops, moved_bytes):
    return pl.CostEstimate(flops=flops, bytes_accessed=moved_bytes, transcendentals=0)


def small_call(kernel, inputs, out_shapes, work):
    columns = inputs[0].shape[-1]

    def spec(shape):
        lead = len(shape) - 1
        return pl.BlockSpec(
            (*shape[:-1], 128), lambda j: (*(0,) * lead, j)
        )

    return pl.pallas_call(
        kernel,
        grid=(columns // 128,),
        in_specs=[spec(item.shape) for item in inputs],
        out_specs=[spec(shape) for shape in out_shapes],
        out_shape=[jax.ShapeDtypeStruct(shape, BF) for shape in out_shapes],
        compiler_params=params(),
        cost_estimate=cost(0, 2 * work),
    )(*inputs)


def gate(values):
    def nothing(*refs):
        del refs

    count = len(values)
    return pl.pallas_call(
        nothing,
        in_specs=[ANYWHERE] * count,
        out_specs=[ANYWHERE] * count,
        out_shape=[jax.ShapeDtypeStruct(item.shape, item.dtype) for item in values],
        input_output_aliases={i: i for i in range(count)},
        compiler_params=params(),
        cost_estimate=cost(0, 1024),
    )(*values)


def join_kernel(mine, from_y, from_x, one, two, out):
    half = one.shape[0]
    out[0] = mine[...]
    out[1] = from_y[...]
    out[2] = from_x[...]
    out[3, :half] = one[...]
    out[3, half:] = two[...]


def join(mine, from_y, from_x, one, two):
    shape = (4, *mine.shape)
    return small_call(
        join_kernel, [mine, from_y, from_x, one, two], [shape], 8 * mine.size
    )[0]


def both_kernel(keep, got, send_x, send_y, rest_x, rest_y, own):
    half = keep.shape[1] // 2

    def total(cell, part):
        return (keep[cell, part].astype(F32) + got[cell, part].astype(F32)).astype(BF)

    low, high = slice(0, half), slice(half, 2 * half)
    send_x[0], send_x[1] = total(3, low), total(2, low)
    send_y[0], send_y[1] = total(3, high), total(1, high)
    rest_x[...], rest_y[...] = total(2, high), total(1, low)
    own[:half], own[half:] = total(0, low), total(0, high)


def both_cores(keep, got):
    _, zs, *rest = keep.shape
    part = (zs // 2, *rest)
    shapes = [(2, *part), (2, *part), part, part, (zs, *rest)]
    return small_call(both_kernel, [keep, got], shapes, 3 * keep.size)


def sides_kernel(rest_x, rest_y, got_x, got_y, send_x, send_y):
    send_x[...] = (rest_x[...].astype(F32) + got_y[0].astype(F32)).astype(BF)
    send_y[...] = (rest_y[...].astype(F32) + got_x[0].astype(F32)).astype(BF)


def add_sides(rest_x, rest_y, got_x, got_y):
    return small_call(
        sides_kernel,
        [rest_x, rest_y, got_x, got_y],
        [rest_x.shape] * 2,
        8 * rest_x.size,
    )


def own_kernel(own, got_x, got_y, side_x, side_y, out):
    half = side_x.shape[0]
    low = own[:half].astype(F32) + got_x[1].astype(F32) + side_y[...].astype(F32)
    high = own[half:].astype(F32) + got_y[1].astype(F32) + side_x[...].astype(F32)
    out[:half] = low.astype(BF)
    out[half:] = high.astype(BF)


def add_own(own, got_x, got_y, side_x, side_y):
    return small_call(
        own_kernel, [own, got_x, got_y, side_x, side_y], [own.shape], 5 * own.size
    )[0]


def ffn_kernel(first, last, ties, *refs):
    feed = iter(refs)
    take = lambda n: [next(feed) for _ in range(n)]
    normed, normed_twin, grad_out, grad_out_twin = take(4)
    mine, from_y, from_x, one, two = take(5)
    before = [] if first else take(4)
    take(ties)
    send_x, send_y, rest_x, rest_y, own = take(5)
    totals = take(4)
    wide, rows_n, rows_g, active, grad_gate, grad_up = take(6)
    step = pl.program_id(0)
    steps = pl.num_programs(0)
    zs, _, kinds, block, tile = mine.shape
    half = zs // 2
    height = normed.shape[0]
    places = [(core, x, z) for core in range(2) for x in range(2) for z in range(zs)]

    @pl.when(step == 0)
    def _():
        for at, (core, x, z) in enumerate(places):
            rows = slice(at * block, (at + 1) * block)
            for k in range(kinds):
                if x == 0:
                    wide[k, rows, :tile] = mine[z, core, k]
                    wide[k, rows, tile:] = from_y[z, core, k]
                else:
                    wide[k, rows, :tile] = from_x[z, core, k]
                    corner = one[z, core, k] if z < half else two[z - half, core, k]
                    wide[k, rows, tile:] = corner

    at = pl.ds(pl.multiple_of(step * height, height), height)

    def work(normed, grad_out, before, totals, turn):
        left = normed[...]
        right = grad_out[...]
        rows_n[at, :] = left
        rows_g[at, :] = right
        gate, upward = dot_nn(left, wide[0]), dot_nn(left, wide[1])
        grad_active = dot_nn(right, wide[2])
        sigma = 1.0 / (1.0 + jnp.exp(-gate))
        silu = gate * sigma
        act = (silu * upward).astype(BF)
        g_up = (grad_active * silu).astype(BF)
        g_gate = (grad_active * upward * (sigma + silu * (1.0 - sigma))).astype(BF)
        active[at, :] = act
        grad_up[at, :] = g_up
        grad_gate[at, :] = g_gate
        ffn = dot_nt(act, wide[2])
        back = dot_nt(g_gate, wide[0]) + dot_nt(g_up, wide[1])
        if not first:
            ffn = ffn + before[0][...]
            back = back + before[1][...]
        if turn:
            ffn, back = other_core_first(ffn), other_core_first(back)
        totals[0][...] = ffn.astype(totals[0].dtype)
        totals[1][...] = back.astype(totals[1].dtype)

    @pl.when(step < steps // 2)
    def _():
        work(normed, grad_out, before[:2], totals[:2], False)

    @pl.when(step >= steps // 2)
    def _():
        work(normed_twin, grad_out_twin, before[2:], totals[2:], last)

    @pl.when(step == steps - 1)
    def _():
        group = 256 // block
        for first_place in range(0, len(places), group):
            rows = slice(first_place * block, (first_place + group) * block)
            for k, (left, right) in enumerate(
                ((rows_n, grad_gate), (rows_n, grad_up), (rows_g, active))
            ):
                value = dot_tn(left[:, rows], right[...]).astype(BF)
                for i in range(group):
                    core, x, z = places[first_place + i]
                    part = value[i * block : (i + 1) * block]
                    low, zh = z < half, z % half
                    near, far = part[:, :tile], part[:, tile:]
                    if x == 0:
                        own[z, core, k] = near
                        if low:
                            rest_y[zh, core, k] = far
                        else:
                            send_y[1, zh, core, k] = far
                    else:
                        if low:
                            send_x[1, zh, core, k] = near
                            send_x[0, zh, core, k] = far
                        else:
                            rest_x[zh, core, k] = near
                            send_y[0, zh, core, k] = far


def ffn_piece(inputs, cells, before, last, ties):
    rows, width = inputs[0].shape
    zs, _, kinds, block, columns = cells[0].shape
    first = before is None
    height = min(ROW_TILE, rows)
    half = rows // height
    near = pl.BlockSpec((height, width), lambda i: (jnp.minimum(i, half - 1), 0))
    far = pl.BlockSpec((height, width), lambda i: (jnp.maximum(i - half, 0), 0))
    operands = [*inputs, *cells, *(() if first else before), *ties]
    part = (zs // 2, 2, kinds, block, columns)
    grads = [(2, *part), (2, *part), part, part, (zs, *part[1:])]
    twin = BF if last else F32
    return pl.pallas_call(
        functools.partial(ffn_kernel, first, last, len(ties)),
        grid=(2 * half,),
        in_specs=[near, far, near, far]
        + [whole_spec(item.shape) for item in cells]
        + ([] if first else [near, near, far, far])
        + [ANYWHERE] * len(ties),
        out_specs=[whole_spec(shape) for shape in grads] + [near, near, far, far],
        out_shape=[jax.ShapeDtypeStruct(shape, BF) for shape in grads]
        + [jax.ShapeDtypeStruct((rows, width), dtype) for dtype in (F32, F32, twin, twin)],
        scratch_shapes=[pltpu.VMEM((kinds, width, 2 * columns), BF)]
        + [pltpu.VMEM((2 * rows, width), BF)] * 2
        + [pltpu.VMEM((2 * rows, 2 * columns), BF)] * 3,
        compiler_params=params(),
        cost_estimate=cost(
            72 * COST * rows * width * columns, 24 * width * columns + 40 * rows * width
        ),
    )(*operands)


def lay_out(near, twin, wide):
    _, zs, kinds, block, tile = near.shape
    for core, cells in enumerate((near, twin)):
        for x in range(2):
            for z in range(zs):
                at = ((core * 2 + x) * zs + z) * block
                for k in range(kinds):
                    for y in range(2):
                        wide[k, at : at + block, y * tile : (y + 1) * tile] = cells[
                            2 * x + y, z, k
                        ]


def cell_specs(cells, tile, skip=0):
    return [
        pl.BlockSpec((*item.shape[:-1], tile), lambda j: (0, 0, 0, 0, j + skip))
        for item in cells
    ]


def other_core_first(values):
    half = values.shape[1] // 2
    return jnp.concatenate([values[:, half:], values[:, :half]], axis=1)


def moved(values, shift, position):
    rows = values.shape[0]
    turned = pltpu.roll(values, shift % rows, 0)
    inside = position >= shift if shift > 0 else position < rows + shift
    return jnp.where(inside, turned, 0.0)


def mixed_of(gated, conv, position):
    total = conv[0:1] * gated
    for shift in range(1, conv.shape[0]):
        total = total + conv[shift : shift + 1] * moved(gated, shift, position)
    return total


def tile_conv(conv):
    return jnp.concatenate([conv[0], conv[1]], axis=1)


def mixer_kernel(first, last, ties, row_tile, *refs):
    feed = iter(refs)
    take = lambda n: [next(feed) for _ in range(n)]
    lengths, normed, tokens, conv, gain = take(5)
    cells = take(2)
    before = [] if first else take(1)
    take(ties)
    project, hidden = take(2)
    normed_two, for_twin = take(2) if last else (None, None)
    wide, branch = take(2)
    step = pl.program_id(0)
    rows = normed.shape[0]
    lay_out(*cells, wide)

    @pl.loop(0, rows // row_tile)
    def _(i):
        at = pl.ds(pl.multiple_of(i * row_tile, row_tile), row_tile)
        left = normed[at, :]
        for k in range(3):
            project[k, at, :] = dot_nn(left, wide[k])

    taps = tile_conv(conv[...])
    for sequence in range(rows // SLOTS):
        at = slice(sequence * SLOTS, (sequence + 1) * SLOTS)
        position = lax.broadcasted_iota(jnp.int32, (SLOTS, wide.shape[2]), 0)
        gated = project[0, at] * project[2, at]
        gated = jnp.where(position < lengths[sequence], gated, 0.0)
        branch[at, :] = (project[1, at] * mixed_of(gated, taps, position)).astype(BF)

    @pl.when(step == 0)
    def _():
        if first:
            hidden[...] = tokens[...].astype(F32)
        else:
            hidden[...] = before[0][...]

    ending = step == pl.num_programs(0) - 1

    @pl.loop(0, rows // row_tile)
    def _(i):
        at = pl.ds(pl.multiple_of(i * row_tile, row_tile), row_tile)
        value = hidden[at, :] + dot_nt(branch[at, :], wide[3])
        hidden[at, :] = value
        if last:

            @pl.when(ending)
            def _():
                unit = norm_stats(value)[1]
                value_two = (unit * gain[...]).astype(BF)
                normed_two[at, :] = value_two
                for_twin[at, :] = other_core_first(value_two)


def mixer_part(lengths, normed, tokens, conv, gain, cells, before, last, ties, tile):
    rows, width = normed.shape
    _, zs, kinds, block, columns = cells[0].shape
    first = before is None
    whole = whole_spec((rows, width))
    inputs = [lengths, normed, tokens, conv, gain, *cells]
    inputs += ([] if first else [before]) + list(ties)
    outs = [jax.ShapeDtypeStruct((3, rows, 2 * columns), F32), jax.ShapeDtypeStruct((rows, width), F32)]
    out_specs = [pl.BlockSpec((3, rows, 2 * tile), lambda j: (0, 0, j)), whole]
    if last:
        outs += [jax.ShapeDtypeStruct((rows, width), BF)] * 2
        out_specs += [whole] * 2
    return pl.pallas_call(
        functools.partial(mixer_kernel, first, last, len(ties), min(rows, 256)),
        grid=(columns // tile,),
        in_specs=[pl.BlockSpec(memory_space=pltpu.SMEM), whole, whole]
        + [pl.BlockSpec((2, conv.shape[1], tile), lambda j: (0, 0, j)), whole_spec((1, width))]
        + cell_specs(cells, tile)
        + [whole] * (0 if first else 1)
        + [ANYWHERE] * len(ties),
        out_specs=out_specs,
        out_shape=outs,
        scratch_shapes=[
            pltpu.VMEM((kinds, width, 2 * tile), BF),
            pltpu.VMEM((rows, 2 * tile), BF),
        ],
        input_output_aliases={} if first else {7: 1},
        compiler_params=params(),
        cost_estimate=pl.CostEstimate(
            flops=16 * COST * rows * width * columns,
            bytes_accessed=24 * rows * columns + 16 * width * columns + 8 * rows * width,
            transcendentals=0,
        ),
    )(*inputs)


def mixer_back_kernel(first, ties, row_tile, *refs):
    feed = iter(refs)
    take = lambda n: [next(feed) for _ in range(n)]
    lengths, normed, grad_mix, project, conv = take(5)
    cells = take(2)
    before = [] if first else take(1)
    take(ties)
    keep, send, tap_grads, grad_normed = take(4)
    wide, branch, grads, grad_branch = take(4)
    step = pl.program_id(0)
    rows = normed.shape[0]
    _, zs, _, block, tile = cells[0].shape
    lay_out(*cells, wide)

    @pl.when(step == 0)
    def _():
        grad_normed[...] = jnp.zeros_like(grad_normed) if first else before[0][...]

    @pl.loop(0, rows // row_tile)
    def _(i):
        at = pl.ds(pl.multiple_of(i * row_tile, row_tile), row_tile)
        grad_branch[at, :] = dot_nn(grad_mix[at, :], wide[3])

    taps = tile_conv(conv[...])
    count = taps.shape[0]
    sums = [jnp.zeros((1, 2 * tile), F32)] * count
    for sequence in range(rows // SLOTS):
        at = slice(sequence * SLOTS, (sequence + 1) * SLOTS)
        position = lax.broadcasted_iota(jnp.int32, (SLOTS, 2 * tile), 0)
        living = position < lengths[sequence]
        gated = jnp.where(living, project[0, at] * project[2, at], 0.0)
        mixed = taps[0:1] * gated
        g_mixed = grad_branch[at, :] * project[1, at]
        sums[0] = sums[0] + jnp.sum(g_mixed * gated, axis=0, keepdims=True)
        g_gated = taps[0:1] * g_mixed
        for shift in range(1, count):
            lower = moved(gated, shift, position)
            mixed = mixed + taps[shift : shift + 1] * lower
            sums[shift] = sums[shift] + jnp.sum(g_mixed * lower, axis=0, keepdims=True)
            g_gated = g_gated + taps[shift : shift + 1] * moved(g_mixed, -shift, position)
        g_gated = jnp.where(living, g_gated, 0.0)
        branch[at, :] = (project[1, at] * mixed).astype(BF)
        grads[0, at, :] = (g_gated * project[2, at]).astype(BF)
        grads[1, at, :] = (grad_branch[at, :] * mixed).astype(BF)
        grads[2, at, :] = (g_gated * project[0, at]).astype(BF)
    tap_grads[...] = jnp.concatenate(
        sums + [jnp.zeros((8 - count, 2 * tile), F32)], axis=0
    )

    @pl.loop(0, rows // row_tile)
    def _(i):
        at = pl.ds(pl.multiple_of(i * row_tile, row_tile), row_tile)
        value = dot_nt(grads[0, at, :], wide[0]) + dot_nt(grads[1, at, :], wide[1])
        grad_normed[at, :] += value + dot_nt(grads[2, at, :], wide[2])

    depth = zs * block
    for place in range(4):
        at = slice(place * depth, (place + 1) * depth)
        core, x = divmod(place, 2)
        out = send if core else keep
        for k in range(4):
            if k < 3:
                value = dot_tn(normed[:, at], grads[k])
            else:
                value = dot_tn(grad_mix[:, at], branch[...])
            value = value.astype(BF)
            for z in range(zs):
                part = value[z * block : (z + 1) * block]
                out[2 * x, z, k] = part[:, :tile]
                out[2 * x + 1, z, k] = part[:, tile:]


def mixer_back(lengths, normed, grad_mix, project, conv, cells, before, ties, tile, part, parts):
    rows, width = normed.shape
    _, zs, kinds, block, columns = cells[0].shape
    columns = columns // parts
    skip = part * (columns // tile)
    first = before is None
    whole = whole_spec((rows, width))
    inputs = [lengths, normed, grad_mix, project, conv, *cells]
    inputs += ([] if first else [before]) + list(ties)
    grads = pl.BlockSpec((4, zs, kinds, block, tile), lambda j: (0, 0, 0, 0, j))
    grad_shape = jax.ShapeDtypeStruct((4, zs, kinds, block, columns), BF)
    return pl.pallas_call(
        functools.partial(mixer_back_kernel, first, len(ties), min(rows, 256)),
        grid=(columns // tile,),
        in_specs=[pl.BlockSpec(memory_space=pltpu.SMEM), whole, whole]
        + [pl.BlockSpec((3, rows, 2 * tile), lambda j: (0, 0, j + skip))]
        + [pl.BlockSpec((2, conv.shape[1], tile), lambda j: (0, 0, j + skip))]
        + cell_specs(cells, tile, skip)
        + [whole] * (0 if first else 1)
        + [ANYWHERE] * len(ties),
        out_specs=[grads, grads, pl.BlockSpec((8, 2 * tile), lambda j: (0, j)), whole],
        out_shape=[
            grad_shape,
            grad_shape,
            jax.ShapeDtypeStruct((8, 2 * columns), F32),
            jax.ShapeDtypeStruct((rows, width), F32),
        ],
        scratch_shapes=[
            pltpu.VMEM((kinds, width, 2 * tile), BF),
            pltpu.VMEM((rows, 2 * tile), BF),
            pltpu.VMEM((3, rows, 2 * tile), BF),
            pltpu.VMEM((rows, 2 * tile), F32),
        ],
        input_output_aliases={} if first else {7: 3},
        compiler_params=params(),
        cost_estimate=pl.CostEstimate(
            flops=32 * COST * rows * width * columns,
            bytes_accessed=24 * rows * columns + 32 * width * columns + 8 * rows * width,
            transcendentals=0,
        ),
    )(*inputs)


def reorder(source, target, flip, inward):
    width = source.shape[1]
    for case in range(4):

        @pl.when(flip == case)
        def _():
            count = SHARDS[0]
            block, zs = width // count, count // 4
            for place in range(count):
                core, x, z = place // (2 * zs), place // zs % 2, place % zs
                absolute = z * 4 + (case ^ (x * 2 + core))
                here = slice(place * block, (place + 1) * block)
                there = slice(absolute * block, (absolute + 1) * block)
                if inward:
                    target[:, here] = source[:, there]
                else:
                    target[:, there] = source[:, here]


def row_call(kernel, flip, inputs, outs, sums=0, ties=()):
    rows, width = next(item.shape for item in inputs if item.shape[0] > 1)
    height = min(ROW_TILE, rows)
    tiled = pl.BlockSpec((height, width), lambda i: (i, 0))
    scalar = pl.BlockSpec(memory_space=pltpu.SMEM)
    specs = [
        scalar if item.ndim == 1 else tiled if item.shape[0] > 1 else whole_spec((1, width))
        for item in inputs
    ]
    count = len(inputs) + 1

    def body(*refs):
        kernel(*refs[:count], *refs[count + len(ties) :])

    return pl.pallas_call(
        body,
        grid=(rows // height,),
        in_specs=[scalar] + specs + [ANYWHERE] * len(ties),
        out_specs=[tiled] * len(outs) + [whole_spec((8, width))] * sums,
        out_shape=[jax.ShapeDtypeStruct((rows, width), dtype) for dtype in outs]
        + [jax.ShapeDtypeStruct((8, width), F32)] * sums,
        scratch_shapes=[pltpu.VMEM((height, width), F32)] * 2,
        compiler_params=params(),
        cost_estimate=cost(20 * rows * width, 12 * rows * width),
    )(flip, *inputs, *ties)


def enter_kernel(flip, lengths, tokens, cotangent, gain, low, normed, grad, for_twin, one, two):
    one[...] = tokens[...].astype(F32)
    reorder(one, two, flip[0], True)
    value = two[...]
    low[...] = value.astype(BF)
    normed[...] = (norm_stats(value)[1] * gain[...]).astype(BF)
    one[...] = cotangent[...].astype(F32)
    reorder(one, two, flip[0], True)
    height = value.shape[0]
    first = pl.program_id(0) * height
    position = first % SLOTS + lax.broadcasted_iota(jnp.int32, value.shape, 0)
    value = jnp.where(position < lengths[first // SLOTS], two[...], 0.0).astype(BF)
    grad[...] = value
    for_twin[...] = other_core_first(value)


def add_up(total, values):
    part = jnp.sum(values.reshape(-1, 8, values.shape[1]), axis=0)

    @pl.when(pl.program_id(0) == 0)
    def _():
        total[...] = part

    @pl.when(pl.program_id(0) > 0)
    def _():
        total[...] += part


def between_kernel(flip, mine, twin, hidden, grad_out, gain, mix, grad_hidden, total, one, two):
    grad = mine[...] + twin[...].astype(F32)
    inverse, unit = norm_stats(hidden[...])
    value = grad_out[...].astype(F32) + norm_back(grad, gain[...], inverse, unit)
    mix[...] = value.astype(BF)
    grad_hidden[...] = value
    add_up(total, grad * unit)


def leave_kernel(flip, grad, tokens, grad_hidden, gain, out, total, one, two):
    inverse, unit = norm_stats(tokens[...].astype(F32))
    value = grad[...]
    one[...] = grad_hidden[...] + norm_back(value, gain[...], inverse, unit)
    reorder(one, out, flip[0], False)
    add_up(total, value * unit)


def result_kernel(flip, hidden, mine, twin, out, one, two):
    one[...] = hidden[...] + mine[...] + twin[...].astype(F32)
    reorder(one, two, flip[0], False)
    out[...] = two[...].astype(BF)


SHARDS = [16]


def ffn_sizes(columns, rows):
    if rows <= 1024 and columns == sum(SIZES):
        return SIZES
    return (128,) * (columns // 128)


def norm_stats(values):
    inverse = lax.rsqrt(jnp.mean(values * values, axis=-1, keepdims=True) + EPS)
    return (inverse, values * inverse)


def norm_back(grad_normed, gain, inverse, unit):
    scaled = grad_normed * gain
    return inverse * (scaled - unit * jnp.mean(scaled * unit, axis=-1, keepdims=True))


def body(
    tokens,
    lengths,
    in_proj,
    conv_weight,
    out_proj,
    norm_gain,
    ffn_gain,
    w_gate,
    w_up,
    w_down,
    cotangent,
):
    rows, width = tokens.shape
    links = Links(lax.axis_size("dp"), lax.axis_size("tensor"))
    rank = lax.axis_index("tensor")
    kernel = conv_weight.shape[0]
    half = in_proj.shape[2]
    hidden_half = w_gate.shape[1]
    block = width // links.dp

    core = lax.axis_index("dp") % 2
    mixer_own = jnp.concatenate([in_proj.astype(BF), out_proj.T.astype(BF)[None]], axis=0)
    ffn_own = jnp.stack([w_gate.astype(BF), w_up.astype(BF), w_down.T.astype(BF)])
    tile = 256 if half % 512 == 0 and rows <= 1024 else 128
    shared = hidden_half // 2
    mine_of = lax.dynamic_slice_in_dim(ffn_own, core * shared, shared, 2)
    twin_of = lax.dynamic_slice_in_dim(ffn_own, (1 - core) * shared, shared, 2)
    ffn_both = jnp.stack([mine_of, links.swap(twin_of, c=1)])
    sizes = ffn_sizes(shared, rows)
    starts = [sum(sizes[:p]) for p in range(len(sizes))]
    own = [mixer_own] + [ffn_both[..., at : at + size] for at, size in zip(starts, sizes)]
    own = [links.spread(item) for item in own]
    pieces = len(own)
    last = pieces - 1
    mine, sides, corner = {}, {}, {}

    def cells(p):
        from_x, from_y = sides[p]
        return [mine[p], from_y, from_x, *corner[p]]

    sums = {}

    def start(stage, p):
        if stage == "z":
            mine[p] = links.turn_z(own[p])
            return mine, p
        if stage == "sides":
            sides[p] = links.gather_sides(mine[p])
            return sides, p
        if stage == "corner":
            corner[p] = links.gather_corner(*sides[p])
            return corner, p
        item = sums[p]
        if stage == "sum core":
            item["got"] = links.swap(item["send"], c=1)
            return item, "got"
        if stage == "sum corner":
            if "keep" in item:
                item["parts"] = both_cores(item["keep"], item["got"])
            send_x, send_y = item["parts"][:2]
            item["corner"] = links.swap(send_x, x=1), links.swap(send_y, y=1)
            return item, "corner"
        rest_x, rest_y, here = item["parts"][2:]
        if stage == "sum sides":
            next_x, next_y = add_sides(rest_x, rest_y, *item["corner"])
            item["sides"] = links.swap(next_x, x=1), links.swap(next_y, y=1)
            return item, "sides"
        item["z"] = links.turn_z(add_own(here, *item["corner"], *item["sides"]))
        return item, "z"

    def close(kept, places):
        kept, tree = jax.tree.flatten([kept, [store[key] for store, key in places]])
        kept, arrived = jax.tree.unflatten(tree, gate(kept))
        for (store, key), value in zip(places, arrived):
            store[key] = value
        return kept

    blocks = links.absolute(jnp.arange(links.dp))
    gain_one = jnp.take(norm_gain.reshape(links.dp, block), blocks, axis=0).reshape(1, width)
    gain_two = jnp.take(ffn_gain.reshape(links.dp, block), blocks, axis=0).reshape(1, width)
    conv = jnp.where(rank == 0, conv_weight, jnp.roll(conv_weight, half, axis=1))
    conv = conv.reshape(kernel, 2, half).transpose(1, 0, 2)
    count = rows // SLOTS
    own_lengths = lax.dynamic_slice_in_dim(lengths, rank * count, count)
    flip = (lax.axis_index("dp") % 4)[None]
    SHARDS[0] = links.dp
    tokens_low, normed, grad_ffn, for_twin_grad = row_call(
        enter_kernel, flip, [own_lengths, tokens, cotangent, gain_one], [BF] * 4, ties=own[1:]
    )

    places = [start("z", 0)]
    normed, for_twin_grad, own = close([normed, for_twin_grad, own], places)
    grad_ffn_twin = links.swap(for_twin_grad, c=1)
    places = [start("sides", 0), start("z", 1)]
    own[2:3], mine[0] = close([own[2:3], mine[0]], places)
    places = [start("corner", 0), start("z", 2)]
    own[3:4], mine[1] = close([own[3:4], mine[1]], places)
    joined = join(*cells(0))
    mixer_cells = [joined, links.swap(joined, c=1)]

    places = [start("sides", 1), start("sides", 2), start("z", 3)]
    project, hidden, normed_two, for_twin = mixer_part(
        own_lengths, normed, tokens_low, conv, gain_two, mixer_cells, None, True, [], tile
    )
    normed_two, for_twin, own[4:5] = close([normed_two, for_twin, own[4:5]], places)
    start("corner", 1)
    inputs = [normed_two, links.swap(for_twin, c=1), grad_ffn, grad_ffn_twin]

    totals = None
    for p in range(1, pieces):
        places = []
        for stage, q in (("corner", p + 1), ("sides", p + 2), ("z", p + 3)):
            if q < pieces:
                places.append(start(stage, q))
        for stage, q in (("sum z", p - 4), ("sum sides", p - 3), ("sum corner", p - 2)):
            if q > 0:
                places.append(start(stage, q))
        *parts, t0, t1, t2, t3 = ffn_piece(inputs, cells(p), totals, p == last, [])
        parts, totals = close([parts, [t0, t1, t2, t3]], places)
        sums[p] = dict(parts=parts)
    grad_mix, grad_hidden, gain_two_part = row_call(
        between_kernel,
        flip,
        [totals[1], links.swap(totals[3], c=1), hidden, grad_ffn, gain_two],
        [BF, F32],
        1,
    )
    places = [
        start("sum z", last - 3),
        start("sum sides", last - 2),
        start("sum corner", last - 1),
    ]
    parts = 2 if half % 256 == 0 else 1
    names = [f"mixer {p}" for p in range(parts)]
    grad_normed, taps = None, []
    for p, name in enumerate(names):
        if p:
            places = [start("sum core", names[0])]
        if p == parts - 1:
            later = [start("sum z", last - 2), start("sum sides", last - 1)]
            later.append(start("sum corner", last))
            places += later
        keep, send, tap_grads, grad_normed = mixer_back(
            own_lengths, normed, grad_mix, project, conv, mixer_cells, grad_normed, [],
            tile, p, parts,
        )
        keep, send, tap_grads, grad_normed, totals[0], totals[2] = close(
            [keep, send, tap_grads, grad_normed, totals[0], totals[2]], places
        )
        taps.append(tap_grads)
        sums[name] = dict(keep=keep, send=send)
    places = [start("sum core", names[-1]), start("sum z", last - 1), start("sum sides", last)]
    if parts > 1:
        places.append(start("sum corner", names[0]))
    grad_tokens, gain_one_part = row_call(
        leave_kernel, flip, [grad_normed, tokens_low, grad_hidden, gain_one], [F32], 1
    )
    item = sums[names[-1]]
    grad_tokens, gain_one_part, item["keep"] = close(
        [grad_tokens, gain_one_part, item["keep"]], places
    )

    place = links.place(jnp.arange(links.dp))
    taps = jnp.concatenate(taps, axis=1)[:kernel].reshape(kernel, -1, 2, tile)
    taps = taps.transpose(0, 2, 1, 3).reshape(kernel, width)
    taps = jnp.where(rank == 0, taps, jnp.roll(taps, half, axis=1))
    gains = jnp.stack([gain_one_part.sum(0), gain_two_part.sum(0)])
    gains = jnp.take(gains.reshape(2, links.dp, block), place, axis=1).reshape(2, width)
    small = links.sum_chip(jnp.concatenate([gains, taps], axis=0))

    places = [start("sum corner", names[-1]), start("sum z", last)]
    if parts > 1:
        places.append(start("sum sides", names[0]))
    result = row_call(
        result_kernel, flip, [hidden, totals[0], links.swap(totals[2], c=1)], [BF]
    )[0]
    result, small = close([result, small], places)
    places = [start("sum sides", names[-1])]
    if parts > 1:
        places.append(start("sum z", names[0]))
    (small,) = close([links.sum_rest(small)], places)
    start("sum z", names[-1])
    shard = lambda p: jnp.sum(sums[p]["z"].astype(F32), axis=0)
    mixer_shard = jnp.concatenate([shard(name) for name in names], axis=2)
    ffn_shard = jnp.concatenate([shard(p) for p in range(1, pieces)], axis=3)
    here, there = ffn_shard[0], links.swap(ffn_shard[1], c=1)
    ffn_shard = jnp.concatenate(
        [jnp.where(core == 0, here, there), jnp.where(core == 0, there, here)], axis=2
    )
    return (
        result,
        grad_tokens,
        mixer_shard[:3],
        small[2:],
        mixer_shard[3].T,
        small[0],
        small[1],
        ffn_shard[0],
        ffn_shard[1],
        ffn_shard[2].T,
    )


def solution(mesh):
    rows = P(("dp", "tensor"), None)
    in_specs = (
        rows,
        P("dp"),
        P(None, "dp", "tensor"),
        P(),
        P("tensor", "dp"),
        P(),
        P(),
        P("dp", "tensor"),
        P("dp", "tensor"),
        P("tensor", "dp"),
        rows,
    )
    out_specs = (
        rows,
        rows,
        P(None, "dp", "tensor"),
        P(),
        P("tensor", "dp"),
        P(),
        P(),
        P("dp", "tensor"),
        P("dp", "tensor"),
        P("tensor", "dp"),
    )
    return jax.shard_map(body, mesh=mesh, in_specs=in_specs, out_specs=out_specs, check_vma=False)
```

```python
import functools

import jax
import jax.numpy as jnp
from jax import lax
from jax.experimental import pallas as pl
from jax.experimental.pallas import tpu as pltpu
from jax.sharding import PartitionSpec as P

SLOTS = 1024
EPS = 1e-05
AXES = ("dp", "tensor")
ROW_TILE = 256
SIZES = (256, 256, 384, 256)
COST = 4
VMEM = 60 * 2**20
BF = jnp.bfloat16
F32 = jnp.float32
ANYWHERE = pl.BlockSpec(memory_space=pl.ANY)


def dot_nn(left, right):
    return jnp.dot(left, right, preferred_element_type=F32)


def dot_tn(left, right):
    return lax.dot_general(left, right, (((0,), (0,)), ((), ())), preferred_element_type=F32)


def dot_nt(left, right):
    return lax.dot_general(left, right, (((1,), (1,)), ((), ())), preferred_element_type=F32)


class Links:
    def __init__(self, dp, tp):
        self.dp, self.tp, self.zs = dp, tp, dp // 4

    def swap(self, value, x=0, c=0, y=0, z=0):
        flip = (z * 2 + x) * 2 + c
        pairs = [
            (q * self.tp + t, (q ^ flip) * self.tp + (t ^ y))
            for q in range(self.dp)
            for t in range(self.tp)
        ]
        return lax.ppermute(value, AXES, pairs)

    def turn_z(self, value):
        groups = [[z * 4 + rest for z in range(self.zs)] for rest in range(4)]
        return lax.all_to_all(value, "dp", 0, 0, axis_index_groups=groups, tiled=True)

    def spread(self, own):
        return jnp.broadcast_to(own[None], (self.zs, *own.shape))

    def gather_sides(self, mine):
        return self.swap(mine, x=1), self.swap(mine, y=1)

    def gather_corner(self, from_x, from_y):
        low, high = cut(from_x, from_y)
        return self.swap(low, y=1), self.swap(high, x=1)

    def sum_chip(self, value):
        value = value + self.swap(value, c=1)
        return value + self.swap(value, y=1)

    def sum_rest(self, value):
        value = value + self.swap(value, x=1)
        step = 1
        while step < self.zs:
            value = value + self.swap(value, z=step)
            step *= 2
        return value

    def absolute(self, place):
        q = lax.axis_index("dp")
        core, x, z = place // (2 * self.zs), place // self.zs % 2, place % self.zs
        return z * 4 + ((q % 4) ^ (x * 2 + core))

    def place(self, absolute):
        q = lax.axis_index("dp")
        apart = (absolute % 4) ^ (q % 4)
        return ((apart % 2) * 2 + apart // 2) * self.zs + absolute // 4


def whole_spec(shape, buffers=1):
    return pl.BlockSpec(
        shape, lambda *_: (0,) * len(shape), pipeline_mode=pl.Buffered(buffers)
    )


def params():
    return pltpu.CompilerParams(vmem_limit_bytes=VMEM)


def cost(flops, moved_bytes):
    return pl.CostEstimate(flops=flops, bytes_accessed=moved_bytes, transcendentals=0)


def small_call(kernel, inputs, out_shapes, work):
    columns = inputs[0].shape[-1]

    def spec(shape):
        lead = len(shape) - 1
        return pl.BlockSpec(
            (*shape[:-1], 128), lambda j: (*(0,) * lead, j)
        )

    return pl.pallas_call(
        kernel,
        grid=(columns // 128,),
        in_specs=[spec(item.shape) for item in inputs],
        out_specs=[spec(shape) for shape in out_shapes],
        out_shape=[jax.ShapeDtypeStruct(shape, BF) for shape in out_shapes],
        compiler_params=params(),
        cost_estimate=cost(0, 2 * work),
    )(*inputs)


def gate(values):
    def nothing(*refs):
        del refs

    count = len(values)
    return pl.pallas_call(
        nothing,
        in_specs=[ANYWHERE] * count,
        out_specs=[ANYWHERE] * count,
        out_shape=[jax.ShapeDtypeStruct(item.shape, item.dtype) for item in values],
        input_output_aliases={i: i for i in range(count)},
        compiler_params=params(),
        cost_estimate=cost(0, 1024),
    )(*values)


def cut_kernel(from_x, from_y, low, high):
    low[...] = from_x[...]
    high[...] = from_y[...]


def cut(from_x, from_y):
    half, *rest, columns = from_x.shape
    half //= 2
    lead = (0,) * len(rest)
    block = (half, *rest, 128)
    low = pl.BlockSpec(block, lambda j: (0, *lead, j))
    high = pl.BlockSpec(block, lambda j: (1, *lead, j))
    return pl.pallas_call(
        cut_kernel,
        grid=(columns // 128,),
        in_specs=[low, high],
        out_specs=[low] * 2,
        out_shape=[jax.ShapeDtypeStruct((half, *rest, columns), BF)] * 2,
        compiler_params=params(),
        cost_estimate=cost(0, 4 * from_x.size),
    )(from_x, from_y)


def join_kernel(mine, from_y, from_x, one, two, out):
    half = one.shape[0]
    out[0] = mine[...]
    out[1] = from_y[...]
    out[2] = from_x[...]
    out[3, :half] = one[...]
    out[3, half:] = two[...]


def join(mine, from_y, from_x, one, two):
    shape = (4, *mine.shape)
    return small_call(
        join_kernel, [mine, from_y, from_x, one, two], [shape], 8 * mine.size
    )[0]


def both_kernel(keep, got, send_x, send_y, rest_x, rest_y, own):
    half = keep.shape[1] // 2

    def total(cell, part):
        return (keep[cell, part].astype(F32) + got[cell, part].astype(F32)).astype(BF)

    low, high = slice(0, half), slice(half, 2 * half)
    send_x[0], send_x[1] = total(3, low), total(2, low)
    send_y[0], send_y[1] = total(3, high), total(1, high)
    rest_x[...], rest_y[...] = total(2, high), total(1, low)
    own[:half], own[half:] = total(0, low), total(0, high)


def both_cores(keep, got):
    _, zs, *rest = keep.shape
    part = (zs // 2, *rest)
    shapes = [(2, *part), (2, *part), part, part, (zs, *rest)]
    return small_call(both_kernel, [keep, got], shapes, 3 * keep.size)


def sides_kernel(rest_x, rest_y, got_x, got_y, send_x, send_y):
    send_x[...] = (rest_x[...].astype(F32) + got_y[0].astype(F32)).astype(BF)
    send_y[...] = (rest_y[...].astype(F32) + got_x[0].astype(F32)).astype(BF)


def add_sides(rest_x, rest_y, got_x, got_y):
    return small_call(
        sides_kernel,
        [rest_x, rest_y, got_x, got_y],
        [rest_x.shape] * 2,
        8 * rest_x.size,
    )


def own_kernel(own, got_x, got_y, side_x, side_y, out):
    half = side_x.shape[0]
    low = own[:half].astype(F32) + got_x[1].astype(F32) + side_y[...].astype(F32)
    high = own[half:].astype(F32) + got_y[1].astype(F32) + side_x[...].astype(F32)
    out[:half] = low.astype(BF)
    out[half:] = high.astype(BF)


def add_own(own, got_x, got_y, side_x, side_y):
    return small_call(
        own_kernel, [own, got_x, got_y, side_x, side_y], [own.shape], 5 * own.size
    )[0]


def ffn_kernel(first, last, ties, *refs):
    feed = iter(refs)
    take = lambda n: [next(feed) for _ in range(n)]
    normed, normed_twin, grad_out, grad_out_twin = take(4)
    mine, from_y, from_x, one, two = take(5)
    before = [] if first else take(4)
    take(ties)
    send_x, send_y, rest_x, rest_y, own = take(5)
    totals = take(4)
    wide, rows_n, rows_g, active, grad_gate, grad_up = take(6)
    step = pl.program_id(0)
    steps = pl.num_programs(0)
    zs, _, kinds, block, tile = mine.shape
    half = zs // 2
    height = normed.shape[0]
    places = [(core, x, z) for core in range(2) for x in range(2) for z in range(zs)]

    @pl.when(step == 0)
    def _():
        for at, (core, x, z) in enumerate(places):
            rows = slice(at * block, (at + 1) * block)
            for k in range(kinds):
                if x == 0:
                    wide[k, rows, :tile] = mine[z, core, k]
                    wide[k, rows, tile:] = from_y[z, core, k]
                else:
                    wide[k, rows, :tile] = from_x[z, core, k]
                    corner = one[z, core, k] if z < half else two[z - half, core, k]
                    wide[k, rows, tile:] = corner

    at = pl.ds(pl.multiple_of(step * height, height), height)

    def work(normed, grad_out, before, totals, turn):
        left = normed[...]
        right = grad_out[...]
        rows_n[at, :] = left
        rows_g[at, :] = right
        gate, upward = dot_nn(left, wide[0]), dot_nn(left, wide[1])
        grad_active = dot_nn(right, wide[2])
        sigma = 1.0 / (1.0 + jnp.exp(-gate))
        silu = gate * sigma
        act = (silu * upward).astype(BF)
        g_up = (grad_active * silu).astype(BF)
        g_gate = (grad_active * upward * (sigma + silu * (1.0 - sigma))).astype(BF)
        active[at, :] = act
        grad_up[at, :] = g_up
        grad_gate[at, :] = g_gate
        ffn = dot_nt(act, wide[2])
        back = dot_nt(g_gate, wide[0]) + dot_nt(g_up, wide[1])
        if not first:
            ffn = ffn + before[0][...].astype(F32)
            back = back + before[1][...].astype(F32)
        if turn:
            ffn, back = other_core_first(ffn), other_core_first(back)
        totals[0][...] = ffn.astype(totals[0].dtype)
        totals[1][...] = back.astype(totals[1].dtype)

    @pl.when(step < steps // 2)
    def _():
        work(normed, grad_out, before[:2], totals[:2], False)

    @pl.when(step >= steps // 2)
    def _():
        work(normed_twin, grad_out_twin, before[2:], totals[2:], last)

    @pl.when(step == steps - 1)
    def _():
        group = 256 // block
        for first_place in range(0, len(places), group):
            rows = slice(first_place * block, (first_place + group) * block)
            for k, (left, right) in enumerate(
                ((rows_n, grad_gate), (rows_n, grad_up), (rows_g, active))
            ):
                value = dot_tn(left[:, rows], right[...]).astype(BF)
                for i in range(group):
                    core, x, z = places[first_place + i]
                    part = value[i * block : (i + 1) * block]
                    low, zh = z < half, z % half
                    near, far = part[:, :tile], part[:, tile:]
                    if x == 0:
                        own[z, core, k] = near
                        if low:
                            rest_y[zh, core, k] = far
                        else:
                            send_y[1, zh, core, k] = far
                    else:
                        if low:
                            send_x[1, zh, core, k] = near
                            send_x[0, zh, core, k] = far
                        else:
                            rest_x[zh, core, k] = near
                            send_y[0, zh, core, k] = far


def ffn_piece(inputs, cells, before, last, ties):
    rows, width = inputs[0].shape
    zs, _, kinds, block, columns = cells[0].shape
    first = before is None
    height = min(ROW_TILE, rows)
    half = rows // height
    near = pl.BlockSpec((height, width), lambda i: (jnp.minimum(i, half - 1), 0))
    far = pl.BlockSpec((height, width), lambda i: (jnp.maximum(i - half, 0), 0))
    operands = [*inputs, *cells, *(() if first else before), *ties]
    part = (zs // 2, 2, kinds, block, columns)
    grads = [(2, *part), (2, *part), part, part, (zs, *part[1:])]
    mine = F32 if last else BF
    return pl.pallas_call(
        functools.partial(ffn_kernel, first, last, len(ties)),
        grid=(2 * half,),
        in_specs=[near, far, near, far]
        + [whole_spec(item.shape) for item in cells]
        + ([] if first else [near, near, far, far])
        + [ANYWHERE] * len(ties),
        out_specs=[whole_spec(shape) for shape in grads] + [near, near, far, far],
        out_shape=[jax.ShapeDtypeStruct(shape, BF) for shape in grads]
        + [jax.ShapeDtypeStruct((rows, width), dtype) for dtype in (mine, mine, BF, BF)],
        scratch_shapes=[pltpu.VMEM((kinds, width, 2 * columns), BF)]
        + [pltpu.VMEM((2 * rows, width), BF)] * 2
        + [pltpu.VMEM((2 * rows, 2 * columns), BF)] * 3,
        compiler_params=params(),
        cost_estimate=cost(
            72 * COST * rows * width * columns, 24 * width * columns + 40 * rows * width
        ),
    )(*operands)


def lay_out(near, twin, wide):
    _, zs, kinds, block, tile = near.shape
    for core, cells in enumerate((near, twin)):
        for x in range(2):
            for z in range(zs):
                at = ((core * 2 + x) * zs + z) * block
                for k in range(kinds):
                    for y in range(2):
                        wide[k, at : at + block, y * tile : (y + 1) * tile] = cells[
                            2 * x + y, z, k
                        ]


def cell_specs(cells, tile, skip=0):
    return [
        pl.BlockSpec((*item.shape[:-1], tile), lambda j: (0, 0, 0, 0, j + skip))
        for item in cells
    ]


def other_core_first(values):
    half = values.shape[1] // 2
    return jnp.concatenate([values[:, half:], values[:, :half]], axis=1)


def moved(values, shift, position):
    rows = values.shape[0]
    turned = pltpu.roll(values, shift % rows, 0)
    inside = position >= shift if shift > 0 else position < rows + shift
    return jnp.where(inside, turned, 0.0)


def mixed_of(gated, conv, position):
    total = conv[0:1] * gated
    for shift in range(1, conv.shape[0]):
        total = total + conv[shift : shift + 1] * moved(gated, shift, position)
    return total


def tile_conv(conv):
    return jnp.concatenate([conv[0], conv[1]], axis=1)


def mixer_kernel(first, last, ties, row_tile, *refs):
    feed = iter(refs)
    take = lambda n: [next(feed) for _ in range(n)]
    lengths, normed, tokens, conv, gain = take(5)
    cells = take(2)
    before = [] if first else take(1)
    take(ties)
    project, hidden = take(2)
    normed_two, for_twin = take(2) if last else (None, None)
    wide, branch = take(2)
    step = pl.program_id(0)
    rows = normed.shape[0]
    lay_out(*cells, wide)

    @pl.loop(0, rows // row_tile)
    def _(i):
        at = pl.ds(pl.multiple_of(i * row_tile, row_tile), row_tile)
        left = normed[at, :]
        for k in range(3):
            project[k, at, :] = dot_nn(left, wide[k])

    taps = tile_conv(conv[...])
    for sequence in range(rows // SLOTS):
        at = slice(sequence * SLOTS, (sequence + 1) * SLOTS)
        position = lax.broadcasted_iota(jnp.int32, (SLOTS, wide.shape[2]), 0)
        gated = project[0, at] * project[2, at]
        gated = jnp.where(position < lengths[sequence], gated, 0.0)
        branch[at, :] = (project[1, at] * mixed_of(gated, taps, position)).astype(BF)

    @pl.when(step == 0)
    def _():
        if first:
            hidden[...] = tokens[...].astype(F32)
        else:
            hidden[...] = before[0][...]

    ending = step == pl.num_programs(0) - 1

    @pl.loop(0, rows // row_tile)
    def _(i):
        at = pl.ds(pl.multiple_of(i * row_tile, row_tile), row_tile)
        value = hidden[at, :] + dot_nt(branch[at, :], wide[3])
        hidden[at, :] = value
        if last:

            @pl.when(ending)
            def _():
                unit = norm_stats(value)[1]
                value_two = (unit * gain[...]).astype(BF)
                normed_two[at, :] = value_two
                for_twin[at, :] = other_core_first(value_two)


def mixer_part(lengths, normed, tokens, conv, gain, cells, before, last, ties, tile):
    rows, width = normed.shape
    _, zs, kinds, block, columns = cells[0].shape
    first = before is None
    whole = whole_spec((rows, width))
    inputs = [lengths, normed, tokens, conv, gain, *cells]
    inputs += ([] if first else [before]) + list(ties)
    outs = [jax.ShapeDtypeStruct((3, rows, 2 * columns), F32), jax.ShapeDtypeStruct((rows, width), F32)]
    out_specs = [pl.BlockSpec((3, rows, 2 * tile), lambda j: (0, 0, j)), whole]
    if last:
        outs += [jax.ShapeDtypeStruct((rows, width), BF)] * 2
        out_specs += [whole] * 2
    return pl.pallas_call(
        functools.partial(mixer_kernel, first, last, len(ties), min(rows, 256)),
        grid=(columns // tile,),
        in_specs=[pl.BlockSpec(memory_space=pltpu.SMEM), whole, whole]
        + [pl.BlockSpec((2, conv.shape[1], tile), lambda j: (0, 0, j)), whole_spec((1, width))]
        + cell_specs(cells, tile)
        + [whole] * (0 if first else 1)
        + [ANYWHERE] * len(ties),
        out_specs=out_specs,
        out_shape=outs,
        scratch_shapes=[
            pltpu.VMEM((kinds, width, 2 * tile), BF),
            pltpu.VMEM((rows, 2 * tile), BF),
        ],
        input_output_aliases={} if first else {7: 1},
        compiler_params=params(),
        cost_estimate=pl.CostEstimate(
            flops=16 * COST * rows * width * columns,
            bytes_accessed=24 * rows * columns + 16 * width * columns + 8 * rows * width,
            transcendentals=0,
        ),
    )(*inputs)


def mixer_back_kernel(first, ties, row_tile, *refs):
    feed = iter(refs)
    take = lambda n: [next(feed) for _ in range(n)]
    lengths, normed, grad_mix, project, conv = take(5)
    cells = take(2)
    before = [] if first else take(1)
    take(ties)
    keep, send, tap_grads, grad_normed = take(4)
    wide, branch, grads, grad_branch = take(4)
    step = pl.program_id(0)
    rows = normed.shape[0]
    _, zs, _, block, tile = cells[0].shape
    lay_out(*cells, wide)

    @pl.when(step == 0)
    def _():
        grad_normed[...] = jnp.zeros_like(grad_normed) if first else before[0][...]

    @pl.loop(0, rows // row_tile)
    def _(i):
        at = pl.ds(pl.multiple_of(i * row_tile, row_tile), row_tile)
        grad_branch[at, :] = dot_nn(grad_mix[at, :], wide[3])

    taps = tile_conv(conv[...])
    count = taps.shape[0]
    sums = [jnp.zeros((1, 2 * tile), F32)] * count
    for sequence in range(rows // SLOTS):
        at = slice(sequence * SLOTS, (sequence + 1) * SLOTS)
        position = lax.broadcasted_iota(jnp.int32, (SLOTS, 2 * tile), 0)
        living = position < lengths[sequence]
        gated = jnp.where(living, project[0, at] * project[2, at], 0.0)
        mixed = taps[0:1] * gated
        g_mixed = grad_branch[at, :] * project[1, at]
        sums[0] = sums[0] + jnp.sum(g_mixed * gated, axis=0, keepdims=True)
        g_gated = taps[0:1] * g_mixed
        for shift in range(1, count):
            lower = moved(gated, shift, position)
            mixed = mixed + taps[shift : shift + 1] * lower
            sums[shift] = sums[shift] + jnp.sum(g_mixed * lower, axis=0, keepdims=True)
            g_gated = g_gated + taps[shift : shift + 1] * moved(g_mixed, -shift, position)
        g_gated = jnp.where(living, g_gated, 0.0)
        branch[at, :] = (project[1, at] * mixed).astype(BF)
        grads[0, at, :] = (g_gated * project[2, at]).astype(BF)
        grads[1, at, :] = (grad_branch[at, :] * mixed).astype(BF)
        grads[2, at, :] = (g_gated * project[0, at]).astype(BF)
    tap_grads[...] = jnp.concatenate(
        sums + [jnp.zeros((8 - count, 2 * tile), F32)], axis=0
    )

    @pl.loop(0, rows // row_tile)
    def _(i):
        at = pl.ds(pl.multiple_of(i * row_tile, row_tile), row_tile)
        value = dot_nt(grads[0, at, :], wide[0]) + dot_nt(grads[1, at, :], wide[1])
        grad_normed[at, :] += value + dot_nt(grads[2, at, :], wide[2])

    depth = zs * block
    for place in range(4):
        at = slice(place * depth, (place + 1) * depth)
        core, x = divmod(place, 2)
        out = send if core else keep
        for k in range(4):
            if k < 3:
                value = dot_tn(normed[:, at], grads[k])
            else:
                value = dot_tn(grad_mix[:, at], branch[...])
            value = value.astype(BF)
            for z in range(zs):
                part = value[z * block : (z + 1) * block]
                out[2 * x, z, k] = part[:, :tile]
                out[2 * x + 1, z, k] = part[:, tile:]


def mixer_back(lengths, normed, grad_mix, project, conv, cells, before, ties, tile, part, parts):
    rows, width = normed.shape
    _, zs, kinds, block, columns = cells[0].shape
    columns = columns // parts
    skip = part * (columns // tile)
    first = before is None
    whole = whole_spec((rows, width))
    inputs = [lengths, normed, grad_mix, project, conv, *cells]
    inputs += ([] if first else [before]) + list(ties)
    grads = pl.BlockSpec((4, zs, kinds, block, tile), lambda j: (0, 0, 0, 0, j))
    grad_shape = jax.ShapeDtypeStruct((4, zs, kinds, block, columns), BF)
    return pl.pallas_call(
        functools.partial(mixer_back_kernel, first, len(ties), min(rows, 256)),
        grid=(columns // tile,),
        in_specs=[pl.BlockSpec(memory_space=pltpu.SMEM), whole, whole]
        + [pl.BlockSpec((3, rows, 2 * tile), lambda j: (0, 0, j + skip))]
        + [pl.BlockSpec((2, conv.shape[1], tile), lambda j: (0, 0, j + skip))]
        + cell_specs(cells, tile, skip)
        + [whole] * (0 if first else 1)
        + [ANYWHERE] * len(ties),
        out_specs=[grads, grads, pl.BlockSpec((8, 2 * tile), lambda j: (0, j)), whole],
        out_shape=[
            grad_shape,
            grad_shape,
            jax.ShapeDtypeStruct((8, 2 * columns), F32),
            jax.ShapeDtypeStruct((rows, width), F32),
        ],
        scratch_shapes=[
            pltpu.VMEM((kinds, width, 2 * tile), BF),
            pltpu.VMEM((rows, 2 * tile), BF),
            pltpu.VMEM((3, rows, 2 * tile), BF),
            pltpu.VMEM((rows, 2 * tile), F32),
        ],
        input_output_aliases={} if first else {7: 3},
        compiler_params=params(),
        cost_estimate=pl.CostEstimate(
            flops=32 * COST * rows * width * columns,
            bytes_accessed=24 * rows * columns + 32 * width * columns + 8 * rows * width,
            transcendentals=0,
        ),
    )(*inputs)


def reorder(source, target, flip, inward):
    width = source.shape[1]
    for case in range(4):

        @pl.when(flip == case)
        def _():
            count = SHARDS[0]
            block, zs = width // count, count // 4
            for place in range(count):
                core, x, z = place // (2 * zs), place // zs % 2, place % zs
                absolute = z * 4 + (case ^ (x * 2 + core))
                here = slice(place * block, (place + 1) * block)
                there = slice(absolute * block, (absolute + 1) * block)
                if inward:
                    target[:, here] = source[:, there]
                else:
                    target[:, there] = source[:, here]


def row_call(kernel, flip, inputs, outs, sums=0, ties=()):
    rows, width = next(item.shape for item in inputs if item.shape[0] > 1)
    height = min(ROW_TILE, rows)
    tiled = pl.BlockSpec((height, width), lambda i: (i, 0))
    scalar = pl.BlockSpec(memory_space=pltpu.SMEM)
    specs = [
        scalar if item.ndim == 1 else tiled if item.shape[0] > 1 else whole_spec((1, width))
        for item in inputs
    ]
    count = len(inputs) + 1

    def body(*refs):
        kernel(*refs[:count], *refs[count + len(ties) :])

    return pl.pallas_call(
        body,
        grid=(rows // height,),
        in_specs=[scalar] + specs + [ANYWHERE] * len(ties),
        out_specs=[tiled] * len(outs) + [whole_spec((8, width))] * sums,
        out_shape=[jax.ShapeDtypeStruct((rows, width), dtype) for dtype in outs]
        + [jax.ShapeDtypeStruct((8, width), F32)] * sums,
        scratch_shapes=[pltpu.VMEM((height, width), F32)] * 2,
        compiler_params=params(),
        cost_estimate=cost(20 * rows * width, 12 * rows * width),
    )(flip, *inputs, *ties)


def enter_kernel(flip, lengths, tokens, cotangent, gain, low, normed, grad, for_twin, one, two):
    one[...] = tokens[...].astype(F32)
    reorder(one, two, flip[0], True)
    value = two[...]
    low[...] = value.astype(BF)
    normed[...] = (norm_stats(value)[1] * gain[...]).astype(BF)
    one[...] = cotangent[...].astype(F32)
    reorder(one, two, flip[0], True)
    height = value.shape[0]
    first = pl.program_id(0) * height
    position = first % SLOTS + lax.broadcasted_iota(jnp.int32, value.shape, 0)
    value = jnp.where(position < lengths[first // SLOTS], two[...], 0.0).astype(BF)
    grad[...] = value
    for_twin[...] = other_core_first(value)


def add_up(total, values):
    part = jnp.sum(values.reshape(-1, 8, values.shape[1]), axis=0)

    @pl.when(pl.program_id(0) == 0)
    def _():
        total[...] = part

    @pl.when(pl.program_id(0) > 0)
    def _():
        total[...] += part


def between_kernel(flip, mine, twin, hidden, grad_out, gain, mix, total, one, two):
    grad = mine[...] + twin[...].astype(F32)
    inverse, unit = norm_stats(hidden[...])
    value = grad_out[...].astype(F32) + norm_back(grad, gain[...], inverse, unit)
    mix[...] = value.astype(BF)
    add_up(total, grad * unit)


def leave_kernel(flip, grad, tokens, grad_hidden, gain, out, total, one, two):
    inverse, unit = norm_stats(tokens[...].astype(F32))
    value = grad[...]
    one[...] = grad_hidden[...].astype(F32) + norm_back(value, gain[...], inverse, unit)
    reorder(one, out, flip[0], False)
    add_up(total, value * unit)


def result_kernel(flip, hidden, mine, twin, out, one, two):
    one[...] = hidden[...] + mine[...] + twin[...].astype(F32)
    reorder(one, two, flip[0], False)
    out[...] = two[...].astype(BF)


SHARDS = [16]


def ffn_sizes(columns, rows):
    if rows <= 1024 and columns == sum(SIZES):
        return SIZES
    return (128,) * (columns // 128)


def norm_stats(values):
    inverse = lax.rsqrt(jnp.mean(values * values, axis=-1, keepdims=True) + EPS)
    return (inverse, values * inverse)


def norm_back(grad_normed, gain, inverse, unit):
    scaled = grad_normed * gain
    return inverse * (scaled - unit * jnp.mean(scaled * unit, axis=-1, keepdims=True))


def body(
    tokens,
    lengths,
    in_proj,
    conv_weight,
    out_proj,
    norm_gain,
    ffn_gain,
    w_gate,
    w_up,
    w_down,
    cotangent,
):
    rows, width = tokens.shape
    links = Links(lax.axis_size("dp"), lax.axis_size("tensor"))
    rank = lax.axis_index("tensor")
    kernel = conv_weight.shape[0]
    half = in_proj.shape[2]
    hidden_half = w_gate.shape[1]
    block = width // links.dp

    core = lax.axis_index("dp") % 2
    mixer_own = jnp.concatenate([in_proj.astype(BF), out_proj.T.astype(BF)[None]], axis=0)
    ffn_own = jnp.stack([w_gate.astype(BF), w_up.astype(BF), w_down.T.astype(BF)])
    tile = 256 if half % 512 == 0 and rows <= 1024 else 128
    shared = hidden_half // 2
    mine_of = lax.dynamic_slice_in_dim(ffn_own, core * shared, shared, 2)
    twin_of = lax.dynamic_slice_in_dim(ffn_own, (1 - core) * shared, shared, 2)
    ffn_both = jnp.stack([mine_of, links.swap(twin_of, c=1)])
    sizes = ffn_sizes(shared, rows)
    starts = [sum(sizes[:p]) for p in range(len(sizes))]
    own = [mixer_own] + [ffn_both[..., at : at + size] for at, size in zip(starts, sizes)]
    own = [links.spread(item) for item in own]
    pieces = len(own)
    last = pieces - 1
    mine, sides, corner = {}, {}, {}

    def cells(p):
        from_x, from_y = sides[p]
        return [mine[p], from_y, from_x, *corner[p]]

    sums = {}

    def start(stage, p):
        if stage == "z":
            mine[p] = links.turn_z(own[p])
            return mine, p
        if stage == "sides":
            sides[p] = links.gather_sides(mine[p])
            return sides, p
        if stage == "corner":
            corner[p] = links.gather_corner(*sides[p])
            return corner, p
        item = sums[p]
        if stage == "sum core":
            item["got"] = links.swap(item["send"], c=1)
            return item, "got"
        if stage == "sum corner":
            if "keep" in item:
                item["parts"] = both_cores(item["keep"], item["got"])
            send_x, send_y = item["parts"][:2]
            item["corner"] = links.swap(send_x, x=1), links.swap(send_y, y=1)
            return item, "corner"
        rest_x, rest_y, here = item["parts"][2:]
        if stage == "sum sides":
            next_x, next_y = add_sides(rest_x, rest_y, *item["corner"])
            item["sides"] = links.swap(next_x, x=1), links.swap(next_y, y=1)
            return item, "sides"
        item["z"] = links.turn_z(add_own(here, *item["corner"], *item["sides"]))
        return item, "z"

    def close(kept, places):
        kept, tree = jax.tree.flatten([kept, [store[key] for store, key in places]])
        kept, arrived = jax.tree.unflatten(tree, gate(kept))
        for (store, key), value in zip(places, arrived):
            store[key] = value
        return kept

    blocks = links.absolute(jnp.arange(links.dp))
    gain_one = jnp.take(norm_gain.reshape(links.dp, block), blocks, axis=0).reshape(1, width)
    gain_two = jnp.take(ffn_gain.reshape(links.dp, block), blocks, axis=0).reshape(1, width)
    conv = jnp.where(rank == 0, conv_weight, jnp.roll(conv_weight, half, axis=1))
    conv = conv.reshape(kernel, 2, half).transpose(1, 0, 2)
    count = rows // SLOTS
    own_lengths = lax.dynamic_slice_in_dim(lengths, rank * count, count)
    flip = (lax.axis_index("dp") % 4)[None]
    SHARDS[0] = links.dp
    tokens_low, normed, grad_ffn, for_twin_grad = row_call(
        enter_kernel, flip, [own_lengths, tokens, cotangent, gain_one], [BF] * 4, ties=own[1:]
    )

    places = [start("z", 0)]
    normed, for_twin_grad, own = close([normed, for_twin_grad, own], places)
    grad_ffn_twin = links.swap(for_twin_grad, c=1)
    places = [start("sides", 0), start("z", 1)]
    own[2:3], mine[0] = close([own[2:3], mine[0]], places)
    places = [start("corner", 0), start("z", 2)]
    own[3:4], mine[1] = close([own[3:4], mine[1]], places)
    joined = join(*cells(0))
    mixer_cells = [joined, links.swap(joined, c=1)]

    places = [start("sides", 1), start("sides", 2), start("z", 3)]
    project, hidden, normed_two, for_twin = mixer_part(
        own_lengths, normed, tokens_low, conv, gain_two, mixer_cells, None, True, [], tile
    )
    normed_two, for_twin, own[4:5] = close([normed_two, for_twin, own[4:5]], places)
    start("corner", 1)
    inputs = [normed_two, links.swap(for_twin, c=1), grad_ffn, grad_ffn_twin]

    totals = None
    for p in range(1, pieces):
        places = []
        for stage, q in (("corner", p + 1), ("sides", p + 2), ("z", p + 3)):
            if q < pieces:
                places.append(start(stage, q))
        for stage, q in (("sum z", p - 4), ("sum sides", p - 3), ("sum corner", p - 2)):
            if q > 0:
                places.append(start(stage, q))
        *parts, t0, t1, t2, t3 = ffn_piece(inputs, cells(p), totals, p == last, [])
        held = sums[p - 1]["parts"][:2] if p > 1 else []
        parts, totals, held = close([parts, [t0, t1, t2, t3], held], places)
        if p > 1:
            sums[p - 1]["parts"][:2] = held
        sums[p] = dict(parts=list(parts))
    grad_mix, gain_two_part = row_call(
        between_kernel,
        flip,
        [totals[1], links.swap(totals[3], c=1), hidden, grad_ffn, gain_two],
        [BF],
        1,
    )
    places = [
        start("sum z", last - 3),
        start("sum sides", last - 2),
        start("sum corner", last - 1),
    ]
    parts = 2 if half % 256 == 0 else 1
    names = [f"mixer {p}" for p in range(parts)]
    grad_normed, taps = None, []
    for p, name in enumerate(names):
        if p:
            places = [start("sum core", names[0])]
        if p == parts - 1:
            later = [start("sum z", last - 2), start("sum sides", last - 1)]
            later.append(start("sum corner", last))
            places += later
        keep, send, tap_grads, grad_normed = mixer_back(
            own_lengths, normed, grad_mix, project, conv, mixer_cells, grad_normed, [],
            tile, p, parts,
        )
        held = sums[last]["parts"][:2] if p < parts - 1 else []
        keep, send, tap_grads, grad_normed, totals[0], totals[2], held = close(
            [keep, send, tap_grads, grad_normed, totals[0], totals[2], held], places
        )
        if p < parts - 1:
            sums[last]["parts"][:2] = held
        taps.append(tap_grads)
        sums[name] = dict(keep=keep, send=send)
    places = [start("sum core", names[-1]), start("sum z", last - 1), start("sum sides", last)]
    if parts > 1:
        places.append(start("sum corner", names[0]))
    grad_tokens, gain_one_part = row_call(
        leave_kernel, flip, [grad_normed, tokens_low, grad_mix, gain_one], [F32], 1
    )
    item = sums[names[-1]]
    grad_tokens, gain_one_part, item["keep"] = close(
        [grad_tokens, gain_one_part, item["keep"]], places
    )

    place = links.place(jnp.arange(links.dp))
    taps = jnp.concatenate(taps, axis=1)[:kernel].reshape(kernel, -1, 2, tile)
    taps = taps.transpose(0, 2, 1, 3).reshape(kernel, width)
    taps = jnp.where(rank == 0, taps, jnp.roll(taps, half, axis=1))
    gains = jnp.stack([gain_one_part.sum(0), gain_two_part.sum(0)])
    gains = jnp.take(gains.reshape(2, links.dp, block), place, axis=1).reshape(2, width)
    small = links.sum_chip(jnp.concatenate([gains, taps], axis=0))

    places = [start("sum corner", names[-1]), start("sum z", last)]
    if parts > 1:
        places.append(start("sum sides", names[0]))
    result = row_call(
        result_kernel, flip, [hidden, totals[0], links.swap(totals[2], c=1)], [BF]
    )[0]
    result, small = close([result, small], places)
    places = [start("sum sides", names[-1])]
    if parts > 1:
        places.append(start("sum z", names[0]))
    (small,) = close([links.sum_rest(small)], places)
    start("sum z", names[-1])
    shard = lambda p: jnp.sum(sums[p]["z"].astype(F32), axis=0)
    mixer_shard = jnp.concatenate([shard(name) for name in names], axis=2)
    ffn_shard = jnp.concatenate([shard(p) for p in range(1, pieces)], axis=3)
    here, there = ffn_shard[0], links.swap(ffn_shard[1], c=1)
    ffn_shard = jnp.concatenate(
        [jnp.where(core == 0, here, there), jnp.where(core == 0, there, here)], axis=2
    )
    return (
        result,
        grad_tokens,
        mixer_shard[:3],
        small[2:],
        mixer_shard[3].T,
        small[0],
        small[1],
        ffn_shard[0],
        ffn_shard[1],
        ffn_shard[2].T,
    )


def solution(mesh):
    rows = P(("dp", "tensor"), None)
    in_specs = (
        rows,
        P("dp"),
        P(None, "dp", "tensor"),
        P(),
        P("tensor", "dp"),
        P(),
        P(),
        P("dp", "tensor"),
        P("dp", "tensor"),
        P("tensor", "dp"),
        rows,
    )
    out_specs = (
        rows,
        rows,
        P(None, "dp", "tensor"),
        P(),
        P("tensor", "dp"),
        P(),
        P(),
        P("dp", "tensor"),
        P("dp", "tensor"),
        P("tensor", "dp"),
    )
    return jax.shard_map(body, mesh=mesh, in_specs=in_specs, out_specs=out_specs, check_vma=False)
```

```python
import functools

import jax
import jax.numpy as jnp
from jax import lax
from jax.experimental import pallas as pl
from jax.experimental.pallas import tpu as pltpu
from jax.sharding import PartitionSpec as P

SLOTS = 1024
EPS = 1e-05
AXES = ("dp", "tensor")
ROW_TILE = 256
SIZES = (256, 256, 384, 256)
COST = 4
VMEM = 60 * 2**20
BF = jnp.bfloat16
F32 = jnp.float32
ANYWHERE = pl.BlockSpec(memory_space=pl.ANY)


def dot_nn(left, right):
    return jnp.dot(left, right, preferred_element_type=F32)


def dot_tn(left, right):
    return lax.dot_general(left, right, (((0,), (0,)), ((), ())), preferred_element_type=F32)


def dot_nt(left, right):
    return lax.dot_general(left, right, (((1,), (1,)), ((), ())), preferred_element_type=F32)


class Links:
    def __init__(self, dp, tp):
        self.dp, self.tp, self.zs = dp, tp, dp // 4

    def swap(self, value, x=0, c=0, y=0, z=0):
        flip = (z * 2 + x) * 2 + c
        pairs = [
            (q * self.tp + t, (q ^ flip) * self.tp + (t ^ y))
            for q in range(self.dp)
            for t in range(self.tp)
        ]
        return lax.ppermute(value, AXES, pairs)

    def turn_z(self, value):
        groups = [[z * 4 + rest for z in range(self.zs)] for rest in range(4)]
        return lax.all_to_all(value, "dp", 0, 0, axis_index_groups=groups, tiled=True)

    def spread(self, own):
        return jnp.broadcast_to(own[None], (self.zs, *own.shape))

    def gather_sides(self, mine):
        return self.swap(mine, x=1), self.swap(mine, y=1)

    def gather_corner(self, from_x, from_y):
        low, high = cut(from_x, from_y)
        return self.swap(low, y=1), self.swap(high, x=1)

    def sum_chip(self, value):
        value = value + self.swap(value, c=1)
        return value + self.swap(value, y=1)

    def sum_rest(self, value):
        value = value + self.swap(value, x=1)
        others = [self.swap(value, z=z) for z in range(1, self.zs)]
        return functools.reduce(jnp.add, others, value)

    def absolute(self, place):
        q = lax.axis_index("dp")
        core, x, z = place // (2 * self.zs), place // self.zs % 2, place % self.zs
        return z * 4 + ((q % 4) ^ (x * 2 + core))

    def place(self, absolute):
        q = lax.axis_index("dp")
        apart = (absolute % 4) ^ (q % 4)
        return ((apart % 2) * 2 + apart // 2) * self.zs + absolute // 4


def whole_spec(shape, buffers=1):
    return pl.BlockSpec(
        shape, lambda *_: (0,) * len(shape), pipeline_mode=pl.Buffered(buffers)
    )


def params():
    return pltpu.CompilerParams(vmem_limit_bytes=VMEM)


def cost(flops, moved_bytes):
    return pl.CostEstimate(flops=flops, bytes_accessed=moved_bytes, transcendentals=0)


def small_calls(jobs):
    tiles = [inputs[0].shape[-1] // 128 for _, inputs, _ in jobs]

    def spec(shape, count):
        zeros = (0,) * (len(shape) - 1)
        return pl.BlockSpec(
            (*shape[:-1], 128), lambda j: (*zeros, jnp.minimum(j, count - 1))
        )

    n_in = [len(inputs) for _, inputs, _ in jobs]
    n_out = [len(shapes) for _, _, shapes in jobs]

    def body(*refs):
        ins, outs = list(refs[: sum(n_in)]), list(refs[sum(n_in) :])
        for (kernel, _, _), count, i, o in zip(jobs, tiles, n_in, n_out):
            here, ins = ins[:i], ins[i:]
            there, outs = outs[:o], outs[o:]

            @pl.when(pl.program_id(0) < count)
            def _():
                kernel(*here, *there)

    arrays = [item for _, inputs, _ in jobs for item in inputs]
    out = pl.pallas_call(
        body,
        grid=(max(tiles),),
        in_specs=[
            spec(item.shape, count) for (_, inputs, _), count in zip(jobs, tiles) for item in inputs
        ],
        out_specs=[
            spec(shape, count) for (_, _, shapes), count in zip(jobs, tiles) for shape in shapes
        ],
        out_shape=[jax.ShapeDtypeStruct(shape, BF) for _, _, shapes in jobs for shape in shapes],
        compiler_params=params(),
        cost_estimate=cost(0, 4 * sum(item.size for item in arrays)),
    )(*arrays)
    result = []
    for o in n_out:
        result.append(out[:o])
        out = out[o:]
    return result


def gate(values):
    def nothing(*refs):
        del refs

    count = len(values)
    return pl.pallas_call(
        nothing,
        in_specs=[ANYWHERE] * count,
        out_specs=[ANYWHERE] * count,
        out_shape=[jax.ShapeDtypeStruct(item.shape, item.dtype) for item in values],
        input_output_aliases={i: i for i in range(count)},
        compiler_params=params(),
        cost_estimate=cost(0, 1024),
    )(*values)


def cut_kernel(from_x, from_y, low, high):
    low[...] = from_x[...]
    high[...] = from_y[...]


def cut(from_x, from_y):
    half, *rest, columns = from_x.shape
    half //= 2
    lead = (0,) * len(rest)
    block = (half, *rest, 128)
    low = pl.BlockSpec(block, lambda j: (0, *lead, j))
    high = pl.BlockSpec(block, lambda j: (1, *lead, j))
    return pl.pallas_call(
        cut_kernel,
        grid=(columns // 128,),
        in_specs=[low, high],
        out_specs=[low] * 2,
        out_shape=[jax.ShapeDtypeStruct((half, *rest, columns), BF)] * 2,
        compiler_params=params(),
        cost_estimate=cost(0, 4 * from_x.size),
    )(from_x, from_y)


def join_kernel(mine, from_y, from_x, one, two, out):
    half = one.shape[0]
    out[0] = mine[...]
    out[1] = from_y[...]
    out[2] = from_x[...]
    out[3, :half] = one[...]
    out[3, half:] = two[...]


def join(mine, from_y, from_x, one, two):
    job = (join_kernel, [mine, from_y, from_x, one, two], [(4, *mine.shape)])
    return small_calls([job])[0][0]


def both_kernel(keep, got, send_x, send_y, rest_x, rest_y, own):
    half = keep.shape[1] // 2

    def total(cell, part):
        return (keep[cell, part].astype(F32) + got[cell, part].astype(F32)).astype(BF)

    low, high = slice(0, half), slice(half, 2 * half)
    send_x[0], send_x[1] = total(3, low), total(2, low)
    send_y[0], send_y[1] = total(3, high), total(1, high)
    rest_x[...], rest_y[...] = total(2, high), total(1, low)
    own[:half], own[half:] = total(0, low), total(0, high)


def both_cores(keep, got):
    _, zs, *rest = keep.shape
    part = (zs // 2, *rest)
    shapes = [(2, *part), (2, *part), part, part, (zs, *rest)]
    return both_kernel, [keep, got], shapes


def sides_kernel(rest_x, rest_y, got_x, got_y, send_x, send_y):
    send_x[...] = (rest_x[...].astype(F32) + got_y[0].astype(F32)).astype(BF)
    send_y[...] = (rest_y[...].astype(F32) + got_x[0].astype(F32)).astype(BF)


def add_sides(rest_x, rest_y, got_x, got_y):
    return sides_kernel, [rest_x, rest_y, got_x, got_y], [rest_x.shape] * 2


def own_kernel(own, got_x, got_y, side_x, side_y, out):
    half = side_x.shape[0]
    low = own[:half].astype(F32) + got_x[1].astype(F32) + side_y[...].astype(F32)
    high = own[half:].astype(F32) + got_y[1].astype(F32) + side_x[...].astype(F32)
    out[:half] = low.astype(BF)
    out[half:] = high.astype(BF)


def add_own(own, got_x, got_y, side_x, side_y):
    return own_kernel, [own, got_x, got_y, side_x, side_y], [own.shape]


def ffn_kernel(first, last, ties, *refs):
    feed = iter(refs)
    take = lambda n: [next(feed) for _ in range(n)]
    normed, normed_twin, grad_out, grad_out_twin = take(4)
    mine, from_y, from_x, one, two = take(5)
    before = [] if first else take(4)
    take(ties)
    send_x, send_y, rest_x, rest_y, own = take(5)
    totals = take(4)
    wide, rows_n, rows_g, active, grad_gate, grad_up = take(6)
    step = pl.program_id(0)
    steps = pl.num_programs(0)
    zs, _, kinds, block, tile = mine.shape
    half = zs // 2
    height = normed.shape[0]
    places = [(core, x, z) for core in range(2) for x in range(2) for z in range(zs)]

    @pl.when(step == 0)
    def _():
        for at, (core, x, z) in enumerate(places):
            rows = slice(at * block, (at + 1) * block)
            for k in range(kinds):
                if x == 0:
                    wide[k, rows, :tile] = mine[z, core, k]
                    wide[k, rows, tile:] = from_y[z, core, k]
                else:
                    wide[k, rows, :tile] = from_x[z, core, k]
                    corner = one[z, core, k] if z < half else two[z - half, core, k]
                    wide[k, rows, tile:] = corner

    at = pl.ds(pl.multiple_of(step * height, height), height)

    def work(normed, grad_out, before, totals, turn):
        left = normed[...]
        right = grad_out[...]
        rows_n[at, :] = left
        rows_g[at, :] = right
        gate, upward = dot_nn(left, wide[0]), dot_nn(left, wide[1])
        grad_active = dot_nn(right, wide[2])
        sigma = 1.0 / (1.0 + jnp.exp(-gate))
        silu = gate * sigma
        act = (silu * upward).astype(BF)
        g_up = (grad_active * silu).astype(BF)
        g_gate = (grad_active * upward * (sigma + silu * (1.0 - sigma))).astype(BF)
        active[at, :] = act
        grad_up[at, :] = g_up
        grad_gate[at, :] = g_gate
        ffn = dot_nt(act, wide[2])
        back = dot_nt(g_gate, wide[0]) + dot_nt(g_up, wide[1])
        if not first:
            ffn = ffn + before[0][...].astype(F32)
            back = back + before[1][...].astype(F32)
        if turn:
            ffn, back = other_core_first(ffn), other_core_first(back)
        totals[0][...] = ffn.astype(totals[0].dtype)
        totals[1][...] = back.astype(totals[1].dtype)

    @pl.when(step < steps // 2)
    def _():
        work(normed, grad_out, before[:2], totals[:2], False)

    @pl.when(step >= steps // 2)
    def _():
        work(normed_twin, grad_out_twin, before[2:], totals[2:], last)

    @pl.when(step == steps - 1)
    def _():
        group = 256 // block
        for first_place in range(0, len(places), group):
            rows = slice(first_place * block, (first_place + group) * block)
            for k, (left, right) in enumerate(
                ((rows_n, grad_gate), (rows_n, grad_up), (rows_g, active))
            ):
                value = dot_tn(left[:, rows], right[...]).astype(BF)
                for i in range(group):
                    core, x, z = places[first_place + i]
                    part = value[i * block : (i + 1) * block]
                    low, zh = z < half, z % half
                    near, far = part[:, :tile], part[:, tile:]
                    if x == 0:
                        own[z, core, k] = near
                        if low:
                            rest_y[zh, core, k] = far
                        else:
                            send_y[1, zh, core, k] = far
                    else:
                        if low:
                            send_x[1, zh, core, k] = near
                            send_x[0, zh, core, k] = far
                        else:
                            rest_x[zh, core, k] = near
                            send_y[0, zh, core, k] = far


def ffn_piece(inputs, cells, before, last, ties):
    rows, width = inputs[0].shape
    zs, _, kinds, block, columns = cells[0].shape
    first = before is None
    height = min(ROW_TILE, rows)
    half = rows // height
    near = pl.BlockSpec((height, width), lambda i: (jnp.minimum(i, half - 1), 0))
    far = pl.BlockSpec((height, width), lambda i: (jnp.maximum(i - half, 0), 0))
    operands = [*inputs, *cells, *(() if first else before), *ties]
    part = (zs // 2, 2, kinds, block, columns)
    grads = [(2, *part), (2, *part), part, part, (zs, *part[1:])]
    mine = F32 if last else BF
    return pl.pallas_call(
        functools.partial(ffn_kernel, first, last, len(ties)),
        grid=(2 * half,),
        in_specs=[near, far, near, far]
        + [whole_spec(item.shape) for item in cells]
        + ([] if first else [near, near, far, far])
        + [ANYWHERE] * len(ties),
        out_specs=[whole_spec(shape) for shape in grads] + [near, near, far, far],
        out_shape=[jax.ShapeDtypeStruct(shape, BF) for shape in grads]
        + [jax.ShapeDtypeStruct((rows, width), dtype) for dtype in (mine, mine, BF, BF)],
        scratch_shapes=[pltpu.VMEM((kinds, width, 2 * columns), BF)]
        + [pltpu.VMEM((2 * rows, width), BF)] * 2
        + [pltpu.VMEM((2 * rows, 2 * columns), BF)] * 3,
        compiler_params=params(),
        cost_estimate=cost(
            72 * COST * rows * width * columns, 24 * width * columns + 40 * rows * width
        ),
    )(*operands)


def lay_out(near, twin, wide):
    _, zs, kinds, block, tile = near.shape
    for core, cells in enumerate((near, twin)):
        for x in range(2):
            for z in range(zs):
                at = ((core * 2 + x) * zs + z) * block
                for k in range(kinds):
                    for y in range(2):
                        wide[k, at : at + block, y * tile : (y + 1) * tile] = cells[
                            2 * x + y, z, k
                        ]


def cell_specs(cells, tile, skip=0):
    return [
        pl.BlockSpec((*item.shape[:-1], tile), lambda j: (0, 0, 0, 0, j + skip))
        for item in cells
    ]


def other_core_first(values):
    half = values.shape[1] // 2
    return jnp.concatenate([values[:, half:], values[:, :half]], axis=1)


def moved(values, shift, position):
    rows = values.shape[0]
    turned = pltpu.roll(values, shift % rows, 0)
    inside = position >= shift if shift > 0 else position < rows + shift
    return jnp.where(inside, turned, 0.0)


def mixed_of(gated, conv, position):
    total = conv[0:1] * gated
    for shift in range(1, conv.shape[0]):
        total = total + conv[shift : shift + 1] * moved(gated, shift, position)
    return total


def tile_conv(conv):
    return jnp.concatenate([conv[0], conv[1]], axis=1)


def mixer_kernel(first, last, ties, row_tile, *refs):
    feed = iter(refs)
    take = lambda n: [next(feed) for _ in range(n)]
    lengths, normed, tokens, conv, gain = take(5)
    cells = take(2)
    before = [] if first else take(1)
    take(ties)
    project, hidden = take(2)
    normed_two, for_twin = take(2) if last else (None, None)
    wide, branch = take(2)
    step = pl.program_id(0)
    rows = normed.shape[0]
    lay_out(*cells, wide)

    @pl.loop(0, rows // row_tile)
    def _(i):
        at = pl.ds(pl.multiple_of(i * row_tile, row_tile), row_tile)
        left = normed[at, :]
        for k in range(3):
            project[k, at, :] = dot_nn(left, wide[k])

    taps = tile_conv(conv[...])
    for sequence in range(rows // SLOTS):
        at = slice(sequence * SLOTS, (sequence + 1) * SLOTS)
        position = lax.broadcasted_iota(jnp.int32, (SLOTS, wide.shape[2]), 0)
        gated = project[0, at] * project[2, at]
        gated = jnp.where(position < lengths[sequence], gated, 0.0)
        branch[at, :] = (project[1, at] * mixed_of(gated, taps, position)).astype(BF)

    @pl.when(step == 0)
    def _():
        if first:
            hidden[...] = tokens[...].astype(F32)
        else:
            hidden[...] = before[0][...]

    ending = step == pl.num_programs(0) - 1

    @pl.loop(0, rows // row_tile)
    def _(i):
        at = pl.ds(pl.multiple_of(i * row_tile, row_tile), row_tile)
        value = hidden[at, :] + dot_nt(branch[at, :], wide[3])
        hidden[at, :] = value
        if last:

            @pl.when(ending)
            def _():
                unit = norm_stats(value)[1]
                value_two = (unit * gain[...]).astype(BF)
                normed_two[at, :] = value_two
                for_twin[at, :] = other_core_first(value_two)


def mixer_part(lengths, normed, tokens, conv, gain, cells, before, last, ties, tile):
    rows, width = normed.shape
    _, zs, kinds, block, columns = cells[0].shape
    first = before is None
    whole = whole_spec((rows, width))
    inputs = [lengths, normed, tokens, conv, gain, *cells]
    inputs += ([] if first else [before]) + list(ties)
    outs = [jax.ShapeDtypeStruct((3, rows, 2 * columns), F32), jax.ShapeDtypeStruct((rows, width), F32)]
    out_specs = [pl.BlockSpec((3, rows, 2 * tile), lambda j: (0, 0, j)), whole]
    if last:
        outs += [jax.ShapeDtypeStruct((rows, width), BF)] * 2
        out_specs += [whole] * 2
    return pl.pallas_call(
        functools.partial(mixer_kernel, first, last, len(ties), min(rows, 256)),
        grid=(columns // tile,),
        in_specs=[pl.BlockSpec(memory_space=pltpu.SMEM), whole, whole]
        + [pl.BlockSpec((2, conv.shape[1], tile), lambda j: (0, 0, j)), whole_spec((1, width))]
        + cell_specs(cells, tile)
        + [whole] * (0 if first else 1)
        + [ANYWHERE] * len(ties),
        out_specs=out_specs,
        out_shape=outs,
        scratch_shapes=[
            pltpu.VMEM((kinds, width, 2 * tile), BF),
            pltpu.VMEM((rows, 2 * tile), BF),
        ],
        input_output_aliases={} if first else {7: 1},
        compiler_params=params(),
        cost_estimate=pl.CostEstimate(
            flops=16 * COST * rows * width * columns,
            bytes_accessed=24 * rows * columns + 16 * width * columns + 8 * rows * width,
            transcendentals=0,
        ),
    )(*inputs)


def mixer_back_kernel(first, ties, row_tile, *refs):
    feed = iter(refs)
    take = lambda n: [next(feed) for _ in range(n)]
    lengths, normed, grad_mix, project, conv = take(5)
    cells = take(2)
    before = [] if first else take(1)
    take(ties)
    keep, send, tap_grads, grad_normed = take(4)
    wide, branch, grads, grad_branch = take(4)
    step = pl.program_id(0)
    rows = normed.shape[0]
    _, zs, _, block, tile = cells[0].shape
    lay_out(*cells, wide)

    @pl.when(step == 0)
    def _():
        grad_normed[...] = jnp.zeros_like(grad_normed) if first else before[0][...]

    @pl.loop(0, rows // row_tile)
    def _(i):
        at = pl.ds(pl.multiple_of(i * row_tile, row_tile), row_tile)
        grad_branch[at, :] = dot_nn(grad_mix[at, :], wide[3])

    taps = tile_conv(conv[...])
    count = taps.shape[0]
    sums = [jnp.zeros((1, 2 * tile), F32)] * count
    for sequence in range(rows // SLOTS):
        at = slice(sequence * SLOTS, (sequence + 1) * SLOTS)
        position = lax.broadcasted_iota(jnp.int32, (SLOTS, 2 * tile), 0)
        living = position < lengths[sequence]
        gated = jnp.where(living, project[0, at] * project[2, at], 0.0)
        mixed = taps[0:1] * gated
        g_mixed = grad_branch[at, :] * project[1, at]
        sums[0] = sums[0] + jnp.sum(g_mixed * gated, axis=0, keepdims=True)
        g_gated = taps[0:1] * g_mixed
        for shift in range(1, count):
            lower = moved(gated, shift, position)
            mixed = mixed + taps[shift : shift + 1] * lower
            sums[shift] = sums[shift] + jnp.sum(g_mixed * lower, axis=0, keepdims=True)
            g_gated = g_gated + taps[shift : shift + 1] * moved(g_mixed, -shift, position)
        g_gated = jnp.where(living, g_gated, 0.0)
        branch[at, :] = (project[1, at] * mixed).astype(BF)
        grads[0, at, :] = (g_gated * project[2, at]).astype(BF)
        grads[1, at, :] = (grad_branch[at, :] * mixed).astype(BF)
        grads[2, at, :] = (g_gated * project[0, at]).astype(BF)
    tap_grads[...] = jnp.concatenate(
        sums + [jnp.zeros((8 - count, 2 * tile), F32)], axis=0
    )

    @pl.loop(0, rows // row_tile)
    def _(i):
        at = pl.ds(pl.multiple_of(i * row_tile, row_tile), row_tile)
        value = dot_nt(grads[0, at, :], wide[0]) + dot_nt(grads[1, at, :], wide[1])
        grad_normed[at, :] += value + dot_nt(grads[2, at, :], wide[2])

    depth = zs * block
    for place in range(4):
        at = slice(place * depth, (place + 1) * depth)
        core, x = divmod(place, 2)
        out = send if core else keep
        for k in range(4):
            if k < 3:
                value = dot_tn(normed[:, at], grads[k])
            else:
                value = dot_tn(grad_mix[:, at], branch[...])
            value = value.astype(BF)
            for z in range(zs):
                part = value[z * block : (z + 1) * block]
                out[2 * x, z, k] = part[:, :tile]
                out[2 * x + 1, z, k] = part[:, tile:]


def mixer_back(lengths, normed, grad_mix, project, conv, cells, before, ties, tile, part, parts):
    rows, width = normed.shape
    _, zs, kinds, block, columns = cells[0].shape
    columns = columns // parts
    skip = part * (columns // tile)
    first = before is None
    whole = whole_spec((rows, width))
    inputs = [lengths, normed, grad_mix, project, conv, *cells]
    inputs += ([] if first else [before]) + list(ties)
    grads = pl.BlockSpec((4, zs, kinds, block, tile), lambda j: (0, 0, 0, 0, j))
    grad_shape = jax.ShapeDtypeStruct((4, zs, kinds, block, columns), BF)
    return pl.pallas_call(
        functools.partial(mixer_back_kernel, first, len(ties), min(rows, 256)),
        grid=(columns // tile,),
        in_specs=[pl.BlockSpec(memory_space=pltpu.SMEM), whole, whole]
        + [pl.BlockSpec((3, rows, 2 * tile), lambda j: (0, 0, j + skip))]
        + [pl.BlockSpec((2, conv.shape[1], tile), lambda j: (0, 0, j + skip))]
        + cell_specs(cells, tile, skip)
        + [whole] * (0 if first else 1)
        + [ANYWHERE] * len(ties),
        out_specs=[grads, grads, pl.BlockSpec((8, 2 * tile), lambda j: (0, j)), whole],
        out_shape=[
            grad_shape,
            grad_shape,
            jax.ShapeDtypeStruct((8, 2 * columns), F32),
            jax.ShapeDtypeStruct((rows, width), F32),
        ],
        scratch_shapes=[
            pltpu.VMEM((kinds, width, 2 * tile), BF),
            pltpu.VMEM((rows, 2 * tile), BF),
            pltpu.VMEM((3, rows, 2 * tile), BF),
            pltpu.VMEM((rows, 2 * tile), F32),
        ],
        input_output_aliases={} if first else {7: 3},
        compiler_params=params(),
        cost_estimate=pl.CostEstimate(
            flops=32 * COST * rows * width * columns,
            bytes_accessed=24 * rows * columns + 32 * width * columns + 8 * rows * width,
            transcendentals=0,
        ),
    )(*inputs)


def reorder(source, target, flip, inward):
    width = source.shape[1]
    for case in range(4):

        @pl.when(flip == case)
        def _():
            count = SHARDS[0]
            block, zs = width // count, count // 4
            for place in range(count):
                core, x, z = place // (2 * zs), place // zs % 2, place % zs
                absolute = z * 4 + (case ^ (x * 2 + core))
                here = slice(place * block, (place + 1) * block)
                there = slice(absolute * block, (absolute + 1) * block)
                if inward:
                    target[:, here] = source[:, there]
                else:
                    target[:, there] = source[:, here]


def row_call(kernel, flip, inputs, outs, sums=0, ties=()):
    rows, width = next(item.shape for item in inputs if item.shape[0] > 1)
    height = min(ROW_TILE, rows)
    tiled = pl.BlockSpec((height, width), lambda i: (i, 0))
    scalar = pl.BlockSpec(memory_space=pltpu.SMEM)
    specs = [
        scalar if item.ndim == 1 else tiled if item.shape[0] > 1 else whole_spec((1, width))
        for item in inputs
    ]
    count = len(inputs) + 1

    def body(*refs):
        kernel(*refs[:count], *refs[count + len(ties) :])

    return pl.pallas_call(
        body,
        grid=(rows // height,),
        in_specs=[scalar] + specs + [ANYWHERE] * len(ties),
        out_specs=[tiled] * len(outs) + [whole_spec((8, width))] * sums,
        out_shape=[jax.ShapeDtypeStruct((rows, width), dtype) for dtype in outs]
        + [jax.ShapeDtypeStruct((8, width), F32)] * sums,
        scratch_shapes=[pltpu.VMEM((height, width), F32)] * 2,
        compiler_params=params(),
        cost_estimate=cost(20 * rows * width, 12 * rows * width),
    )(flip, *inputs, *ties)


def enter_kernel(flip, lengths, tokens, cotangent, gain, low, normed, grad, for_twin, one, two):
    one[...] = tokens[...].astype(F32)
    reorder(one, two, flip[0], True)
    value = two[...]
    low[...] = value.astype(BF)
    normed[...] = (norm_stats(value)[1] * gain[...]).astype(BF)
    one[...] = cotangent[...].astype(F32)
    reorder(one, two, flip[0], True)
    height = value.shape[0]
    first = pl.program_id(0) * height
    position = first % SLOTS + lax.broadcasted_iota(jnp.int32, value.shape, 0)
    value = jnp.where(position < lengths[first // SLOTS], two[...], 0.0).astype(BF)
    grad[...] = value
    for_twin[...] = other_core_first(value)


def add_up(total, values):
    part = jnp.sum(values.reshape(-1, 8, values.shape[1]), axis=0)

    @pl.when(pl.program_id(0) == 0)
    def _():
        total[...] = part

    @pl.when(pl.program_id(0) > 0)
    def _():
        total[...] += part


def between_kernel(flip, mine, twin, hidden, grad_out, gain, mix, total, one, two):
    grad = mine[...] + twin[...].astype(F32)
    inverse, unit = norm_stats(hidden[...])
    value = grad_out[...].astype(F32) + norm_back(grad, gain[...], inverse, unit)
    mix[...] = value.astype(BF)
    add_up(total, grad * unit)


def leave_kernel(flip, grad, tokens, grad_hidden, gain, out, total, one, two):
    inverse, unit = norm_stats(tokens[...].astype(F32))
    value = grad[...]
    one[...] = grad_hidden[...].astype(F32) + norm_back(value, gain[...], inverse, unit)
    reorder(one, out, flip[0], False)
    add_up(total, value * unit)


def result_kernel(flip, hidden, mine, twin, out, one, two):
    one[...] = hidden[...] + mine[...] + twin[...].astype(F32)
    reorder(one, two, flip[0], False)
    out[...] = two[...].astype(BF)


SHARDS = [16]


def ffn_sizes(columns, rows):
    if rows <= 1024 and columns == sum(SIZES):
        return SIZES
    return (128,) * (columns // 128)


def norm_stats(values):
    inverse = lax.rsqrt(jnp.mean(values * values, axis=-1, keepdims=True) + EPS)
    return (inverse, values * inverse)


def norm_back(grad_normed, gain, inverse, unit):
    scaled = grad_normed * gain
    return inverse * (scaled - unit * jnp.mean(scaled * unit, axis=-1, keepdims=True))


def body(
    tokens,
    lengths,
    in_proj,
    conv_weight,
    out_proj,
    norm_gain,
    ffn_gain,
    w_gate,
    w_up,
    w_down,
    cotangent,
):
    rows, width = tokens.shape
    links = Links(lax.axis_size("dp"), lax.axis_size("tensor"))
    rank = lax.axis_index("tensor")
    kernel = conv_weight.shape[0]
    half = in_proj.shape[2]
    hidden_half = w_gate.shape[1]
    block = width // links.dp

    core = lax.axis_index("dp") % 2
    mixer_own = jnp.concatenate([in_proj.astype(BF), out_proj.T.astype(BF)[None]], axis=0)
    ffn_own = jnp.stack([w_gate.astype(BF), w_up.astype(BF), w_down.T.astype(BF)])
    tile = 256 if half % 512 == 0 and rows <= 1024 else 128
    shared = hidden_half // 2
    mine_of = lax.dynamic_slice_in_dim(ffn_own, core * shared, shared, 2)
    twin_of = lax.dynamic_slice_in_dim(ffn_own, (1 - core) * shared, shared, 2)
    ffn_both = jnp.stack([mine_of, links.swap(twin_of, c=1)])
    sizes = ffn_sizes(shared, rows)
    starts = [sum(sizes[:p]) for p in range(len(sizes))]
    own = [mixer_own] + [ffn_both[..., at : at + size] for at, size in zip(starts, sizes)]
    own = [links.spread(item) for item in own]
    pieces = len(own)
    last = pieces - 1
    mine, sides, corner = {}, {}, {}

    def cells(p):
        from_x, from_y = sides[p]
        return [mine[p], from_y, from_x, *corner[p]]

    sums = {}

    def start(stage, p):
        if stage == "z":
            mine[p] = links.turn_z(own[p])
            return mine, p
        if stage == "sides":
            sides[p] = links.gather_sides(mine[p])
            return sides, p
        if stage == "corner":
            corner[p] = links.gather_corner(*sides[p])
            return corner, p
        item = sums[p]
        if stage == "sum core":
            item["got"] = links.swap(item["send"], c=1)
            return item, "got"
        raise ValueError(stage)

    def add(*steps):
        jobs, keys = [], []
        for stage, p in steps:
            item = sums[p]
            if stage == "sum sides":
                jobs.append(add_sides(*item["parts"][2:4], *item["corner"]))
                keys.append((item, "next"))
            elif stage == "sum z":
                jobs.append(add_own(item["parts"][4], *item["corner"], *item["sides"]))
                keys.append((item, "total"))
            elif "keep" in item:
                jobs.append(both_cores(item["keep"], item["got"]))
                keys.append((item, "parts"))
        if jobs:
            for (item, key), out in zip(keys, small_calls(jobs)):
                item[key] = out
        places = []
        for stage, p in steps:
            item = sums[p]
            if stage == "sum z":
                item["z"] = links.turn_z(item["total"][0])
                places.append((item, "z"))
                continue
            pair = item["next"] if stage == "sum sides" else item["parts"][:2]
            key = stage[4:]
            item[key] = links.swap(pair[0], x=1), links.swap(pair[1], y=1)
            places.append((item, key))
        return places

    def close(kept, places):
        kept, tree = jax.tree.flatten([kept, [store[key] for store, key in places]])
        kept, arrived = jax.tree.unflatten(tree, gate(kept))
        for (store, key), value in zip(places, arrived):
            store[key] = value
        return kept

    blocks = links.absolute(jnp.arange(links.dp))
    gain_one = jnp.take(norm_gain.reshape(links.dp, block), blocks, axis=0).reshape(1, width)
    gain_two = jnp.take(ffn_gain.reshape(links.dp, block), blocks, axis=0).reshape(1, width)
    conv = jnp.where(rank == 0, conv_weight, jnp.roll(conv_weight, half, axis=1))
    conv = conv.reshape(kernel, 2, half).transpose(1, 0, 2)
    count = rows // SLOTS
    own_lengths = lax.dynamic_slice_in_dim(lengths, rank * count, count)
    flip = (lax.axis_index("dp") % 4)[None]
    SHARDS[0] = links.dp
    tokens_low, normed, grad_ffn, for_twin_grad = row_call(
        enter_kernel, flip, [own_lengths, tokens, cotangent, gain_one], [BF] * 4, ties=own[1:]
    )

    places = [start("z", 0)]
    normed, for_twin_grad, own = close([normed, for_twin_grad, own], places)
    grad_ffn_twin = links.swap(for_twin_grad, c=1)
    places = [start("sides", 0), start("z", 1)]
    own[2:3], mine[0] = close([own[2:3], mine[0]], places)
    places = [start("corner", 0), start("z", 2)]
    own[3:4], mine[1] = close([own[3:4], mine[1]], places)
    joined = join(*cells(0))
    mixer_cells = [joined, links.swap(joined, c=1)]

    places = [start("sides", 1), start("sides", 2), start("z", 3)]
    project, hidden, normed_two, for_twin = mixer_part(
        own_lengths, normed, tokens_low, conv, gain_two, mixer_cells, None, True, [], tile
    )
    normed_two, for_twin, own[4:5] = close([normed_two, for_twin, own[4:5]], places)
    start("corner", 1)
    inputs = [normed_two, links.swap(for_twin, c=1), grad_ffn, grad_ffn_twin]

    totals = None
    for p in range(1, pieces):
        places = []
        for stage, q in (("corner", p + 1), ("sides", p + 2), ("z", p + 3)):
            if q < pieces:
                places.append(start(stage, q))
        steps = (("sum z", p - 4), ("sum sides", p - 3), ("sum corner", p - 2))
        places += add(*[step for step in steps if step[1] > 0])
        *parts, t0, t1, t2, t3 = ffn_piece(inputs, cells(p), totals, p == last, [])
        held = sums[p - 1]["parts"][:2] if p > 1 else []
        parts, totals, held = close([parts, [t0, t1, t2, t3], held], places)
        if p > 1:
            sums[p - 1]["parts"][:2] = held
        sums[p] = dict(parts=list(parts))
    ffn_twin = links.swap(totals[2], c=1)
    grad_mix, gain_two_part = row_call(
        between_kernel,
        flip,
        [totals[1], links.swap(totals[3], c=1), hidden, grad_ffn, gain_two],
        [BF],
        1,
    )
    places = add(("sum z", last - 3), ("sum sides", last - 2), ("sum corner", last - 1))
    parts = 2 if half % 256 == 0 else 1
    names = [f"mixer {p}" for p in range(parts)]
    grad_normed, taps = None, []
    for p, name in enumerate(names):
        if p:
            places = [start("sum core", names[0])]
        if p == parts - 1:
            places += add(("sum z", last - 2), ("sum sides", last - 1), ("sum corner", last))
        keep, send, tap_grads, grad_normed = mixer_back(
            own_lengths, normed, grad_mix, project, conv, mixer_cells, grad_normed, [],
            tile, p, parts,
        )
        held = sums[last]["parts"][:2] if p < parts - 1 else []
        keep, send, tap_grads, grad_normed, ffn_twin, held = close(
            [keep, send, tap_grads, grad_normed, ffn_twin, held], places
        )
        if p < parts - 1:
            sums[last]["parts"][:2] = held
        taps.append(tap_grads)
        sums[name] = dict(keep=keep, send=send)
    places = [start("sum core", names[-1])]
    steps = [("sum z", last - 1), ("sum sides", last)]
    if parts > 1:
        steps.append(("sum corner", names[0]))
    places += add(*steps)[1:]
    grad_tokens, gain_one_part = row_call(
        leave_kernel, flip, [grad_normed, tokens_low, grad_mix, gain_one], [F32], 1
    )
    item = sums[names[-1]]
    grad_tokens, gain_one_part, item["keep"] = close(
        [grad_tokens, gain_one_part, item["keep"]], places
    )

    place = links.place(jnp.arange(links.dp))
    taps = jnp.concatenate(taps, axis=1)[:kernel].reshape(kernel, -1, 2, tile)
    taps = taps.transpose(0, 2, 1, 3).reshape(kernel, width)
    taps = jnp.where(rank == 0, taps, jnp.roll(taps, half, axis=1))
    gains = jnp.stack([gain_one_part.sum(0), gain_two_part.sum(0)])
    gains = jnp.take(gains.reshape(2, links.dp, block), place, axis=1).reshape(2, width)
    small = links.sum_chip(jnp.concatenate([gains, taps], axis=0))

    steps = [("sum corner", names[-1]), ("sum z", last)]
    if parts > 1:
        steps.append(("sum sides", names[0]))
    places = add(*steps)
    result = row_call(
        result_kernel, flip, [hidden, totals[0], ffn_twin], [BF]
    )[0]
    result, small = close([result, small], places)
    steps = [("sum sides", names[-1])]
    if parts > 1:
        steps.append(("sum z", names[0]))
    places = add(*steps)
    (small,) = close([links.sum_rest(small)], places)
    add(("sum z", names[-1]))
    shard = lambda p: jnp.sum(sums[p]["z"].astype(F32), axis=0)
    mixer_shard = jnp.concatenate([shard(name) for name in names], axis=2)
    ffn_shard = jnp.concatenate([shard(p) for p in range(1, pieces)], axis=3)
    here, there = ffn_shard[0], links.swap(ffn_shard[1], c=1)
    ffn_shard = jnp.concatenate(
        [jnp.where(core == 0, here, there), jnp.where(core == 0, there, here)], axis=2
    )
    return (
        result,
        grad_tokens,
        mixer_shard[:3],
        small[2:],
        mixer_shard[3].T,
        small[0],
        small[1],
        ffn_shard[0],
        ffn_shard[1],
        ffn_shard[2].T,
    )


def solution(mesh):
    rows = P(("dp", "tensor"), None)
    in_specs = (
        rows,
        P("dp"),
        P(None, "dp", "tensor"),
        P(),
        P("tensor", "dp"),
        P(),
        P(),
        P("dp", "tensor"),
        P("dp", "tensor"),
        P("tensor", "dp"),
        rows,
    )
    out_specs = (
        rows,
        rows,
        P(None, "dp", "tensor"),
        P(),
        P("tensor", "dp"),
        P(),
        P(),
        P("dp", "tensor"),
        P("dp", "tensor"),
        P("tensor", "dp"),
    )
    return jax.shard_map(body, mesh=mesh, in_specs=in_specs, out_specs=out_specs, check_vma=False)
```

```python
import functools

import jax
import jax.numpy as jnp
from jax import lax
from jax.experimental import pallas as pl
from jax.experimental.pallas import tpu as pltpu
from jax.sharding import PartitionSpec as P

SLOTS = 1024
EPS = 1e-05
AXES = ("dp", "tensor")
ROW_TILE = 256
SIZES = (256, 256, 384, 256)
COST = 4
VMEM = 60 * 2**20
BF = jnp.bfloat16
F32 = jnp.float32
ANYWHERE = pl.BlockSpec(memory_space=pl.ANY)


def dot_nn(left, right):
    return jnp.dot(left, right, preferred_element_type=F32)


def dot_tn(left, right):
    return lax.dot_general(left, right, (((0,), (0,)), ((), ())), preferred_element_type=F32)


def dot_nt(left, right):
    return lax.dot_general(left, right, (((1,), (1,)), ((), ())), preferred_element_type=F32)


class Links:
    def __init__(self, dp, tp):
        self.dp, self.tp, self.zs = dp, tp, dp // 4

    def swap(self, value, x=0, c=0, y=0, z=0):
        flip = (z * 2 + x) * 2 + c
        pairs = [
            (q * self.tp + t, (q ^ flip) * self.tp + (t ^ y))
            for q in range(self.dp)
            for t in range(self.tp)
        ]
        return lax.ppermute(value, AXES, pairs)

    def turn_z(self, value):
        groups = [[z * 4 + rest for z in range(self.zs)] for rest in range(4)]
        return lax.all_to_all(value, "dp", 0, 0, axis_index_groups=groups, tiled=True)

    def spread(self, own):
        return jnp.broadcast_to(own[None], (self.zs, *own.shape))

    def gather_sides(self, mine):
        return self.swap(mine, x=1), self.swap(mine, y=1)

    def gather_corner(self, from_x, from_y):
        low, high = cut(from_x, from_y)
        return self.swap(low, y=1), self.swap(high, x=1)

    def sum_chip(self, value):
        value = value + self.swap(value, c=1)
        return value + self.swap(value, y=1)

    def sum_rest(self, value):
        value = value + self.swap(value, x=1)
        others = [self.swap(value, z=z) for z in range(1, self.zs)]
        return functools.reduce(jnp.add, others, value)

    def absolute(self, place):
        q = lax.axis_index("dp")
        core, x, z = place // (2 * self.zs), place // self.zs % 2, place % self.zs
        return z * 4 + ((q % 4) ^ (x * 2 + core))

    def place(self, absolute):
        q = lax.axis_index("dp")
        apart = (absolute % 4) ^ (q % 4)
        return ((apart % 2) * 2 + apart // 2) * self.zs + absolute // 4


def whole_spec(shape, buffers=1):
    return pl.BlockSpec(
        shape, lambda *_: (0,) * len(shape), pipeline_mode=pl.Buffered(buffers)
    )


def params():
    return pltpu.CompilerParams(vmem_limit_bytes=VMEM)


def cost(flops, moved_bytes):
    return pl.CostEstimate(flops=flops, bytes_accessed=moved_bytes, transcendentals=0)


def small_calls(jobs):
    tiles = [inputs[0].shape[-1] // 128 for _, inputs, _ in jobs]

    def spec(shape, count):
        zeros = (0,) * (len(shape) - 1)
        return pl.BlockSpec(
            (*shape[:-1], 128), lambda j: (*zeros, jnp.minimum(j, count - 1))
        )

    n_in = [len(inputs) for _, inputs, _ in jobs]
    n_out = [len(shapes) for _, _, shapes in jobs]

    def body(*refs):
        ins, outs = list(refs[: sum(n_in)]), list(refs[sum(n_in) :])
        for (kernel, _, _), count, i, o in zip(jobs, tiles, n_in, n_out):
            here, ins = ins[:i], ins[i:]
            there, outs = outs[:o], outs[o:]

            @pl.when(pl.program_id(0) < count)
            def _():
                kernel(*here, *there)

    arrays = [item for _, inputs, _ in jobs for item in inputs]
    out = pl.pallas_call(
        body,
        grid=(max(tiles),),
        in_specs=[
            spec(item.shape, count) for (_, inputs, _), count in zip(jobs, tiles) for item in inputs
        ],
        out_specs=[
            spec(shape, count) for (_, _, shapes), count in zip(jobs, tiles) for shape in shapes
        ],
        out_shape=[jax.ShapeDtypeStruct(shape, BF) for _, _, shapes in jobs for shape in shapes],
        compiler_params=params(),
        cost_estimate=cost(0, 4 * sum(item.size for item in arrays)),
    )(*arrays)
    result = []
    for o in n_out:
        result.append(out[:o])
        out = out[o:]
    return result


def gate(values):
    def nothing(*refs):
        del refs

    count = len(values)
    return pl.pallas_call(
        nothing,
        in_specs=[ANYWHERE] * count,
        out_specs=[ANYWHERE] * count,
        out_shape=[jax.ShapeDtypeStruct(item.shape, item.dtype) for item in values],
        input_output_aliases={i: i for i in range(count)},
        compiler_params=params(),
        cost_estimate=cost(0, 1024),
    )(*values)


def cut_kernel(from_x, from_y, low, high):
    low[...] = from_x[...]
    high[...] = from_y[...]


def cut(from_x, from_y):
    half, *rest, columns = from_x.shape
    half //= 2
    lead = (0,) * len(rest)
    block = (half, *rest, 128)
    low = pl.BlockSpec(block, lambda j: (0, *lead, j))
    high = pl.BlockSpec(block, lambda j: (1, *lead, j))
    return pl.pallas_call(
        cut_kernel,
        grid=(columns // 128,),
        in_specs=[low, high],
        out_specs=[low] * 2,
        out_shape=[jax.ShapeDtypeStruct((half, *rest, columns), BF)] * 2,
        compiler_params=params(),
        cost_estimate=cost(0, 4 * from_x.size),
    )(from_x, from_y)


def join_kernel(mine, from_y, from_x, one, two, out):
    half = one.shape[0]
    out[0] = mine[...]
    out[1] = from_y[...]
    out[2] = from_x[...]
    out[3, :half] = one[...]
    out[3, half:] = two[...]


def join(mine, from_y, from_x, one, two):
    job = (join_kernel, [mine, from_y, from_x, one, two], [(4, *mine.shape)])
    return small_calls([job])[0][0]


def both_kernel(keep, got, send_x, send_y, rest_x, rest_y, own):
    half = keep.shape[1] // 2

    def total(cell, part):
        return (keep[cell, part].astype(F32) + got[cell, part].astype(F32)).astype(BF)

    low, high = slice(0, half), slice(half, 2 * half)
    send_x[0], send_x[1] = total(3, low), total(2, low)
    send_y[0], send_y[1] = total(3, high), total(1, high)
    rest_x[...], rest_y[...] = total(2, high), total(1, low)
    own[:half], own[half:] = total(0, low), total(0, high)


def both_cores(keep, got):
    _, zs, *rest = keep.shape
    part = (zs // 2, *rest)
    shapes = [(2, *part), (2, *part), part, part, (zs, *rest)]
    return both_kernel, [keep, got], shapes


def sides_kernel(rest_x, rest_y, got_x, got_y, send_x, send_y):
    send_x[...] = (rest_x[...].astype(F32) + got_y[0].astype(F32)).astype(BF)
    send_y[...] = (rest_y[...].astype(F32) + got_x[0].astype(F32)).astype(BF)


def add_sides(rest_x, rest_y, got_x, got_y):
    return sides_kernel, [rest_x, rest_y, got_x, got_y], [rest_x.shape] * 2


def own_kernel(own, got_x, got_y, side_x, side_y, out):
    half = side_x.shape[0]
    low = own[:half].astype(F32) + got_x[1].astype(F32) + side_y[...].astype(F32)
    high = own[half:].astype(F32) + got_y[1].astype(F32) + side_x[...].astype(F32)
    out[:half] = low.astype(BF)
    out[half:] = high.astype(BF)


def add_own(own, got_x, got_y, side_x, side_y):
    return own_kernel, [own, got_x, got_y, side_x, side_y], [own.shape]


def ffn_kernel(first, last, ties, *refs):
    feed = iter(refs)
    take = lambda n: [next(feed) for _ in range(n)]
    normed, normed_twin, grad_out, grad_out_twin = take(4)
    mine, from_y, from_x, one, two = take(5)
    before = [] if first else take(4)
    take(ties)
    send_x, send_y, rest_x, rest_y, own = take(5)
    totals = take(4)
    wide, rows_n, rows_g, active, grad_gate, grad_up = take(6)
    step = pl.program_id(0)
    steps = pl.num_programs(0)
    zs, _, kinds, block, tile = mine.shape
    half = zs // 2
    height = normed.shape[0]
    places = [(core, x, z) for core in range(2) for x in range(2) for z in range(zs)]

    @pl.when(step == 0)
    def _():
        for at, (core, x, z) in enumerate(places):
            rows = slice(at * block, (at + 1) * block)
            for k in range(kinds):
                if x == 0:
                    wide[k, rows, :tile] = mine[z, core, k]
                    wide[k, rows, tile:] = from_y[z, core, k]
                else:
                    wide[k, rows, :tile] = from_x[z, core, k]
                    corner = one[z, core, k] if z < half else two[z - half, core, k]
                    wide[k, rows, tile:] = corner

    at = pl.ds(pl.multiple_of(step * height, height), height)

    def work(normed, grad_out, before, totals, turn):
        left = normed[...]
        right = grad_out[...]
        rows_n[at, :] = left
        rows_g[at, :] = right
        gate, upward = dot_nn(left, wide[0]), dot_nn(left, wide[1])
        grad_active = dot_nn(right, wide[2])
        sigma = 1.0 / (1.0 + jnp.exp(-gate))
        silu = gate * sigma
        act = (silu * upward).astype(BF)
        g_up = (grad_active * silu).astype(BF)
        g_gate = (grad_active * upward * (sigma + silu * (1.0 - sigma))).astype(BF)
        active[at, :] = act
        grad_up[at, :] = g_up
        grad_gate[at, :] = g_gate
        ffn = dot_nt(act, wide[2])
        back = dot_nt(g_gate, wide[0]) + dot_nt(g_up, wide[1])
        if not first:
            ffn = ffn + before[0][...].astype(F32)
            back = back + before[1][...].astype(F32)
        if turn:
            ffn, back = other_core_first(ffn), other_core_first(back)
        totals[0][...] = ffn.astype(totals[0].dtype)
        totals[1][...] = back.astype(totals[1].dtype)

    @pl.when(step < steps // 2)
    def _():
        work(normed, grad_out, before[:2], totals[:2], False)

    @pl.when(step >= steps // 2)
    def _():
        work(normed_twin, grad_out_twin, before[2:], totals[2:], last)

    @pl.when(step == steps - 1)
    def _():
        group = 256 // block
        for first_place in range(0, len(places), group):
            rows = slice(first_place * block, (first_place + group) * block)
            for k, (left, right) in enumerate(
                ((rows_n, grad_gate), (rows_n, grad_up), (rows_g, active))
            ):
                value = dot_tn(left[:, rows], right[...]).astype(BF)
                for i in range(group):
                    core, x, z = places[first_place + i]
                    part = value[i * block : (i + 1) * block]
                    low, zh = z < half, z % half
                    near, far = part[:, :tile], part[:, tile:]
                    if x == 0:
                        own[z, core, k] = near
                        if low:
                            rest_y[zh, core, k] = far
                        else:
                            send_y[1, zh, core, k] = far
                    else:
                        if low:
                            send_x[1, zh, core, k] = near
                            send_x[0, zh, core, k] = far
                        else:
                            rest_x[zh, core, k] = near
                            send_y[0, zh, core, k] = far


def ffn_piece(inputs, cells, before, last, ties):
    rows, width = inputs[0].shape
    zs, _, kinds, block, columns = cells[0].shape
    first = before is None
    height = min(ROW_TILE, rows)
    half = rows // height
    near = pl.BlockSpec((height, width), lambda i: (jnp.minimum(i, half - 1), 0))
    far = pl.BlockSpec((height, width), lambda i: (jnp.maximum(i - half, 0), 0))
    operands = [*inputs, *cells, *(() if first else before), *ties]
    part = (zs // 2, 2, kinds, block, columns)
    grads = [(2, *part), (2, *part), part, part, (zs, *part[1:])]
    mine = F32 if last else BF
    return pl.pallas_call(
        functools.partial(ffn_kernel, first, last, len(ties)),
        grid=(2 * half,),
        in_specs=[near, far, near, far]
        + [whole_spec(item.shape) for item in cells]
        + ([] if first else [near, near, far, far])
        + [ANYWHERE] * len(ties),
        out_specs=[whole_spec(shape) for shape in grads] + [near, near, far, far],
        out_shape=[jax.ShapeDtypeStruct(shape, BF) for shape in grads]
        + [jax.ShapeDtypeStruct((rows, width), dtype) for dtype in (mine, mine, BF, BF)],
        scratch_shapes=[pltpu.VMEM((kinds, width, 2 * columns), BF)]
        + [pltpu.VMEM((2 * rows, width), BF)] * 2
        + [pltpu.VMEM((2 * rows, 2 * columns), BF)] * 3,
        compiler_params=params(),
        cost_estimate=cost(
            72 * COST * rows * width * columns, 24 * width * columns + 40 * rows * width
        ),
    )(*operands)


def lay_out(near, twin, wide):
    _, zs, kinds, block, tile = near.shape
    for core, cells in enumerate((near, twin)):
        for x in range(2):
            for z in range(zs):
                at = ((core * 2 + x) * zs + z) * block
                for k in range(kinds):
                    for y in range(2):
                        wide[k, at : at + block, y * tile : (y + 1) * tile] = cells[
                            2 * x + y, z, k
                        ]


def cell_specs(cells, tile, skip=0):
    return [
        pl.BlockSpec((*item.shape[:-1], tile), lambda j: (0, 0, 0, 0, j + skip))
        for item in cells
    ]


def other_core_first(values):
    half = values.shape[1] // 2
    return jnp.concatenate([values[:, half:], values[:, :half]], axis=1)


def moved(values, shift, position):
    rows = values.shape[0]
    turned = pltpu.roll(values, shift % rows, 0)
    inside = position >= shift if shift > 0 else position < rows + shift
    return jnp.where(inside, turned, 0.0)


def mixed_of(gated, conv, position):
    total = conv[0:1] * gated
    for shift in range(1, conv.shape[0]):
        total = total + conv[shift : shift + 1] * moved(gated, shift, position)
    return total


def tile_conv(conv):
    return jnp.concatenate([conv[0], conv[1]], axis=1)


def mixer_kernel(first, last, ties, row_tile, *refs):
    feed = iter(refs)
    take = lambda n: [next(feed) for _ in range(n)]
    lengths, normed, tokens, conv, gain = take(5)
    cells = take(2)
    before = [] if first else take(1)
    take(ties)
    project, hidden = take(2)
    normed_two, for_twin = take(2) if last else (None, None)
    wide, branch = take(2)
    step = pl.program_id(0)
    rows = normed.shape[0]
    lay_out(*cells, wide)

    @pl.loop(0, rows // row_tile)
    def _(i):
        at = pl.ds(pl.multiple_of(i * row_tile, row_tile), row_tile)
        left = normed[at, :]
        for k in range(3):
            project[k, at, :] = dot_nn(left, wide[k])

    taps = tile_conv(conv[...])
    for sequence in range(rows // SLOTS):
        at = slice(sequence * SLOTS, (sequence + 1) * SLOTS)
        position = lax.broadcasted_iota(jnp.int32, (SLOTS, wide.shape[2]), 0)
        gated = project[0, at] * project[2, at]
        gated = jnp.where(position < lengths[sequence], gated, 0.0)
        branch[at, :] = (project[1, at] * mixed_of(gated, taps, position)).astype(BF)

    @pl.when(step == 0)
    def _():
        if first:
            hidden[...] = tokens[...].astype(F32)
        else:
            hidden[...] = before[0][...]

    ending = step == pl.num_programs(0) - 1

    @pl.loop(0, rows // row_tile)
    def _(i):
        at = pl.ds(pl.multiple_of(i * row_tile, row_tile), row_tile)
        value = hidden[at, :] + dot_nt(branch[at, :], wide[3])
        hidden[at, :] = value
        if last:

            @pl.when(ending)
            def _():
                unit = norm_stats(value)[1]
                value_two = (unit * gain[...]).astype(BF)
                normed_two[at, :] = value_two
                for_twin[at, :] = other_core_first(value_two)


def mixer_part(lengths, normed, tokens, conv, gain, cells, before, last, ties, tile):
    rows, width = normed.shape
    _, zs, kinds, block, columns = cells[0].shape
    first = before is None
    whole = whole_spec((rows, width))
    inputs = [lengths, normed, tokens, conv, gain, *cells]
    inputs += ([] if first else [before]) + list(ties)
    outs = [jax.ShapeDtypeStruct((3, rows, 2 * columns), F32), jax.ShapeDtypeStruct((rows, width), F32)]
    out_specs = [pl.BlockSpec((3, rows, 2 * tile), lambda j: (0, 0, j)), whole]
    if last:
        outs += [jax.ShapeDtypeStruct((rows, width), BF)] * 2
        out_specs += [whole] * 2
    return pl.pallas_call(
        functools.partial(mixer_kernel, first, last, len(ties), min(rows, 256)),
        grid=(columns // tile,),
        in_specs=[pl.BlockSpec(memory_space=pltpu.SMEM), whole, whole]
        + [pl.BlockSpec((2, conv.shape[1], tile), lambda j: (0, 0, j)), whole_spec((1, width))]
        + cell_specs(cells, tile)
        + [whole] * (0 if first else 1)
        + [ANYWHERE] * len(ties),
        out_specs=out_specs,
        out_shape=outs,
        scratch_shapes=[
            pltpu.VMEM((kinds, width, 2 * tile), BF),
            pltpu.VMEM((rows, 2 * tile), BF),
        ],
        input_output_aliases={} if first else {7: 1},
        compiler_params=params(),
        cost_estimate=pl.CostEstimate(
            flops=16 * COST * rows * width * columns,
            bytes_accessed=24 * rows * columns + 16 * width * columns + 8 * rows * width,
            transcendentals=0,
        ),
    )(*inputs)


def mixer_back_kernel(first, ties, row_tile, *refs):
    feed = iter(refs)
    take = lambda n: [next(feed) for _ in range(n)]
    lengths, normed, grad_mix, project, conv = take(5)
    cells = take(2)
    before = [] if first else take(1)
    take(ties)
    keep, send, tap_grads, grad_normed = take(4)
    wide, branch, grads, grad_branch = take(4)
    step = pl.program_id(0)
    rows = normed.shape[0]
    _, zs, _, block, tile = cells[0].shape
    lay_out(*cells, wide)

    @pl.when(step == 0)
    def _():
        grad_normed[...] = jnp.zeros_like(grad_normed) if first else before[0][...]

    @pl.loop(0, rows // row_tile)
    def _(i):
        at = pl.ds(pl.multiple_of(i * row_tile, row_tile), row_tile)
        grad_branch[at, :] = dot_nn(grad_mix[at, :], wide[3])

    taps = tile_conv(conv[...])
    count = taps.shape[0]
    sums = [jnp.zeros((1, 2 * tile), F32)] * count
    for sequence in range(rows // SLOTS):
        at = slice(sequence * SLOTS, (sequence + 1) * SLOTS)
        position = lax.broadcasted_iota(jnp.int32, (SLOTS, 2 * tile), 0)
        living = position < lengths[sequence]
        gated = jnp.where(living, project[0, at] * project[2, at], 0.0)
        mixed = taps[0:1] * gated
        g_mixed = grad_branch[at, :] * project[1, at]
        sums[0] = sums[0] + jnp.sum(g_mixed * gated, axis=0, keepdims=True)
        g_gated = taps[0:1] * g_mixed
        for shift in range(1, count):
            lower = moved(gated, shift, position)
            mixed = mixed + taps[shift : shift + 1] * lower
            sums[shift] = sums[shift] + jnp.sum(g_mixed * lower, axis=0, keepdims=True)
            g_gated = g_gated + taps[shift : shift + 1] * moved(g_mixed, -shift, position)
        g_gated = jnp.where(living, g_gated, 0.0)
        branch[at, :] = (project[1, at] * mixed).astype(BF)
        grads[0, at, :] = (g_gated * project[2, at]).astype(BF)
        grads[1, at, :] = (grad_branch[at, :] * mixed).astype(BF)
        grads[2, at, :] = (g_gated * project[0, at]).astype(BF)
    tap_grads[...] = jnp.concatenate(
        sums + [jnp.zeros((8 - count, 2 * tile), F32)], axis=0
    )

    @pl.loop(0, rows // row_tile)
    def _(i):
        at = pl.ds(pl.multiple_of(i * row_tile, row_tile), row_tile)
        value = dot_nt(grads[0, at, :], wide[0]) + dot_nt(grads[1, at, :], wide[1])
        grad_normed[at, :] += value + dot_nt(grads[2, at, :], wide[2])

    depth = zs * block
    for place in range(4):
        at = slice(place * depth, (place + 1) * depth)
        core, x = divmod(place, 2)
        out = send if core else keep
        for k in range(4):
            if k < 3:
                value = dot_tn(normed[:, at], grads[k])
            else:
                value = dot_tn(grad_mix[:, at], branch[...])
            value = value.astype(BF)
            for z in range(zs):
                part = value[z * block : (z + 1) * block]
                out[2 * x, z, k] = part[:, :tile]
                out[2 * x + 1, z, k] = part[:, tile:]


def mixer_back(lengths, normed, grad_mix, project, conv, cells, before, ties, tile, part, parts):
    rows, width = normed.shape
    _, zs, kinds, block, columns = cells[0].shape
    columns = columns // parts
    skip = part * (columns // tile)
    first = before is None
    whole = whole_spec((rows, width))
    inputs = [lengths, normed, grad_mix, project, conv, *cells]
    inputs += ([] if first else [before]) + list(ties)
    grads = pl.BlockSpec((4, zs, kinds, block, tile), lambda j: (0, 0, 0, 0, j))
    grad_shape = jax.ShapeDtypeStruct((4, zs, kinds, block, columns), BF)
    return pl.pallas_call(
        functools.partial(mixer_back_kernel, first, len(ties), min(rows, 256)),
        grid=(columns // tile,),
        in_specs=[pl.BlockSpec(memory_space=pltpu.SMEM), whole, whole]
        + [pl.BlockSpec((3, rows, 2 * tile), lambda j: (0, 0, j + skip))]
        + [pl.BlockSpec((2, conv.shape[1], tile), lambda j: (0, 0, j + skip))]
        + cell_specs(cells, tile, skip)
        + [whole] * (0 if first else 1)
        + [ANYWHERE] * len(ties),
        out_specs=[grads, grads, pl.BlockSpec((8, 2 * tile), lambda j: (0, j)), whole],
        out_shape=[
            grad_shape,
            grad_shape,
            jax.ShapeDtypeStruct((8, 2 * columns), F32),
            jax.ShapeDtypeStruct((rows, width), F32),
        ],
        scratch_shapes=[
            pltpu.VMEM((kinds, width, 2 * tile), BF),
            pltpu.VMEM((rows, 2 * tile), BF),
            pltpu.VMEM((3, rows, 2 * tile), BF),
            pltpu.VMEM((rows, 2 * tile), F32),
        ],
        input_output_aliases={} if first else {7: 3},
        compiler_params=params(),
        cost_estimate=pl.CostEstimate(
            flops=32 * COST * rows * width * columns,
            bytes_accessed=24 * rows * columns + 32 * width * columns + 8 * rows * width,
            transcendentals=0,
        ),
    )(*inputs)


def reorder(source, target, flip, inward):
    width = source.shape[1]
    for case in range(4):

        @pl.when(flip == case)
        def _():
            count = SHARDS[0]
            block, zs = width // count, count // 4
            for place in range(count):
                core, x, z = place // (2 * zs), place // zs % 2, place % zs
                absolute = z * 4 + (case ^ (x * 2 + core))
                here = slice(place * block, (place + 1) * block)
                there = slice(absolute * block, (absolute + 1) * block)
                if inward:
                    target[:, here] = source[:, there]
                else:
                    target[:, there] = source[:, here]


def row_call(kernel, flip, inputs, outs, sums=0, ties=()):
    rows, width = next(item.shape for item in inputs if item.shape[0] > 1)
    height = min(ROW_TILE, rows)
    tiled = pl.BlockSpec((height, width), lambda i: (i, 0))
    scalar = pl.BlockSpec(memory_space=pltpu.SMEM)
    specs = [
        scalar if item.ndim == 1 else tiled if item.shape[0] > 1 else whole_spec((1, width))
        for item in inputs
    ]
    count = len(inputs) + 1

    def body(*refs):
        kernel(*refs[:count], *refs[count + len(ties) :])

    return pl.pallas_call(
        body,
        grid=(rows // height,),
        in_specs=[scalar] + specs + [ANYWHERE] * len(ties),
        out_specs=[tiled] * len(outs) + [whole_spec((8, width))] * sums,
        out_shape=[jax.ShapeDtypeStruct((rows, width), dtype) for dtype in outs]
        + [jax.ShapeDtypeStruct((8, width), F32)] * sums,
        scratch_shapes=[pltpu.VMEM((height, width), F32)] * 2,
        compiler_params=params(),
        cost_estimate=cost(20 * rows * width, 12 * rows * width),
    )(flip, *inputs, *ties)


def enter_kernel(flip, lengths, tokens, cotangent, gain, low, normed, grad, for_twin, one, two):
    one[...] = tokens[...].astype(F32)
    reorder(one, two, flip[0], True)
    value = two[...]
    low[...] = value.astype(BF)
    normed[...] = (norm_stats(value)[1] * gain[...]).astype(BF)
    one[...] = cotangent[...].astype(F32)
    reorder(one, two, flip[0], True)
    height = value.shape[0]
    first = pl.program_id(0) * height
    position = first % SLOTS + lax.broadcasted_iota(jnp.int32, value.shape, 0)
    value = jnp.where(position < lengths[first // SLOTS], two[...], 0.0).astype(BF)
    grad[...] = value
    for_twin[...] = other_core_first(value)


def add_up(total, values):
    part = jnp.sum(values.reshape(-1, 8, values.shape[1]), axis=0)

    @pl.when(pl.program_id(0) == 0)
    def _():
        total[...] = part

    @pl.when(pl.program_id(0) > 0)
    def _():
        total[...] += part


def between_kernel(flip, mine, twin, hidden, grad_out, gain, mix, total, one, two):
    grad = mine[...] + twin[...].astype(F32)
    inverse, unit = norm_stats(hidden[...])
    value = grad_out[...].astype(F32) + norm_back(grad, gain[...], inverse, unit)
    mix[...] = value.astype(BF)
    add_up(total, grad * unit)


def leave_kernel(flip, grad, tokens, grad_hidden, gain, out, total, one, two):
    inverse, unit = norm_stats(tokens[...].astype(F32))
    value = grad[...]
    one[...] = grad_hidden[...].astype(F32) + norm_back(value, gain[...], inverse, unit)
    reorder(one, out, flip[0], False)
    add_up(total, value * unit)


def result_kernel(flip, hidden, mine, twin, out, one, two):
    one[...] = hidden[...] + mine[...] + twin[...].astype(F32)
    reorder(one, two, flip[0], False)
    out[...] = two[...].astype(BF)


SHARDS = [16]


def ffn_sizes(columns, rows):
    if rows <= 1024 and columns == sum(SIZES):
        return SIZES
    return (128,) * (columns // 128)


def norm_stats(values):
    inverse = lax.rsqrt(jnp.mean(values * values, axis=-1, keepdims=True) + EPS)
    return (inverse, values * inverse)


def norm_back(grad_normed, gain, inverse, unit):
    scaled = grad_normed * gain
    return inverse * (scaled - unit * jnp.mean(scaled * unit, axis=-1, keepdims=True))


def body(
    tokens,
    lengths,
    in_proj,
    conv_weight,
    out_proj,
    norm_gain,
    ffn_gain,
    w_gate,
    w_up,
    w_down,
    cotangent,
):
    rows, width = tokens.shape
    links = Links(lax.axis_size("dp"), lax.axis_size("tensor"))
    rank = lax.axis_index("tensor")
    kernel = conv_weight.shape[0]
    half = in_proj.shape[2]
    hidden_half = w_gate.shape[1]
    block = width // links.dp

    core = lax.axis_index("dp") % 2
    mixer_own = jnp.concatenate([in_proj.astype(BF), out_proj.T.astype(BF)[None]], axis=0)
    ffn_own = jnp.stack([w_gate.astype(BF), w_up.astype(BF), w_down.T.astype(BF)])
    tile = 256 if half % 512 == 0 and rows <= 1024 else 128
    shared = hidden_half // 2
    mine_of = lax.dynamic_slice_in_dim(ffn_own, core * shared, shared, 2)
    twin_of = lax.dynamic_slice_in_dim(ffn_own, (1 - core) * shared, shared, 2)
    ffn_both = jnp.stack([mine_of, links.swap(twin_of, c=1)])
    sizes = ffn_sizes(shared, rows)
    starts = [sum(sizes[:p]) for p in range(len(sizes))]
    own = [mixer_own] + [ffn_both[..., at : at + size] for at, size in zip(starts, sizes)]
    own = [links.spread(item) for item in own]
    pieces = len(own)
    last = pieces - 1
    mine, sides, corner = {}, {}, {}

    def cells(p):
        from_x, from_y = sides[p]
        return [mine[p], from_y, from_x, *corner[p]]

    sums = {}

    def start(stage, p):
        if stage == "z":
            mine[p] = links.turn_z(own[p])
            return mine, p
        if stage == "sides":
            sides[p] = links.gather_sides(mine[p])
            return sides, p
        if stage == "corner":
            corner[p] = links.gather_corner(*sides[p])
            return corner, p
        item = sums[p]
        if stage == "sum core":
            item["got"] = links.swap(item["send"], c=1)
            return item, "got"
        raise ValueError(stage)

    def add(*steps):
        jobs, keys = [], []
        for stage, p in steps:
            item = sums[p]
            if stage == "sum sides":
                jobs.append(add_sides(*item["parts"][2:4], *item["corner"]))
                keys.append((item, "next"))
            elif stage == "sum z":
                jobs.append(add_own(item["parts"][4], *item["corner"], *item["sides"]))
                keys.append((item, "total"))
            elif "keep" in item:
                jobs.append(both_cores(item["keep"], item["got"]))
                keys.append((item, "parts"))
        if jobs:
            for (item, key), out in zip(keys, small_calls(jobs)):
                item[key] = out
        places = []
        for stage, p in steps:
            item = sums[p]
            if stage == "sum z":
                item["z"] = links.turn_z(item["total"][0])
                places.append((item, "z"))
                continue
            pair = item["next"] if stage == "sum sides" else item["parts"][:2]
            key = stage[4:]
            item[key] = links.swap(pair[0], x=1), links.swap(pair[1], y=1)
            places.append((item, key))
        return places

    def close(kept, places):
        kept, tree = jax.tree.flatten([kept, [store[key] for store, key in places]])
        kept, arrived = jax.tree.unflatten(tree, gate(kept))
        for (store, key), value in zip(places, arrived):
            store[key] = value
        return kept

    blocks = links.absolute(jnp.arange(links.dp))
    gain_one = jnp.take(norm_gain.reshape(links.dp, block), blocks, axis=0).reshape(1, width)
    gain_two = jnp.take(ffn_gain.reshape(links.dp, block), blocks, axis=0).reshape(1, width)
    conv = jnp.where(rank == 0, conv_weight, jnp.roll(conv_weight, half, axis=1))
    conv = conv.reshape(kernel, 2, half).transpose(1, 0, 2)
    count = rows // SLOTS
    own_lengths = lax.dynamic_slice_in_dim(lengths, rank * count, count)
    flip = (lax.axis_index("dp") % 4)[None]
    SHARDS[0] = links.dp
    tokens_low, normed, grad_ffn, for_twin_grad = row_call(
        enter_kernel, flip, [own_lengths, tokens, cotangent, gain_one], [BF] * 4, ties=own[1:]
    )

    places = [start("z", 0)]
    normed, for_twin_grad, own = close([normed, for_twin_grad, own], places)
    grad_ffn_twin = links.swap(for_twin_grad, c=1)
    places = [start("sides", 0), start("z", 1)]
    own[2:3], mine[0] = close([own[2:3], mine[0]], places)
    places = [start("corner", 0), start("z", 2)]
    own[3:4], mine[1] = close([own[3:4], mine[1]], places)
    joined = join(*cells(0))
    mixer_cells = [joined, links.swap(joined, c=1)]

    places = [start("sides", 1), start("sides", 2), start("z", 3)]
    project, hidden, normed_two, for_twin = mixer_part(
        own_lengths, normed, tokens_low, conv, gain_two, mixer_cells, None, True, [], tile
    )
    normed_two, for_twin, own[4:5] = close([normed_two, for_twin, own[4:5]], places)
    start("corner", 1)
    inputs = [normed_two, links.swap(for_twin, c=1), grad_ffn, grad_ffn_twin]

    totals = None
    for p in range(1, pieces):
        places = []
        for stage, q in (("corner", p + 1), ("sides", p + 2), ("z", p + 3)):
            if q < pieces:
                places.append(start(stage, q))
        steps = (("sum z", p - 4), ("sum sides", p - 3), ("sum corner", p - 2))
        places += add(*[step for step in steps if step[1] > 0])
        *parts, t0, t1, t2, t3 = ffn_piece(inputs, cells(p), totals, p == last, [])
        held = sums[p - 1]["parts"][:2] if p > 1 else []
        parts, totals, held = close([parts, [t0, t1, t2, t3], held], places)
        if p > 1:
            sums[p - 1]["parts"][:2] = held
        sums[p] = dict(parts=list(parts))
    ffn_twin = links.swap(totals[2], c=1)
    grad_mix, gain_two_part = row_call(
        between_kernel,
        flip,
        [totals[1], links.swap(totals[3], c=1), hidden, grad_ffn, gain_two],
        [BF],
        1,
    )
    places = add(("sum z", last - 3), ("sum sides", last - 2), ("sum corner", last - 1))
    parts = 2 if half % 256 == 0 else 1
    names = [f"mixer {p}" for p in range(parts)]
    grad_normed, taps = None, []
    for p, name in enumerate(names):
        if p:
            places = [start("sum core", names[0])]
        if p == parts - 1:
            places += add(("sum z", last - 2), ("sum sides", last - 1), ("sum corner", last))
        keep, send, tap_grads, grad_normed = mixer_back(
            own_lengths, normed, grad_mix, project, conv, mixer_cells, grad_normed, [],
            tile, p, parts,
        )
        held = sums[last]["parts"][:2] if p < parts - 1 else []
        keep, send, tap_grads, grad_normed, ffn_twin, held = close(
            [keep, send, tap_grads, grad_normed, ffn_twin, held], places
        )
        if p < parts - 1:
            sums[last]["parts"][:2] = held
        taps.append(tap_grads)
        sums[name] = dict(keep=keep, send=send)
    places = [start("sum core", names[-1])]
    steps = [("sum z", last - 1), ("sum sides", last)]
    if parts > 1:
        steps.append(("sum corner", names[0]))
    places += add(*steps)[1:]
    grad_tokens, gain_one_part = row_call(
        leave_kernel, flip, [grad_normed, tokens_low, grad_mix, gain_one], [F32], 1
    )
    item = sums[names[-1]]
    grad_tokens, gain_one_part, item["keep"] = close(
        [grad_tokens, gain_one_part, item["keep"]], places
    )

    place = links.place(jnp.arange(links.dp))
    taps = jnp.concatenate(taps, axis=1)[:kernel].reshape(kernel, -1, 2, tile)
    taps = taps.transpose(0, 2, 1, 3).reshape(kernel, width)
    taps = jnp.where(rank == 0, taps, jnp.roll(taps, half, axis=1))
    gains = jnp.stack([gain_one_part.sum(0), gain_two_part.sum(0)])
    gains = jnp.take(gains.reshape(2, links.dp, block), place, axis=1).reshape(2, width)
    small = links.sum_chip(jnp.concatenate([gains, taps], axis=0))

    steps = [("sum corner", names[-1]), ("sum z", last)]
    if parts > 1:
        steps.append(("sum sides", names[0]))
    places = add(*steps)
    del places[1]
    result = row_call(
        result_kernel, flip, [hidden, totals[0], ffn_twin], [BF]
    )[0]
    result, small = close([result, small], places)
    steps = [("sum sides", names[-1])]
    if parts > 1:
        steps.append(("sum z", names[0]))
    places = add(*steps)[:1]
    (small,) = close([links.sum_rest(small)], places)
    add(("sum z", names[-1]))
    shard = lambda p: jnp.sum(sums[p]["z"].astype(F32), axis=0)
    mixer_shard = jnp.concatenate([shard(name) for name in names], axis=2)
    ffn_shard = jnp.concatenate([shard(p) for p in range(1, pieces)], axis=3)
    here, there = ffn_shard[0], links.swap(ffn_shard[1], c=1)
    ffn_shard = jnp.concatenate(
        [jnp.where(core == 0, here, there), jnp.where(core == 0, there, here)], axis=2
    )
    return (
        result,
        grad_tokens,
        mixer_shard[:3],
        small[2:],
        mixer_shard[3].T,
        small[0],
        small[1],
        ffn_shard[0],
        ffn_shard[1],
        ffn_shard[2].T,
    )


def solution(mesh):
    rows = P(("dp", "tensor"), None)
    in_specs = (
        rows,
        P("dp"),
        P(None, "dp", "tensor"),
        P(),
        P("tensor", "dp"),
        P(),
        P(),
        P("dp", "tensor"),
        P("dp", "tensor"),
        P("tensor", "dp"),
        rows,
    )
    out_specs = (
        rows,
        rows,
        P(None, "dp", "tensor"),
        P(),
        P("tensor", "dp"),
        P(),
        P(),
        P("dp", "tensor"),
        P("dp", "tensor"),
        P("tensor", "dp"),
    )
    return jax.shard_map(body, mesh=mesh, in_specs=in_specs, out_specs=out_specs, check_vma=False)
```

```python
import functools

import jax
import jax.numpy as jnp
from jax import lax
from jax.experimental import pallas as pl
from jax.experimental.pallas import tpu as pltpu
from jax.sharding import PartitionSpec as P

SLOTS = 1024
EPS = 1e-05
AXES = ("dp", "tensor")
ROW_TILE = 256
SIZES = (256, 256, 384, 256)
COST = 4
VMEM = 60 * 2**20
BF = jnp.bfloat16
F32 = jnp.float32
ANYWHERE = pl.BlockSpec(memory_space=pl.ANY)


def dot_nn(left, right):
    return jnp.dot(left, right, preferred_element_type=F32)


def dot_tn(left, right):
    return lax.dot_general(left, right, (((0,), (0,)), ((), ())), preferred_element_type=F32)


def dot_nt(left, right):
    return lax.dot_general(left, right, (((1,), (1,)), ((), ())), preferred_element_type=F32)


class Links:
    def __init__(self, dp, tp):
        self.dp, self.tp, self.zs = dp, tp, dp // 4

    def swap(self, value, x=0, c=0, y=0, z=0):
        flip = (z * 2 + x) * 2 + c
        pairs = [
            (q * self.tp + t, (q ^ flip) * self.tp + (t ^ y))
            for q in range(self.dp)
            for t in range(self.tp)
        ]
        return lax.ppermute(value, AXES, pairs)

    def turn_z(self, value):
        groups = [[z * 4 + rest for z in range(self.zs)] for rest in range(4)]
        return lax.all_to_all(value, "dp", 0, 0, axis_index_groups=groups, tiled=True)

    def spread(self, own):
        return jnp.broadcast_to(own[None], (self.zs, *own.shape))

    def gather_sides(self, mine):
        return self.swap(mine, x=1), self.swap(mine, y=1)

    def gather_corner(self, from_x, from_y):
        low, high = cut(from_x, from_y)
        return self.swap(low, y=1), self.swap(high, x=1)

    def sum_chip(self, value):
        value = value + self.swap(value, c=1)
        return value + self.swap(value, y=1)

    def sum_rest(self, value):
        value = value + self.swap(value, x=1)
        others = [self.swap(value, z=z) for z in range(1, self.zs)]
        return functools.reduce(jnp.add, others, value)

    def absolute(self, place):
        q = lax.axis_index("dp")
        core, x, z = place // (2 * self.zs), place // self.zs % 2, place % self.zs
        return z * 4 + ((q % 4) ^ (x * 2 + core))

    def place(self, absolute):
        q = lax.axis_index("dp")
        apart = (absolute % 4) ^ (q % 4)
        return ((apart % 2) * 2 + apart // 2) * self.zs + absolute // 4


def whole_spec(shape, buffers=1):
    return pl.BlockSpec(
        shape, lambda *_: (0,) * len(shape), pipeline_mode=pl.Buffered(buffers)
    )


def params():
    return pltpu.CompilerParams(vmem_limit_bytes=VMEM)


def cost(flops, moved_bytes):
    return pl.CostEstimate(flops=flops, bytes_accessed=moved_bytes, transcendentals=0)


def small_calls(jobs):
    tiles = [inputs[0].shape[-1] // 128 for _, inputs, _ in jobs]

    def spec(shape, count):
        zeros = (0,) * (len(shape) - 1)
        return pl.BlockSpec(
            (*shape[:-1], 128), lambda j: (*zeros, jnp.minimum(j, count - 1))
        )

    n_in = [len(inputs) for _, inputs, _ in jobs]
    n_out = [len(shapes) for _, _, shapes in jobs]

    def body(*refs):
        ins, outs = list(refs[: sum(n_in)]), list(refs[sum(n_in) :])
        for (kernel, _, _), count, i, o in zip(jobs, tiles, n_in, n_out):
            here, ins = ins[:i], ins[i:]
            there, outs = outs[:o], outs[o:]

            @pl.when(pl.program_id(0) < count)
            def _():
                kernel(*here, *there)

    arrays = [item for _, inputs, _ in jobs for item in inputs]
    out = pl.pallas_call(
        body,
        grid=(max(tiles),),
        in_specs=[
            spec(item.shape, count) for (_, inputs, _), count in zip(jobs, tiles) for item in inputs
        ],
        out_specs=[
            spec(shape, count) for (_, _, shapes), count in zip(jobs, tiles) for shape in shapes
        ],
        out_shape=[jax.ShapeDtypeStruct(shape, BF) for _, _, shapes in jobs for shape in shapes],
        compiler_params=params(),
        cost_estimate=cost(0, 4 * sum(item.size for item in arrays)),
    )(*arrays)
    result = []
    for o in n_out:
        result.append(out[:o])
        out = out[o:]
    return result


def gate(values):
    def nothing(*refs):
        del refs

    count = len(values)
    return pl.pallas_call(
        nothing,
        in_specs=[ANYWHERE] * count,
        out_specs=[ANYWHERE] * count,
        out_shape=[jax.ShapeDtypeStruct(item.shape, item.dtype) for item in values],
        input_output_aliases={i: i for i in range(count)},
        compiler_params=params(),
        cost_estimate=cost(0, 1024),
    )(*values)


def cut_kernel(from_x, from_y, low, high):
    low[...] = from_x[...]
    high[...] = from_y[...]


def cut(from_x, from_y):
    half, *rest, columns = from_x.shape
    half //= 2
    lead = (0,) * len(rest)
    block = (half, *rest, 128)
    low = pl.BlockSpec(block, lambda j: (0, *lead, j))
    high = pl.BlockSpec(block, lambda j: (1, *lead, j))
    return pl.pallas_call(
        cut_kernel,
        grid=(columns // 128,),
        in_specs=[low, high],
        out_specs=[low] * 2,
        out_shape=[jax.ShapeDtypeStruct((half, *rest, columns), BF)] * 2,
        compiler_params=params(),
        cost_estimate=cost(0, 4 * from_x.size),
    )(from_x, from_y)


def join_kernel(mine, from_y, from_x, one, two, out):
    half = one.shape[0]
    out[0] = mine[...]
    out[1] = from_y[...]
    out[2] = from_x[...]
    out[3, :half] = one[...]
    out[3, half:] = two[...]


def join(mine, from_y, from_x, one, two):
    job = (join_kernel, [mine, from_y, from_x, one, two], [(4, *mine.shape)])
    return small_calls([job])[0][0]


def both_kernel(keep, got, send_x, send_y, rest_x, rest_y, own):
    half = keep.shape[1] // 2

    def total(cell, part):
        return (keep[cell, part].astype(F32) + got[cell, part].astype(F32)).astype(BF)

    low, high = slice(0, half), slice(half, 2 * half)
    send_x[0], send_x[1] = total(3, low), total(2, low)
    send_y[0], send_y[1] = total(3, high), total(1, high)
    rest_x[...], rest_y[...] = total(2, high), total(1, low)
    own[:half], own[half:] = total(0, low), total(0, high)


def both_cores(keep, got):
    _, zs, *rest = keep.shape
    part = (zs // 2, *rest)
    shapes = [(2, *part), (2, *part), part, part, (zs, *rest)]
    return both_kernel, [keep, got], shapes


def sides_kernel(rest_x, rest_y, got_x, got_y, send_x, send_y):
    send_x[...] = (rest_x[...].astype(F32) + got_y[0].astype(F32)).astype(BF)
    send_y[...] = (rest_y[...].astype(F32) + got_x[0].astype(F32)).astype(BF)


def add_sides(rest_x, rest_y, got_x, got_y):
    return sides_kernel, [rest_x, rest_y, got_x, got_y], [rest_x.shape] * 2


def own_kernel(own, got_x, got_y, side_x, side_y, out):
    half = side_x.shape[0]
    low = own[:half].astype(F32) + got_x[1].astype(F32) + side_y[...].astype(F32)
    high = own[half:].astype(F32) + got_y[1].astype(F32) + side_x[...].astype(F32)
    out[:half] = low.astype(BF)
    out[half:] = high.astype(BF)


def add_own(own, got_x, got_y, side_x, side_y):
    return own_kernel, [own, got_x, got_y, side_x, side_y], [own.shape]


def ffn_kernel(first, last, ties, *refs):
    feed = iter(refs)
    take = lambda n: [next(feed) for _ in range(n)]
    normed, normed_twin, grad_out, grad_out_twin = take(4)
    mine, from_y, from_x, one, two = take(5)
    before = [] if first else take(4)
    take(ties)
    send_x, send_y, rest_x, rest_y, own = take(5)
    totals = take(4)
    wide, rows_n, rows_g, active, grad_gate, grad_up = take(6)
    step = pl.program_id(0)
    steps = pl.num_programs(0)
    zs, _, kinds, block, tile = mine.shape
    half = zs // 2
    height = normed.shape[0]
    places = [(core, x, z) for core in range(2) for x in range(2) for z in range(zs)]

    @pl.when(step == 0)
    def _():
        for at, (core, x, z) in enumerate(places):
            rows = slice(at * block, (at + 1) * block)
            for k in range(kinds):
                if x == 0:
                    wide[k, rows, :tile] = mine[z, core, k]
                    wide[k, rows, tile:] = from_y[z, core, k]
                else:
                    wide[k, rows, :tile] = from_x[z, core, k]
                    corner = one[z, core, k] if z < half else two[z - half, core, k]
                    wide[k, rows, tile:] = corner

    at = pl.ds(pl.multiple_of(step * height, height), height)

    def work(normed, grad_out, before, totals, turn):
        left = normed[...]
        right = grad_out[...]
        rows_n[at, :] = left
        rows_g[at, :] = right
        gate, upward = dot_nn(left, wide[0]), dot_nn(left, wide[1])
        grad_active = dot_nn(right, wide[2])
        sigma = 1.0 / (1.0 + jnp.exp(-gate))
        silu = gate * sigma
        act = (silu * upward).astype(BF)
        g_up = (grad_active * silu).astype(BF)
        g_gate = (grad_active * upward * (sigma + silu * (1.0 - sigma))).astype(BF)
        active[at, :] = act
        grad_up[at, :] = g_up
        grad_gate[at, :] = g_gate
        ffn = dot_nt(act, wide[2])
        back = dot_nt(g_gate, wide[0]) + dot_nt(g_up, wide[1])
        if not first:
            ffn = ffn + before[0][...].astype(F32)
            back = back + before[1][...].astype(F32)
        if turn:
            ffn, back = other_core_first(ffn), other_core_first(back)
        totals[0][...] = ffn.astype(totals[0].dtype)
        totals[1][...] = back.astype(totals[1].dtype)

    @pl.when(step < steps // 2)
    def _():
        work(normed, grad_out, before[:2], totals[:2], False)

    @pl.when(step >= steps // 2)
    def _():
        work(normed_twin, grad_out_twin, before[2:], totals[2:], last)

    @pl.when(step == steps - 1)
    def _():
        group = 256 // block
        for first_place in range(0, len(places), group):
            rows = slice(first_place * block, (first_place + group) * block)
            for k, (left, right) in enumerate(
                ((rows_n, grad_gate), (rows_n, grad_up), (rows_g, active))
            ):
                value = dot_tn(left[:, rows], right[...]).astype(BF)
                for i in range(group):
                    core, x, z = places[first_place + i]
                    part = value[i * block : (i + 1) * block]
                    low, zh = z < half, z % half
                    near, far = part[:, :tile], part[:, tile:]
                    if x == 0:
                        own[z, core, k] = near
                        if low:
                            rest_y[zh, core, k] = far
                        else:
                            send_y[1, zh, core, k] = far
                    else:
                        if low:
                            send_x[1, zh, core, k] = near
                            send_x[0, zh, core, k] = far
                        else:
                            rest_x[zh, core, k] = near
                            send_y[0, zh, core, k] = far


def ffn_piece(inputs, cells, before, last, ties):
    rows, width = inputs[0].shape
    zs, _, kinds, block, columns = cells[0].shape
    first = before is None
    height = min(ROW_TILE, rows)
    half = rows // height
    near = pl.BlockSpec((height, width), lambda i: (jnp.minimum(i, half - 1), 0))
    far = pl.BlockSpec((height, width), lambda i: (jnp.maximum(i - half, 0), 0))
    operands = [*inputs, *cells, *(() if first else before), *ties]
    part = (zs // 2, 2, kinds, block, columns)
    grads = [(2, *part), (2, *part), part, part, (zs, *part[1:])]
    mine = F32 if last else BF
    return pl.pallas_call(
        functools.partial(ffn_kernel, first, last, len(ties)),
        grid=(2 * half,),
        in_specs=[near, far, near, far]
        + [whole_spec(item.shape) for item in cells]
        + ([] if first else [near, near, far, far])
        + [ANYWHERE] * len(ties),
        out_specs=[whole_spec(shape) for shape in grads] + [near, near, far, far],
        out_shape=[jax.ShapeDtypeStruct(shape, BF) for shape in grads]
        + [jax.ShapeDtypeStruct((rows, width), dtype) for dtype in (mine, mine, BF, BF)],
        scratch_shapes=[pltpu.VMEM((kinds, width, 2 * columns), BF)]
        + [pltpu.VMEM((2 * rows, width), BF)] * 2
        + [pltpu.VMEM((2 * rows, 2 * columns), BF)] * 3,
        compiler_params=params(),
        cost_estimate=cost(
            72 * COST * rows * width * columns, 24 * width * columns + 40 * rows * width
        ),
    )(*operands)


def lay_out(near, twin, wide):
    _, zs, kinds, block, tile = near.shape
    for core, cells in enumerate((near, twin)):
        for x in range(2):
            for z in range(zs):
                at = ((core * 2 + x) * zs + z) * block
                for k in range(kinds):
                    for y in range(2):
                        wide[k, at : at + block, y * tile : (y + 1) * tile] = cells[
                            2 * x + y, z, k
                        ]


def cell_specs(cells, tile, skip=0):
    return [
        pl.BlockSpec((*item.shape[:-1], tile), lambda j: (0, 0, 0, 0, j + skip))
        for item in cells
    ]


def other_core_first(values):
    half = values.shape[1] // 2
    return jnp.concatenate([values[:, half:], values[:, :half]], axis=1)


def moved(values, shift, position):
    rows = values.shape[0]
    turned = pltpu.roll(values, shift % rows, 0)
    inside = position >= shift if shift > 0 else position < rows + shift
    return jnp.where(inside, turned, 0.0)


def mixed_of(gated, conv, position):
    total = conv[0:1] * gated
    for shift in range(1, conv.shape[0]):
        total = total + conv[shift : shift + 1] * moved(gated, shift, position)
    return total


def tile_conv(conv):
    return jnp.concatenate([conv[0], conv[1]], axis=1)


def mixer_kernel(first, last, ties, row_tile, *refs):
    feed = iter(refs)
    take = lambda n: [next(feed) for _ in range(n)]
    lengths, normed, tokens, conv, gain = take(5)
    cells = take(2)
    before = [] if first else take(1)
    take(ties)
    project, hidden = take(2)
    normed_two, for_twin = take(2) if last else (None, None)
    wide, branch = take(2)
    step = pl.program_id(0)
    rows = normed.shape[0]
    lay_out(*cells, wide)

    @pl.loop(0, rows // row_tile)
    def _(i):
        at = pl.ds(pl.multiple_of(i * row_tile, row_tile), row_tile)
        left = normed[at, :]
        for k in range(3):
            project[k, at, :] = dot_nn(left, wide[k])

    taps = tile_conv(conv[...])
    for sequence in range(rows // SLOTS):
        at = slice(sequence * SLOTS, (sequence + 1) * SLOTS)
        position = lax.broadcasted_iota(jnp.int32, (SLOTS, wide.shape[2]), 0)
        gated = project[0, at] * project[2, at]
        gated = jnp.where(position < lengths[sequence], gated, 0.0)
        branch[at, :] = (project[1, at] * mixed_of(gated, taps, position)).astype(BF)

    @pl.when(step == 0)
    def _():
        if first:
            hidden[...] = tokens[...].astype(F32)
        else:
            hidden[...] = before[0][...]

    ending = step == pl.num_programs(0) - 1

    @pl.loop(0, rows // row_tile)
    def _(i):
        at = pl.ds(pl.multiple_of(i * row_tile, row_tile), row_tile)
        value = hidden[at, :] + dot_nt(branch[at, :], wide[3])
        hidden[at, :] = value
        if last:

            @pl.when(ending)
            def _():
                unit = norm_stats(value)[1]
                value_two = (unit * gain[...]).astype(BF)
                normed_two[at, :] = value_two
                for_twin[at, :] = other_core_first(value_two)


def mixer_part(lengths, normed, tokens, conv, gain, cells, before, last, ties, tile):
    rows, width = normed.shape
    _, zs, kinds, block, columns = cells[0].shape
    first = before is None
    whole = whole_spec((rows, width))
    inputs = [lengths, normed, tokens, conv, gain, *cells]
    inputs += ([] if first else [before]) + list(ties)
    outs = [jax.ShapeDtypeStruct((3, rows, 2 * columns), F32), jax.ShapeDtypeStruct((rows, width), F32)]
    out_specs = [pl.BlockSpec((3, rows, 2 * tile), lambda j: (0, 0, j)), whole]
    if last:
        outs += [jax.ShapeDtypeStruct((rows, width), BF)] * 2
        out_specs += [whole] * 2
    return pl.pallas_call(
        functools.partial(mixer_kernel, first, last, len(ties), min(rows, 256)),
        grid=(columns // tile,),
        in_specs=[pl.BlockSpec(memory_space=pltpu.SMEM), whole, whole]
        + [pl.BlockSpec((2, conv.shape[1], tile), lambda j: (0, 0, j)), whole_spec((1, width))]
        + cell_specs(cells, tile)
        + [whole] * (0 if first else 1)
        + [ANYWHERE] * len(ties),
        out_specs=out_specs,
        out_shape=outs,
        scratch_shapes=[
            pltpu.VMEM((kinds, width, 2 * tile), BF),
            pltpu.VMEM((rows, 2 * tile), BF),
        ],
        input_output_aliases={} if first else {7: 1},
        compiler_params=params(),
        cost_estimate=pl.CostEstimate(
            flops=16 * COST * rows * width * columns,
            bytes_accessed=24 * rows * columns + 16 * width * columns + 8 * rows * width,
            transcendentals=0,
        ),
    )(*inputs)


def mixer_back_kernel(first, ties, row_tile, *refs):
    feed = iter(refs)
    take = lambda n: [next(feed) for _ in range(n)]
    lengths, normed, grad_mix, project, conv = take(5)
    cells = take(2)
    before = [] if first else take(1)
    take(ties)
    keep, send, tap_grads, grad_normed = take(4)
    wide, branch, grads, grad_branch = take(4)
    step = pl.program_id(0)
    rows = normed.shape[0]
    _, zs, _, block, tile = cells[0].shape
    lay_out(*cells, wide)

    @pl.when(step == 0)
    def _():
        grad_normed[...] = jnp.zeros_like(grad_normed) if first else before[0][...]

    @pl.loop(0, rows // row_tile)
    def _(i):
        at = pl.ds(pl.multiple_of(i * row_tile, row_tile), row_tile)
        grad_branch[at, :] = dot_nn(grad_mix[at, :], wide[3])

    taps = tile_conv(conv[...])
    count = taps.shape[0]
    sums = [jnp.zeros((1, 2 * tile), F32)] * count
    for sequence in range(rows // SLOTS):
        at = slice(sequence * SLOTS, (sequence + 1) * SLOTS)
        position = lax.broadcasted_iota(jnp.int32, (SLOTS, 2 * tile), 0)
        living = position < lengths[sequence]
        gated = jnp.where(living, project[0, at] * project[2, at], 0.0)
        mixed = taps[0:1] * gated
        g_mixed = grad_branch[at, :] * project[1, at]
        sums[0] = sums[0] + jnp.sum(g_mixed * gated, axis=0, keepdims=True)
        g_gated = taps[0:1] * g_mixed
        for shift in range(1, count):
            lower = moved(gated, shift, position)
            mixed = mixed + taps[shift : shift + 1] * lower
            sums[shift] = sums[shift] + jnp.sum(g_mixed * lower, axis=0, keepdims=True)
            g_gated = g_gated + taps[shift : shift + 1] * moved(g_mixed, -shift, position)
        g_gated = jnp.where(living, g_gated, 0.0)
        branch[at, :] = (project[1, at] * mixed).astype(BF)
        grads[0, at, :] = (g_gated * project[2, at]).astype(BF)
        grads[1, at, :] = (grad_branch[at, :] * mixed).astype(BF)
        grads[2, at, :] = (g_gated * project[0, at]).astype(BF)
    tap_grads[...] = jnp.concatenate(
        sums + [jnp.zeros((8 - count, 2 * tile), F32)], axis=0
    )

    @pl.loop(0, rows // row_tile)
    def _(i):
        at = pl.ds(pl.multiple_of(i * row_tile, row_tile), row_tile)
        value = dot_nt(grads[0, at, :], wide[0]) + dot_nt(grads[1, at, :], wide[1])
        grad_normed[at, :] += value + dot_nt(grads[2, at, :], wide[2])

    depth = zs * block
    for place in range(4):
        at = slice(place * depth, (place + 1) * depth)
        core, x = divmod(place, 2)
        out = send if core else keep
        for k in range(4):
            if k < 3:
                value = dot_tn(normed[:, at], grads[k])
            else:
                value = dot_tn(grad_mix[:, at], branch[...])
            value = value.astype(BF)
            for z in range(zs):
                part = value[z * block : (z + 1) * block]
                out[2 * x, z, k] = part[:, :tile]
                out[2 * x + 1, z, k] = part[:, tile:]


def mixer_back(lengths, normed, grad_mix, project, conv, cells, before, ties, tile, part, parts):
    rows, width = normed.shape
    _, zs, kinds, block, columns = cells[0].shape
    columns = columns // parts
    skip = part * (columns // tile)
    first = before is None
    whole = whole_spec((rows, width))
    inputs = [lengths, normed, grad_mix, project, conv, *cells]
    inputs += ([] if first else [before]) + list(ties)
    grads = pl.BlockSpec((4, zs, kinds, block, tile), lambda j: (0, 0, 0, 0, j))
    grad_shape = jax.ShapeDtypeStruct((4, zs, kinds, block, columns), BF)
    return pl.pallas_call(
        functools.partial(mixer_back_kernel, first, len(ties), min(rows, 256)),
        grid=(columns // tile,),
        in_specs=[pl.BlockSpec(memory_space=pltpu.SMEM), whole, whole]
        + [pl.BlockSpec((3, rows, 2 * tile), lambda j: (0, 0, j + skip))]
        + [pl.BlockSpec((2, conv.shape[1], tile), lambda j: (0, 0, j + skip))]
        + cell_specs(cells, tile, skip)
        + [whole] * (0 if first else 1)
        + [ANYWHERE] * len(ties),
        out_specs=[grads, grads, pl.BlockSpec((8, 2 * tile), lambda j: (0, j)), whole],
        out_shape=[
            grad_shape,
            grad_shape,
            jax.ShapeDtypeStruct((8, 2 * columns), F32),
            jax.ShapeDtypeStruct((rows, width), F32),
        ],
        scratch_shapes=[
            pltpu.VMEM((kinds, width, 2 * tile), BF),
            pltpu.VMEM((rows, 2 * tile), BF),
            pltpu.VMEM((3, rows, 2 * tile), BF),
            pltpu.VMEM((rows, 2 * tile), F32),
        ],
        input_output_aliases={} if first else {7: 3},
        compiler_params=params(),
        cost_estimate=pl.CostEstimate(
            flops=32 * COST * rows * width * columns,
            bytes_accessed=24 * rows * columns + 32 * width * columns + 8 * rows * width,
            transcendentals=0,
        ),
    )(*inputs)


def reorder(source, target, flip, inward):
    width = source.shape[1]
    for case in range(4):

        @pl.when(flip == case)
        def _():
            count = SHARDS[0]
            block, zs = width // count, count // 4
            for place in range(count):
                core, x, z = place // (2 * zs), place // zs % 2, place % zs
                absolute = z * 4 + (case ^ (x * 2 + core))
                here = slice(place * block, (place + 1) * block)
                there = slice(absolute * block, (absolute + 1) * block)
                if inward:
                    target[:, here] = source[:, there]
                else:
                    target[:, there] = source[:, here]


def row_call(kernel, flip, inputs, outs, sums=0, ties=()):
    rows, width = next(item.shape for item in inputs if item.shape[0] > 1)
    height = min(ROW_TILE, rows)
    tiled = pl.BlockSpec((height, width), lambda i: (i, 0))
    scalar = pl.BlockSpec(memory_space=pltpu.SMEM)
    specs = [
        scalar if item.ndim == 1 else tiled if item.shape[0] > 1 else whole_spec((1, width))
        for item in inputs
    ]
    count = len(inputs) + 1

    def body(*refs):
        kernel(*refs[:count], *refs[count + len(ties) :])

    return pl.pallas_call(
        body,
        grid=(rows // height,),
        in_specs=[scalar] + specs + [ANYWHERE] * len(ties),
        out_specs=[tiled] * len(outs) + [whole_spec((8, width))] * sums,
        out_shape=[jax.ShapeDtypeStruct((rows, width), dtype) for dtype in outs]
        + [jax.ShapeDtypeStruct((8, width), F32)] * sums,
        scratch_shapes=[pltpu.VMEM((height, width), F32)] * 2,
        compiler_params=params(),
        cost_estimate=cost(20 * rows * width, 12 * rows * width),
    )(flip, *inputs, *ties)


def enter_kernel(flip, lengths, tokens, cotangent, gain, low, normed, grad, for_twin, one, two):
    one[...] = tokens[...].astype(F32)
    reorder(one, two, flip[0], True)
    value = two[...]
    low[...] = value.astype(BF)
    normed[...] = (norm_stats(value)[1] * gain[...]).astype(BF)
    one[...] = cotangent[...].astype(F32)
    reorder(one, two, flip[0], True)
    height = value.shape[0]
    first = pl.program_id(0) * height
    position = first % SLOTS + lax.broadcasted_iota(jnp.int32, value.shape, 0)
    value = jnp.where(position < lengths[first // SLOTS], two[...], 0.0).astype(BF)
    grad[...] = value
    for_twin[...] = other_core_first(value)


def add_up(total, values):
    part = jnp.sum(values.reshape(-1, 8, values.shape[1]), axis=0)

    @pl.when(pl.program_id(0) == 0)
    def _():
        total[...] = part

    @pl.when(pl.program_id(0) > 0)
    def _():
        total[...] += part


def between_kernel(flip, mine, twin, hidden, grad_out, gain, mix, total, one, two):
    grad = mine[...] + twin[...].astype(F32)
    inverse, unit = norm_stats(hidden[...])
    value = grad_out[...].astype(F32) + norm_back(grad, gain[...], inverse, unit)
    mix[...] = value.astype(BF)
    add_up(total, grad * unit)


def leave_kernel(flip, grad, tokens, grad_hidden, gain, out, total, one, two):
    inverse, unit = norm_stats(tokens[...].astype(F32))
    value = grad[...]
    one[...] = grad_hidden[...].astype(F32) + norm_back(value, gain[...], inverse, unit)
    reorder(one, out, flip[0], False)
    add_up(total, value * unit)


def result_kernel(flip, hidden, mine, twin, out, one, two):
    one[...] = hidden[...] + mine[...] + twin[...].astype(F32)
    reorder(one, two, flip[0], False)
    out[...] = two[...].astype(BF)


SHARDS = [16]


def ffn_sizes(columns, rows):
    if rows <= 1024 and columns == sum(SIZES):
        return SIZES
    return (128,) * (columns // 128)


def norm_stats(values):
    inverse = lax.rsqrt(jnp.mean(values * values, axis=-1, keepdims=True) + EPS)
    return (inverse, values * inverse)


def norm_back(grad_normed, gain, inverse, unit):
    scaled = grad_normed * gain
    return inverse * (scaled - unit * jnp.mean(scaled * unit, axis=-1, keepdims=True))


def body(
    tokens,
    lengths,
    in_proj,
    conv_weight,
    out_proj,
    norm_gain,
    ffn_gain,
    w_gate,
    w_up,
    w_down,
    cotangent,
):
    rows, width = tokens.shape
    links = Links(lax.axis_size("dp"), lax.axis_size("tensor"))
    rank = lax.axis_index("tensor")
    kernel = conv_weight.shape[0]
    half = in_proj.shape[2]
    hidden_half = w_gate.shape[1]
    block = width // links.dp

    core = lax.axis_index("dp") % 2
    mixer_own = jnp.concatenate([in_proj.astype(BF), out_proj.T.astype(BF)[None]], axis=0)
    ffn_own = jnp.stack([w_gate.astype(BF), w_up.astype(BF), w_down.T.astype(BF)])
    tile = 256 if half % 512 == 0 and rows <= 1024 else 128
    shared = hidden_half // 2
    mine_of = lax.dynamic_slice_in_dim(ffn_own, core * shared, shared, 2)
    twin_of = lax.dynamic_slice_in_dim(ffn_own, (1 - core) * shared, shared, 2)
    ffn_both = jnp.stack([mine_of, links.swap(twin_of, c=1)])
    sizes = ffn_sizes(shared, rows)
    starts = [sum(sizes[:p]) for p in range(len(sizes))]
    own = [mixer_own] + [ffn_both[..., at : at + size] for at, size in zip(starts, sizes)]
    own = [links.spread(item) for item in own]
    pieces = len(own)
    last = pieces - 1
    mine, sides, corner = {}, {}, {}

    def cells(p):
        from_x, from_y = sides[p]
        return [mine[p], from_y, from_x, *corner[p]]

    sums = {}

    def start(stage, p):
        if stage == "z":
            mine[p] = links.turn_z(own[p])
            return mine, p
        if stage == "sides":
            sides[p] = links.gather_sides(mine[p])
            return sides, p
        if stage == "corner":
            corner[p] = links.gather_corner(*sides[p])
            return corner, p
        item = sums[p]
        if stage == "sum core":
            item["got"] = links.swap(item["send"], c=1)
            return item, "got"
        raise ValueError(stage)

    def add(*steps):
        jobs, keys = [], []
        for stage, p in steps:
            item = sums[p]
            if stage == "sum sides":
                jobs.append(add_sides(*item["parts"][2:4], *item["corner"]))
                keys.append((item, "next"))
            elif stage == "sum z":
                jobs.append(add_own(item["parts"][4], *item["corner"], *item["sides"]))
                keys.append((item, "total"))
            elif "keep" in item:
                jobs.append(both_cores(item["keep"], item["got"]))
                keys.append((item, "parts"))
        if jobs:
            for (item, key), out in zip(keys, small_calls(jobs)):
                item[key] = out
        places = []
        for stage, p in steps:
            item = sums[p]
            if stage == "sum z":
                item["z"] = links.turn_z(item["total"][0])
                places.append((item, "z"))
                continue
            pair = item["next"] if stage == "sum sides" else item["parts"][:2]
            key = stage[4:]
            item[key] = links.swap(pair[0], x=1), links.swap(pair[1], y=1)
            places.append((item, key))
        return places

    def close(kept, places):
        kept, tree = jax.tree.flatten([kept, [store[key] for store, key in places]])
        kept, arrived = jax.tree.unflatten(tree, gate(kept))
        for (store, key), value in zip(places, arrived):
            store[key] = value
        return kept

    blocks = links.absolute(jnp.arange(links.dp))
    gain_one = jnp.take(norm_gain.reshape(links.dp, block), blocks, axis=0).reshape(1, width)
    gain_two = jnp.take(ffn_gain.reshape(links.dp, block), blocks, axis=0).reshape(1, width)
    conv = jnp.where(rank == 0, conv_weight, jnp.roll(conv_weight, half, axis=1))
    conv = conv.reshape(kernel, 2, half).transpose(1, 0, 2)
    count = rows // SLOTS
    own_lengths = lax.dynamic_slice_in_dim(lengths, rank * count, count)
    flip = (lax.axis_index("dp") % 4)[None]
    SHARDS[0] = links.dp
    tokens_low, normed, grad_ffn, for_twin_grad = row_call(
        enter_kernel, flip, [own_lengths, tokens, cotangent, gain_one], [BF] * 4, ties=own[1:]
    )

    places = [start("z", 0)]
    normed, for_twin_grad, own = close([normed, for_twin_grad, own], places)
    grad_ffn_twin = links.swap(for_twin_grad, c=1)
    places = [start("sides", 0), start("z", 1)]
    own[2:3], mine[0] = close([own[2:3], mine[0]], places)
    places = [start("corner", 0), start("z", 2)]
    own[3:4], mine[1] = close([own[3:4], mine[1]], places)
    joined = join(*cells(0))
    mixer_cells = [joined, links.swap(joined, c=1)]

    places = [start("sides", 1), start("sides", 2), start("z", 3)]
    project, hidden, normed_two, for_twin = mixer_part(
        own_lengths, normed, tokens_low, conv, gain_two, mixer_cells, None, True, [], tile
    )
    normed_two, for_twin, own[4:5] = close([normed_two, for_twin, own[4:5]], places)
    start("corner", 1)
    inputs = [normed_two, links.swap(for_twin, c=1), grad_ffn, grad_ffn_twin]

    totals = None
    for p in range(1, pieces):
        places = []
        for stage, q in (("corner", p + 1), ("sides", p + 2), ("z", p + 3)):
            if q < pieces:
                places.append(start(stage, q))
        steps = (("sum z", p - 4), ("sum sides", p - 3), ("sum corner", p - 2))
        places += add(*[step for step in steps if step[1] > 0])
        *parts, t0, t1, t2, t3 = ffn_piece(inputs, cells(p), totals, p == last, [])
        held = sums[p - 1]["parts"][:2] if p > 1 else []
        parts, totals, held = close([parts, [t0, t1, t2, t3], held], places)
        if p > 1:
            sums[p - 1]["parts"][:2] = held
        sums[p] = dict(parts=list(parts))
    ffn_twin = links.swap(totals[2], c=1)
    grad_mix, gain_two_part = row_call(
        between_kernel,
        flip,
        [totals[1], links.swap(totals[3], c=1), hidden, grad_ffn, gain_two],
        [BF],
        1,
    )
    places = add(("sum z", last - 3), ("sum sides", last - 2), ("sum corner", last - 1))
    parts = 2 if half % 256 == 0 else 1
    names = [f"mixer {p}" for p in range(parts)]
    grad_normed, taps = None, []
    for p, name in enumerate(names):
        if p:
            places = [start("sum core", names[0])]
        if p == parts - 1:
            places += add(("sum z", last - 2), ("sum sides", last - 1), ("sum corner", last))[1:]
        keep, send, tap_grads, grad_normed = mixer_back(
            own_lengths, normed, grad_mix, project, conv, mixer_cells, grad_normed, [],
            tile, p, parts,
        )
        held = sums[last]["parts"][:2] if p < parts - 1 else []
        keep, send, tap_grads, grad_normed, ffn_twin, held = close(
            [keep, send, tap_grads, grad_normed, ffn_twin, held], places
        )
        if p < parts - 1:
            sums[last]["parts"][:2] = held
        taps.append(tap_grads)
        sums[name] = dict(keep=keep, send=send)
    places = [start("sum core", names[-1])]
    steps = [("sum z", last - 1), ("sum sides", last)]
    if parts > 1:
        steps.append(("sum corner", names[0]))
    places += add(*steps)[1:]
    grad_tokens, gain_one_part = row_call(
        leave_kernel, flip, [grad_normed, tokens_low, grad_mix, gain_one], [F32], 1
    )
    item = sums[names[-1]]
    grad_tokens, gain_one_part, item["keep"] = close(
        [grad_tokens, gain_one_part, item["keep"]], places
    )

    place = links.place(jnp.arange(links.dp))
    taps = jnp.concatenate(taps, axis=1)[:kernel].reshape(kernel, -1, 2, tile)
    taps = taps.transpose(0, 2, 1, 3).reshape(kernel, width)
    taps = jnp.where(rank == 0, taps, jnp.roll(taps, half, axis=1))
    gains = jnp.stack([gain_one_part.sum(0), gain_two_part.sum(0)])
    gains = jnp.take(gains.reshape(2, links.dp, block), place, axis=1).reshape(2, width)
    small = links.sum_chip(jnp.concatenate([gains, taps], axis=0))

    steps = [("sum corner", names[-1]), ("sum z", last)]
    if parts > 1:
        steps.append(("sum sides", names[0]))
    places = add(*steps)
    del places[1]
    result = row_call(
        result_kernel, flip, [hidden, totals[0], ffn_twin], [BF]
    )[0]
    result, small = close([result, small], places)
    steps = [("sum sides", names[-1])]
    if parts > 1:
        steps.append(("sum z", names[0]))
    places = add(*steps)[:1]
    (small,) = close([links.sum_rest(small)], places)
    add(("sum z", names[-1]))
    shard = lambda p: jnp.sum(sums[p]["z"].astype(F32), axis=0)
    mixer_shard = jnp.concatenate([shard(name) for name in names], axis=2)
    ffn_shard = jnp.concatenate([shard(p) for p in range(1, pieces)], axis=3)
    here, there = ffn_shard[0], links.swap(ffn_shard[1], c=1)
    ffn_shard = jnp.concatenate(
        [jnp.where(core == 0, here, there), jnp.where(core == 0, there, here)], axis=2
    )
    return (
        result,
        grad_tokens,
        mixer_shard[:3],
        small[2:],
        mixer_shard[3].T,
        small[0],
        small[1],
        ffn_shard[0],
        ffn_shard[1],
        ffn_shard[2].T,
    )


def solution(mesh):
    rows = P(("dp", "tensor"), None)
    in_specs = (
        rows,
        P("dp"),
        P(None, "dp", "tensor"),
        P(),
        P("tensor", "dp"),
        P(),
        P(),
        P("dp", "tensor"),
        P("dp", "tensor"),
        P("tensor", "dp"),
        rows,
    )
    out_specs = (
        rows,
        rows,
        P(None, "dp", "tensor"),
        P(),
        P("tensor", "dp"),
        P(),
        P(),
        P("dp", "tensor"),
        P("dp", "tensor"),
        P("tensor", "dp"),
    )
    return jax.shard_map(body, mesh=mesh, in_specs=in_specs, out_specs=out_specs, check_vma=False)
```
